32 devices in a mesh: fsdp: 8 (over z, x), context: 2 (over y), tensor: 2 (over core).
Axes of the slice: x: 2, y: 2, z: 4, core: 2. Of those that a mesh axis runs over, the one named last changes fastest.
Arguments:
- tokens: bfloat16 [8, 2048, 768], P('fsdp', 'context'), may hold values from -6 to 6
- pack_lengths: int32 [8, 3], P('fsdp'), may hold values from 1 to 1792, as said below
- cotangent: bfloat16 [8, 2048, 768], P('fsdp', 'context'), may hold values from -6 to 6
- projection: bfloat16 [768, 3, 768], P('fsdp', None, 'tensor'), may hold values from -0.21875 to 0.21875
- projection_bias: bfloat16 [3, 768], P(None, ('tensor', 'fsdp')), may hold values from -3 to 3
- outgoing: bfloat16 [768, 768], P('tensor', 'fsdp'), may hold values from -0.875 to 0.875
- outgoing_bias: bfloat16 [768], P('fsdp'), may hold values from -3 to 3
- widening: bfloat16 [768, 3072], P('fsdp', 'tensor'), may hold values from -0.21875 to 0.21875
- widening_bias: bfloat16 [3072], P(('tensor', 'fsdp')), may hold values from -3 to 3
- narrowing: bfloat16 [3072, 768], P('tensor', 'fsdp'), may hold values from -0.109375 to 0.109375
- narrowing_bias: bfloat16 [768], P('fsdp'), may hold values from -3 to 3
- first_gain: bfloat16 [768], P('fsdp'), may hold values from 0.099609375 to 1.8984375
- first_shift: bfloat16 [768], P('fsdp'), may hold values from -3 to 3
- second_gain: bfloat16 [768], P('fsdp'), may hold values from 0.099609375 to 1.8984375
- second_shift: bfloat16 [768], P('fsdp'), may hold values from -3 to 3
Outputs:
- mixed: bfloat16 [8, 2048, 768], P('fsdp', 'context')
- tokens_gradient: float32 [8, 2048, 768], P('fsdp', 'context')
- projection_gradient: float32 [768, 3, 768], P('fsdp', None, 'tensor')
- projection_bias_gradient: float32 [3, 768], P(None, ('tensor', 'fsdp'))
- outgoing_gradient: float32 [768, 768], P('tensor', 'fsdp')
- outgoing_bias_gradient: float32 [768], P('fsdp')
- widening_gradient: float32 [768, 3072], P('fsdp', 'tensor')
- widening_bias_gradient: float32 [3072], P(('tensor', 'fsdp'))
- narrowing_gradient: float32 [3072, 768], P('tensor', 'fsdp')
- narrowing_bias_gradient: float32 [768], P('fsdp')
- first_gain_gradient: float32 [768], P('fsdp')
- first_shift_gradient: float32 [768], P('fsdp')
- second_gain_gradient: float32 [768], P('fsdp')
- second_shift_gradient: float32 [768], P('fsdp')
The draws below stay inside these ranges and needn't reach their ends.
Inputs may be any that keep to these rules, and one draw needn't show every extreme that they name: `pack_lengths`: each row lists the lengths of the 3 sequences of one pack in the order in which they lie from the pack's first token, each starting at a multiple of 128; with every length rounded up to a multiple of 128 they fit into the pack's 2048 tokens, and one of them starts within the first 1024 tokens and ends within the last 1024 tokens.
All inputs are finite; a program needn't handle non-finite values.
Results may differ from the reference program's by a relative error of at most 0.028.
Values may be sent and summed in bfloat16 or wider, within the bound.
No kernel may reach another device: no remote copies, remote signals or barrier semaphores. Data moves between devices by JAX's collectives and lax.ppermute only.
A program may use at most 256 MiB of HBM per device.

```python
import jax
import jax.numpy as jnp
from jax import lax

D = 768
HEADS = 12
HEAD_DIM = 64
ROTARY = 16
FF = 3072
TILE = 128
SEQS = 3
PACKS = 1
GROUP = 2048
LOCAL = 1024
N_FSDP = 8


def draw_pack_lengths(key, part):
    rows = N_FSDP * PACKS
    per_device = LOCAL // TILE
    tiles_all = GROUP // TILE
    first_key, second_key, third_key, fourth_key, fifth_key, sixth_key = jax.random.split(key, 6)
    chosen_row = jax.random.randint(sixth_key, (), 0, rows)
    chosen = jnp.arange(rows, dtype=jnp.int32) == chosen_row
    short_one = jax.random.randint(first_key, (rows,), 1, per_device - 1)
    short_one = jnp.where(chosen, 1, short_one)
    short_two = jax.random.randint(second_key, (rows,), 1, per_device - short_one)
    short_two = jnp.where(chosen, 1, short_two)
    empty = jax.random.randint(third_key, (rows,), 0, per_device - short_one - short_two)
    empty = jnp.where(chosen, 0, empty)
    longest = tiles_all - short_one - short_two - empty
    place = jax.random.randint(fourth_key, (rows,), 0, 3)
    column_zero = jnp.where(place == 0, longest, short_one)
    column_one = jnp.where(place == 1, longest, jnp.where(place == 0, short_one, short_two))
    column_two = jnp.where(place == 2, longest, short_two)
    tiles = jnp.stack([column_zero, column_one, column_two], axis=1)
    trimmed = jax.random.randint(fifth_key, (rows, 3), 0, TILE)
    is_long = place[:, None] == jnp.arange(3, dtype=jnp.int32)[None, :]
    forced = jnp.where(is_long, 0, TILE - 1)
    trimmed = jnp.where(chosen[:, None], forced, trimmed)
    return (tiles * TILE - trimmed).astype(jnp.int32)


def level_of(own_key, dims, pieces, low, largest):
    def one(dim, shards_of):
        steps = jax.random.uniform(jax.random.fold_in(jax.random.fold_in(own_key, 6), dim), (shards_of,), jnp.float32, low / len(pieces), largest / len(pieces))
        return jnp.repeat(jnp.exp(steps), dims[dim] // shards_of).reshape((-1,) + (1,) * (len(dims) - dim - 1))

    level = one(*pieces[0])
    for cut in pieces[1:]:
        level = level * one(*cut)
    return level


def centred(own_key, dims, scale, most, pieces=(), kind=jnp.bfloat16):
    result = jax.random.normal(own_key, dims, jnp.float32) * scale
    if len(pieces) > 0:
        result = level_of(own_key, dims, pieces, -0.22, 0.18) * result
    return jnp.clip(result, min=-most, max=most).astype(kind)


def setup_inputs(seed: int = 0) -> dict:
    streams_of = jax.random.split(jax.random.key(seed), 16)
    tokens = centred(streams_of[0], (N_FSDP * PACKS, GROUP, D), 1.0, 6.0, ((0, 8), (1, 2)))
    pack_lengths = draw_pack_lengths(jax.random.fold_in(streams_of[15], 71), 0)
    cotangent = centred(streams_of[2], (N_FSDP * PACKS, GROUP, D), 1.0, 6.0, ((0, 8), (1, 2)))
    projection = centred(streams_of[3], (D, 3, D), D ** -0.5, 0.21875, ((0, 8), (2, 2)))
    projection_bias = centred(streams_of[4], (3, D), 0.5, 3.0, ((1, 16),))
    outgoing = centred(streams_of[5], (D, D), (D // 16) ** -0.5, 0.875, ((0, 2), (1, 8)))
    outgoing_bias = centred(streams_of[6], (D,), 0.5, 3.0, ((0, 8),))
    widening = centred(streams_of[7], (D, FF), D ** -0.5, 0.21875, ((0, 8), (1, 2)))
    widening_bias = centred(streams_of[8], (FF,), 0.5, 3.0, ((0, 16),))
    narrowing = centred(streams_of[9], (FF, D), FF ** -0.5, 0.109375, ((0, 2), (1, 8)))
    narrowing_bias = centred(streams_of[10], (D,), 0.5, 3.0, ((0, 8),))
    first_gain = jnp.clip(1.0 + 0.18 * jax.random.normal(streams_of[11], (D,), jnp.float32), 0.099609375, 1.8984375).astype(jnp.bfloat16)
    first_shift = centred(streams_of[12], (D,), 0.5, 3.0, ((0, 8),))
    second_gain = jnp.clip(1.0 + 0.18 * jax.random.normal(streams_of[13], (D,), jnp.float32), 0.099609375, 1.8984375).astype(jnp.bfloat16)
    second_shift = centred(streams_of[14], (D,), 0.5, 3.0, ((0, 8),))
    return dict(tokens=tokens, pack_lengths=pack_lengths, cotangent=cotangent, projection=projection, projection_bias=projection_bias, outgoing=outgoing, outgoing_bias=outgoing_bias, widening=widening, widening_bias=widening_bias, narrowing=narrowing, narrowing_bias=narrowing_bias, first_gain=first_gain, first_shift=first_shift, second_gain=second_gain, second_shift=second_shift)


@jax.custom_vjp
def low(v):
    return lax.optimization_barrier(v.astype(jnp.bfloat16)).astype(jnp.float32)

@jax.custom_vjp
def low_back(v):
    return v

def low_keep(v):
    return (low(v), None)

def low_pass(kept, grad):
    return (grad,)

def back_keep(v):
    return (v, None)

def back_low(kept, grad):
    return (low(grad),)
low.defvjp(low_keep, low_pass)
low_back.defvjp(back_keep, back_low)
precise = lax.Precision.HIGHEST

def layout(lengths, index):
    padded = (lengths + TILE - 1) // TILE * TILE
    finish = jnp.cumsum(padded)
    before = (index[:, None] >= finish[None, :]).astype(jnp.int32)
    number = lax.optimization_barrier(jnp.sum(before, axis=1)).astype(jnp.int32)
    start = lax.optimization_barrier(jnp.sum(before * padded[None, :], axis=1)).astype(jnp.int32)
    position = index - start
    labels = jnp.arange(SEQS, dtype=jnp.int32)
    length = lax.optimization_barrier(jnp.sum(jnp.where(number[:, None] == labels[None, :], lengths[None, :], 0), axis=1))
    return (number, position, position < length)

def turn_tables(position):
    frequency = 10000.0 ** (-jnp.arange(0, ROTARY, 2, dtype=jnp.float32) / ROTARY)
    angles = position.astype(jnp.float32)[:, None] * frequency[None, :]
    angles = jnp.concatenate([angles, angles], axis=1)
    return (jnp.cos(angles)[:, None, :], jnp.sin(angles)[:, None, :])

def rotate(field, cosine, sine):
    half = ROTARY // 2
    front = field[..., :ROTARY]
    turned = jnp.concatenate([-front[..., half:], front[..., :half]], axis=-1)
    return jnp.concatenate([front * cosine + turned * sine, field[..., ROTARY:]], axis=-1)

def normalize(values, gain, shift):
    average = lax.optimization_barrier(jnp.mean(values, axis=-1, keepdims=True))
    centered = values - average
    spread = lax.optimization_barrier(jnp.mean(centered * centered, axis=-1, keepdims=True))
    return centered * lax.rsqrt(spread + 1e-05) * gain + shift

def attend(queries, keys, values, number, position, valid):
    block = min(512, GROUP)
    count = GROUP // block
    index = jnp.arange(GROUP, dtype=jnp.int32)

    def one_block(inputs):
        query_block, block_number, block_position, block_index = inputs
        raw = jnp.einsum('qhd,khd->hqk', query_block, keys, precision=precise)
        allowed = (block_number[:, None] == number[None, :]) & (position[None, :] <= block_position[:, None]) & valid[None, :] | (block_index[:, None] == index[None, :])
        scores = jnp.where(allowed[None], low_back(raw * HEAD_DIM ** (-0.5)), -1e+30)
        top = lax.optimization_barrier(jnp.max(scores, axis=-1, keepdims=True))
        total = jnp.log(lax.optimization_barrier(jnp.sum(jnp.exp(scores - top), axis=-1, keepdims=True))) + top
        probs = jnp.exp(scores - total)
        return jnp.einsum('hqk,khd->qhd', low(probs), values, precision=precise)
    stacked = (queries.reshape(count, block, HEADS, HEAD_DIM), number.reshape(count, block), position.reshape(count, block), index.reshape(count, block))
    return lax.map(jax.checkpoint(one_block), stacked).reshape(GROUP, HEADS, HEAD_DIM)

def make_layer(lengths):
    number, position, valid = layout(lengths, jnp.arange(GROUP, dtype=jnp.int32))
    cosine, sine = turn_tables(position)

    def layer(source, projection, projection_bias, outgoing, outgoing_bias, widening, widening_bias, narrowing, narrowing_bias, first_gain, first_shift, second_gain, second_shift):
        normed_one = low(normalize(source, first_gain, first_shift))
        normed_two = low(normalize(source, second_gain, second_shift))
        projected = jnp.einsum('td,dcf->tcf', normed_one, projection, precision=precise) + projection_bias[None]
        projected = low_back(projected).reshape(GROUP, 3, HEADS, HEAD_DIM)
        queries = low(rotate(projected[:, 0], cosine, sine))
        keys = low(rotate(projected[:, 1], cosine, sine))
        values = low(projected[:, 2])
        heads = attend(queries, keys, values, number, position, valid)
        heads = low(low_back(heads)).reshape(GROUP, D)
        hidden = low_back(jnp.dot(normed_two, widening, precision=precise) + widening_bias)
        active = low(jax.nn.gelu(hidden, approximate=False))
        return source + jnp.dot(heads, outgoing, precision=precise) + outgoing_bias + jnp.dot(active, narrowing, precision=precise) + narrowing_bias
    return layer

def reference(tokens, pack_lengths, cotangent, projection, projection_bias, outgoing, outgoing_bias, widening, widening_bias, narrowing, narrowing_bias, first_gain, first_shift, second_gain, second_shift):
    params = tuple((weight.astype(jnp.float32) for weight in (projection, projection_bias, outgoing, outgoing_bias, widening, widening_bias, narrowing, narrowing_bias, first_gain, first_shift, second_gain, second_shift)))

    def step(totals, inputs):
        block_tokens, lengths, block_slope = inputs
        layer = make_layer(lengths)
        output, pullback = jax.vjp(layer, block_tokens.astype(jnp.float32), *params)
        slopes = pullback(block_slope.astype(jnp.float32))
        totals = tuple((left + right for left, right in zip(totals, slopes[1:])))
        return (totals, (output.astype(jnp.bfloat16), slopes[0]))
    zeros = tuple((jnp.zeros_like(weight) for weight in params))
    totals, (mixed, tokens_gradient) = lax.scan(step, zeros, (tokens, pack_lengths, cotangent))
    return (mixed, tokens_gradient, totals[0], totals[1], totals[2], totals[3], totals[4], totals[5], totals[6], totals[7], totals[8], totals[9], totals[10], totals[11])
```

```python
import jax
import jax.numpy as jnp
from jax import lax
from jax.experimental import pallas as pl
from jax.experimental.pallas import tpu as pltpu
from jax.sharding import PartitionSpec as P

HEAD_DIM = 64
ROTARY = 16
TILE = 128
SEQS = 3


epsilon = 1e-05


def layout(lengths, index):
    padded = (lengths + TILE - 1) // TILE * TILE
    labels = jnp.arange(SEQS, dtype=jnp.int32)
    finish = jnp.sum(jnp.where(labels[:, None] <= labels[None, :], padded[:, None], 0), axis=0)
    before = (index[:, None] >= finish[None, :]).astype(jnp.int32)
    number = jnp.sum(before, axis=1)
    start = jnp.sum(before * padded[None, :], axis=1)
    position = index - start
    length = jnp.sum(jnp.where(number[:, None] == labels[None, :], lengths[None, :], 0), axis=1)
    return (number, position, position < length)


def turn_tables(position):
    frequency = 10000.0 ** (-jnp.arange(0, ROTARY, 2, dtype=jnp.float32) / ROTARY)
    angles = position.astype(jnp.float32)[:, None] * frequency[None, :]
    angles = jnp.concatenate([angles, angles], axis=1)
    return (jnp.cos(angles)[:, None, :], jnp.sin(angles)[:, None, :])


def rotate(field, cosine, sine):
    half = ROTARY // 2
    front = field[..., :ROTARY]
    turned = jnp.concatenate([-front[..., half:], front[..., :half]], axis=-1)
    return jnp.concatenate([front * cosine + turned * sine, field[..., ROTARY:]], axis=-1)


def rotate_back(slope, cosine, sine):
    half = ROTARY // 2
    front = slope[..., :ROTARY]
    scaled = front * sine
    turned = jnp.concatenate([scaled[..., half:], -scaled[..., :half]], axis=-1)
    return jnp.concatenate([front * cosine + turned, slope[..., ROTARY:]], axis=-1)


def normalize(values, gain, shift):
    average = jnp.mean(values, axis=-1, keepdims=True)
    centered = values - average
    spread = jnp.mean(centered * centered, axis=-1, keepdims=True)
    factor = lax.rsqrt(spread + epsilon)
    unit = centered * factor
    return (unit, factor, unit * gain + shift)


def normalize_back(slope, unit, factor, gain):
    scaled = slope * gain
    return factor * (
        scaled
        - jnp.mean(scaled, axis=-1, keepdims=True)
        - unit * jnp.mean(scaled * unit, axis=-1, keepdims=True)
    )


def gelu_slope(values):
    return (
        0.5 * (1.0 + lax.erf(values * 0.7071067811865476))
        + values * jnp.exp(-0.5 * values * values) * 0.3989422804014327
    )


def allowed_mask(
    query_number, query_position, query_index, key_number, key_position, key_valid, key_index
):
    same = (
        (query_number[:, None] == key_number[None, :])
        & (key_position[None, :] <= query_position[:, None])
        & key_valid[None, :]
    )
    return same | (query_index[:, None] == key_index[None, :])


def general_body(
    tokens,
    pack_lengths,
    cotangent,
    projection,
    projection_bias,
    outgoing,
    outgoing_bias,
    widening,
    widening_bias,
    narrowing,
    narrowing_bias,
    first_gain,
    first_shift,
    second_gain,
    second_shift,
):
    packs, local, width = tokens.shape
    group = local * lax.axis_size("context")
    rows = packs * local
    (
        projection,
        projection_bias,
        outgoing,
        outgoing_bias,
        widening,
        widening_bias,
        narrowing,
        narrowing_bias,
        first_gain,
        first_shift,
        second_gain,
        second_shift,
    ) = (
        lax.all_gather(projection, "fsdp", axis=0, tiled=True),
        lax.all_gather(projection_bias, "fsdp", axis=1, tiled=True),
        lax.all_gather(outgoing, "fsdp", axis=1, tiled=True),
        lax.all_gather(outgoing_bias, "fsdp", axis=0, tiled=True),
        lax.all_gather(widening, "fsdp", axis=0, tiled=True),
        lax.all_gather(widening_bias, "fsdp", axis=0, tiled=True),
        lax.all_gather(narrowing, "fsdp", axis=1, tiled=True),
        lax.all_gather(narrowing_bias, "fsdp", axis=0, tiled=True),
        lax.all_gather(first_gain, "fsdp", axis=0, tiled=True),
        lax.all_gather(first_shift, "fsdp", axis=0, tiled=True),
        lax.all_gather(second_gain, "fsdp", axis=0, tiled=True),
        lax.all_gather(second_shift, "fsdp", axis=0, tiled=True),
    )
    inner = projection.shape[2]
    heads_here = inner // HEAD_DIM
    score_scale = HEAD_DIM ** (-0.5)
    gain_one = first_gain.astype(jnp.float32)
    gain_two = second_gain.astype(jnp.float32)
    source = tokens.reshape(rows, width).astype(jnp.float32)
    unit_one, factor_one, normed_one = normalize(source, gain_one, first_shift.astype(jnp.float32))
    unit_two, factor_two, normed_two = normalize(source, gain_two, second_shift.astype(jnp.float32))
    normed_one = normed_one.astype(jnp.bfloat16)
    normed_two = normed_two.astype(jnp.bfloat16)
    projected = jnp.dot(
        normed_one, projection.reshape(width, 3 * inner), preferred_element_type=jnp.float32
    ).reshape(rows, 3, inner)
    projected = projected + projection_bias.astype(jnp.float32)[None]
    query_index = lax.axis_index("context") * local + jnp.arange(local, dtype=jnp.int32)
    key_index = jnp.arange(group, dtype=jnp.int32)
    query_number, query_position, query_valid = jax.vmap(layout, in_axes=(0, None))(
        pack_lengths, query_index
    )
    key_number, key_position, key_valid = jax.vmap(layout, in_axes=(0, None))(
        pack_lengths, key_index
    )
    cosine, sine = turn_tables(query_position.reshape(rows))
    shaped = projected.reshape(rows, 3, heads_here, HEAD_DIM)
    queries = rotate(shaped[:, 0], cosine, sine).astype(jnp.bfloat16)
    keys = rotate(shaped[:, 1], cosine, sine).astype(jnp.bfloat16)
    values = shaped[:, 2].astype(jnp.bfloat16)
    all_keys, all_values = (
        lax.all_gather(keys.reshape(packs, local, inner), "context", axis=1, tiled=True),
        lax.all_gather(values.reshape(packs, local, inner), "context", axis=1, tiled=True),
    )
    query_packs = queries.reshape(packs, local, heads_here, HEAD_DIM)

    def scores_for(pack):
        key_block = all_keys[pack].reshape(group, heads_here, HEAD_DIM)
        raw = (
            jnp.einsum(
                "qhd,khd->hqk", query_packs[pack], key_block, preferred_element_type=jnp.float32
            )
            * score_scale
        )
        allowed = allowed_mask(
            query_number[pack],
            query_position[pack],
            query_index,
            key_number[pack],
            key_position[pack],
            key_valid[pack],
            key_index,
        )
        return jnp.where(allowed[None], raw, -1e30)

    pack = 0
    scores = scores_for(pack)
    top = jnp.max(scores, axis=-1, keepdims=True)
    total = jnp.log(jnp.sum(jnp.exp(scores - top), axis=-1, keepdims=True)) + top
    weights = jnp.exp(scores - total).astype(jnp.bfloat16)
    value_block = all_values[pack].reshape(group, heads_here, HEAD_DIM)
    head_blocks = [
        jnp.einsum("hqk,khd->qhd", weights, value_block, preferred_element_type=jnp.float32)
    ]
    totals = [total]
    mixed_heads = jnp.stack(head_blocks).reshape(rows, inner).astype(jnp.bfloat16)
    hidden = jnp.dot(
        normed_two, widening, preferred_element_type=jnp.float32
    ) + widening_bias.astype(jnp.float32)
    active = jax.nn.gelu(hidden, approximate=False).astype(jnp.bfloat16)
    attention_part = jnp.dot(mixed_heads, outgoing, preferred_element_type=jnp.float32)
    feed_part = jnp.dot(active, narrowing, preferred_element_type=jnp.float32)
    biases = outgoing_bias.astype(jnp.float32) + narrowing_bias.astype(jnp.float32)
    attention_sum, feed_sum = (
        lax.psum(attention_part.astype(jnp.bfloat16), "tensor").astype(jnp.float32),
        lax.psum(feed_part.astype(jnp.bfloat16), "tensor").astype(jnp.float32),
    )
    result = source + attention_sum + feed_sum + biases
    mixed = result.astype(jnp.bfloat16).reshape(packs, local, width)
    slope_out = cotangent.reshape(rows, width)
    slope_float = slope_out.astype(jnp.float32)
    outgoing_bias_slope = jnp.sum(slope_float, axis=0)
    outgoing_slope = jnp.einsum(
        "rf,rd->fd", mixed_heads, slope_out, preferred_element_type=jnp.float32
    )
    narrowing_slope = jnp.einsum("rf,rd->fd", active, slope_out, preferred_element_type=jnp.float32)
    heads_slope = jnp.einsum(
        "rd,fd->rf", slope_out, outgoing, preferred_element_type=jnp.float32
    ).astype(jnp.bfloat16)
    hidden_slope = (
        jnp.einsum("rd,fd->rf", slope_out, narrowing, preferred_element_type=jnp.float32)
        * gelu_slope(hidden)
    ).astype(jnp.bfloat16)
    widening_slope = jnp.einsum(
        "rd,rf->df", normed_two, hidden_slope, preferred_element_type=jnp.float32
    )
    widening_bias_slope = jnp.sum(hidden_slope.astype(jnp.float32), axis=0)
    second_back = jnp.einsum(
        "rf,df->rd", hidden_slope, widening, preferred_element_type=jnp.float32
    )
    heads_slope_packs = heads_slope.reshape(packs, local, heads_here, HEAD_DIM)
    balances = []
    pack = 0
    scores = scores_for(pack)
    probs = jnp.exp(scores - totals[pack])
    key_block = all_keys[pack].reshape(group, heads_here, HEAD_DIM)
    value_block = all_values[pack].reshape(group, heads_here, HEAD_DIM)
    outer = heads_slope_packs[pack]
    probs_slope = jnp.einsum("qhd,khd->hqk", outer, value_block, preferred_element_type=jnp.float32)
    balance = jnp.sum(probs * probs_slope, axis=-1, keepdims=True)
    balances.append(balance)
    score_slope = (probs * (probs_slope - balance)).astype(jnp.bfloat16)
    query_slopes = [
        jnp.einsum("hqk,khd->qhd", score_slope, key_block, preferred_element_type=jnp.float32)
        * score_scale
    ]
    weights = probs.astype(jnp.bfloat16)
    key_slopes = [
        jnp.einsum(
            "hqk,qhd->khd", score_slope, query_packs[pack], preferred_element_type=jnp.float32
        )
        * score_scale
    ]
    value_slopes = [jnp.einsum("hqk,qhd->khd", weights, outer, preferred_element_type=jnp.float32)]
    key_total, value_total = (
        lax.psum_scatter(
            jnp.stack(key_slopes).reshape(packs, group, inner).astype(jnp.bfloat16),
            "context",
            scatter_dimension=1,
            tiled=True,
        ).astype(jnp.float32),
        lax.psum_scatter(
            jnp.stack(value_slopes).reshape(packs, group, inner).astype(jnp.bfloat16),
            "context",
            scatter_dimension=1,
            tiled=True,
        ).astype(jnp.float32),
    )
    query_back = rotate_back(
        jnp.stack(query_slopes).reshape(rows, heads_here, HEAD_DIM), cosine, sine
    )
    key_back = rotate_back(key_total.reshape(rows, heads_here, HEAD_DIM), cosine, sine)
    projected_slope = jnp.stack(
        [
            query_back.reshape(rows, inner),
            key_back.reshape(rows, inner),
            value_total.reshape(rows, inner),
        ],
        axis=1,
    ).astype(jnp.bfloat16)
    projection_slope = jnp.einsum(
        "rd,rcf->dcf", normed_one, projected_slope, preferred_element_type=jnp.float32
    )
    projection_bias_slope = jnp.sum(projected_slope.astype(jnp.float32), axis=0)
    first_back = jnp.einsum(
        "rcf,dcf->rd", projected_slope, projection, preferred_element_type=jnp.float32
    )
    first_total, second_total = (
        lax.psum(first_back.astype(jnp.bfloat16), "tensor").astype(jnp.float32),
        lax.psum(second_back.astype(jnp.bfloat16), "tensor").astype(jnp.float32),
    )
    first_gain_slope = jnp.sum(first_total * unit_one, axis=0)
    first_shift_slope = jnp.sum(first_total, axis=0)
    second_gain_slope = jnp.sum(second_total * unit_two, axis=0)
    second_shift_slope = jnp.sum(second_total, axis=0)
    tokens_gradient = (
        slope_float
        + normalize_back(first_total, unit_one, factor_one, gain_one)
        + normalize_back(second_total, unit_two, factor_two, gain_two)
    )
    tokens_gradient = tokens_gradient.reshape(packs, local, width)
    owned = (
        lax.psum_scatter(
            projection_slope.astype(jnp.bfloat16), "fsdp", scatter_dimension=0, tiled=True
        ).astype(jnp.float32),
        lax.psum_scatter(
            projection_bias_slope.astype(jnp.bfloat16), "fsdp", scatter_dimension=1, tiled=True
        ).astype(jnp.float32),
        lax.psum_scatter(
            outgoing_slope.astype(jnp.bfloat16), "fsdp", scatter_dimension=1, tiled=True
        ).astype(jnp.float32),
        lax.psum_scatter(
            outgoing_bias_slope.astype(jnp.bfloat16), "fsdp", scatter_dimension=0, tiled=True
        ).astype(jnp.float32),
        lax.psum_scatter(
            widening_slope.astype(jnp.bfloat16), "fsdp", scatter_dimension=0, tiled=True
        ).astype(jnp.float32),
        lax.psum_scatter(
            widening_bias_slope.astype(jnp.bfloat16), "fsdp", scatter_dimension=0, tiled=True
        ).astype(jnp.float32),
        lax.psum_scatter(
            narrowing_slope.astype(jnp.bfloat16), "fsdp", scatter_dimension=1, tiled=True
        ).astype(jnp.float32),
        lax.psum_scatter(
            outgoing_bias_slope.astype(jnp.bfloat16), "fsdp", scatter_dimension=0, tiled=True
        ).astype(jnp.float32),
        lax.psum_scatter(
            first_gain_slope.astype(jnp.bfloat16), "fsdp", scatter_dimension=0, tiled=True
        ).astype(jnp.float32),
        lax.psum_scatter(
            first_shift_slope.astype(jnp.bfloat16), "fsdp", scatter_dimension=0, tiled=True
        ).astype(jnp.float32),
        lax.psum_scatter(
            second_gain_slope.astype(jnp.bfloat16), "fsdp", scatter_dimension=0, tiled=True
        ).astype(jnp.float32),
        lax.psum_scatter(
            second_shift_slope.astype(jnp.bfloat16), "fsdp", scatter_dimension=0, tiled=True
        ).astype(jnp.float32),
    )
    final = (
        lax.psum(owned[0].astype(jnp.bfloat16), "context").astype(jnp.float32),
        lax.psum(owned[1].astype(jnp.bfloat16), "context").astype(jnp.float32),
        lax.psum(owned[2].astype(jnp.bfloat16), "context").astype(jnp.float32),
        lax.psum(owned[3].astype(jnp.bfloat16), "context").astype(jnp.float32),
        lax.psum(owned[4].astype(jnp.bfloat16), "context").astype(jnp.float32),
        lax.psum(owned[5].astype(jnp.bfloat16), "context").astype(jnp.float32),
        lax.psum(owned[6].astype(jnp.bfloat16), "context").astype(jnp.float32),
        lax.psum(owned[7].astype(jnp.bfloat16), "context").astype(jnp.float32),
        lax.psum(owned[8].astype(jnp.bfloat16), "context").astype(jnp.float32),
        lax.psum(owned[9].astype(jnp.bfloat16), "context").astype(jnp.float32),
        lax.psum(owned[10].astype(jnp.bfloat16), "context").astype(jnp.float32),
        lax.psum(owned[11].astype(jnp.bfloat16), "context").astype(jnp.float32),
    )
    return (mixed, tokens_gradient) + tuple(final)


BLOCK = 256
FLOAT = jnp.float32
LOW = jnp.bfloat16


def nn(left, right):
    return lax.dot_general(left, right, (((1,), (0,)), ((), ())), preferred_element_type=FLOAT)


def nt(left, right):
    return lax.dot_general(left, right, (((1,), (1,)), ((), ())), preferred_element_type=FLOAT)


def tn(left, right):
    return lax.dot_general(left, right, (((0,), (0,)), ((), ())), preferred_element_type=FLOAT)


def center(values):
    average = jnp.mean(values, axis=-1, keepdims=True)
    centered = values - average
    spread = jnp.mean(centered * centered, axis=-1, keepdims=True)
    factor = lax.rsqrt(spread + epsilon)
    return centered * factor, factor


def widen_lanes(table, times):
    return jnp.concatenate([table] * times, axis=1)


def prepare_kernel(
    place, own_x, peer_x, own_g, peer_g, gain, shift, bias, weight, cos, left, right,
    q_out, k_out, v_out, o_out,
):
    inner = q_out.shape[1]
    step = pl.program_id(0)
    half = pl.num_programs(0) // 2

    def work(x_ref, g_ref):
        unit, _ = center(x_ref[...].astype(FLOAT))
        normed = (unit * gain[...] + shift[...]).astype(LOW)
        raw = nn(normed, weight[:, : 3 * inner + 64]) + bias[...]
        both = raw[:, : 2 * inner]
        times = 2 * inner // 128
        turned = (
            both * widen_lanes(cos[...], times)
            + pltpu.roll(both, 2 * inner - ROTARY // 2, 1) * widen_lanes(left[...], times)
            + pltpu.roll(both, ROTARY // 2, 1) * widen_lanes(right[...], times)
        )
        q_out[...] = (turned[:, :inner] * HEAD_DIM ** (-0.5)).astype(LOW)
        k_out[...] = turned[:, inner:].astype(LOW)
        v_out[...] = raw[:, 2 * inner : 3 * inner].astype(LOW)
        o_out[...] = nn(g_ref[...], weight[:, 3 * inner - 64 :])[:, 64:].astype(LOW)

    @pl.when(step < half)
    def _():
        work(own_x, own_g)

    @pl.when(step >= half)
    def _():
        work(peer_x, peer_g)


def prepare(place, own_x, peer_x, own_g, peer_g, gain, shift, bias, weight, tables, inner):
    rows, width = own_x.shape
    half = rows // BLOCK

    def own(s, place):
        return (jnp.minimum(s, half - 1), 0)

    def peer(s, place):
        return (jnp.maximum(s - half, 0), 0)

    def target(s, place):
        return (jnp.where(s < half, place[0] * half + s, (1 - place[0]) * half + s - half), 0)

    def fixed(s, place):
        return (0, 0)

    table = pl.BlockSpec((BLOCK, 128), target)
    return pl.pallas_call(
        prepare_kernel,
        grid_spec=pltpu.PrefetchScalarGridSpec(
            num_scalar_prefetch=1,
            grid=(2 * half,),
            in_specs=[
                pl.BlockSpec((BLOCK, width), own),
                pl.BlockSpec((BLOCK, width), peer),
                pl.BlockSpec((BLOCK, width), own),
                pl.BlockSpec((BLOCK, width), peer),
                pl.BlockSpec((1, width), fixed),
                pl.BlockSpec((1, width), fixed),
                pl.BlockSpec(bias.shape, fixed),
                pl.BlockSpec(weight.shape, fixed),
                table,
                table,
                table,
            ],
            out_specs=[pl.BlockSpec((BLOCK, inner), target)] * 4,
        ),
        out_shape=[jax.ShapeDtypeStruct((2 * rows, inner), LOW)] * 4,
        compiler_params=pltpu.CompilerParams(vmem_limit_bytes=40 << 20),
        cost_estimate=pl.CostEstimate(
            flops=2 * 2 * rows * width * 4 * inner, bytes_accessed=16 * rows * width, transcendentals=0
        ),
        name="prepare",
    )(place, own_x, peer_x, own_g, peer_g, gain, shift, bias, weight, *tables)


def attention_kernel(
    first, q_ref, k_ref, v_ref, o_ref, start_ref, stop_ref, cos, left, right,
    heads_out, slope_out,
    kt, vt, qm, om, probs, outer, dk, dv, ot, dqt,
):
    inner = q_ref.shape[1]
    heads = inner // HEAD_DIM
    wide = heads * BLOCK
    step = pl.program_id(0)
    count = pl.num_programs(0)
    block = count - 1 - step

    @pl.when(step == 0)
    def _():
        dk[...] = jnp.zeros_like(dk)
        dv[...] = jnp.zeros_like(dv)
        ot[...] = jnp.zeros_like(ot)
        dqt[...] = jnp.zeros_like(dqt)

        @pl.loop(0, count)
        def _(j):
            rows = pl.ds(pl.multiple_of(j * BLOCK, BLOCK), BLOCK)
            kt[:, rows] = jnp.transpose(k_ref[rows, :].astype(FLOAT)).astype(LOW)
            vt[:, rows] = jnp.transpose(v_ref[rows, :].astype(FLOAT)).astype(LOW)

    head = lax.broadcasted_iota(jnp.int32, (BLOCK, inner), 1) // HEAD_DIM
    query = q_ref[...].astype(FLOAT)
    slope = o_ref[...].astype(FLOAT)
    for h in range(heads):
        qm[h * BLOCK : (h + 1) * BLOCK, :] = jnp.where(head == h, query, 0.0).astype(LOW)
        om[h * BLOCK : (h + 1) * BLOCK, :] = jnp.where(head == h, slope, 0.0).astype(LOW)
    start = widen_lanes(start_ref[...], heads)
    stop = widen_lanes(stop_ref[...], heads)
    low = first[block]
    row = lax.broadcasted_iota(jnp.int32, (BLOCK, wide), 0)

    def span(j):
        return pl.ds(pl.multiple_of(j * BLOCK, BLOCK), BLOCK)

    def score(j, top):
        raw = nt(k_ref[span(j), :], qm[...])
        raw = jnp.where(row + j * BLOCK >= start, raw, -1e30)
        probs[span(j), :] = raw
        return jnp.maximum(top, jnp.max(raw, axis=0, keepdims=True))

    raw = nt(k_ref[span(block), :], qm[...])
    key = row + block * BLOCK
    itself = widen_lanes(
        lax.broadcasted_iota(jnp.int32, (1, BLOCK), 1) + block * BLOCK, heads
    )
    raw = jnp.where(((key >= start) & (key < stop)) | (key == itself), raw, -1e30)
    probs[span(block), :] = raw
    top = lax.fori_loop(low, block, score, jnp.max(raw, axis=0, keepdims=True))

    def weigh(j, carry):
        total, balance = carry
        weight = jnp.exp(probs[span(j), :] - top)
        back = nt(v_ref[span(j), :], om[...])
        probs[span(j), :] = weight
        outer[span(j), :] = back
        return (
            total + jnp.sum(weight, axis=0, keepdims=True),
            balance + jnp.sum(weight * back, axis=0, keepdims=True),
        )

    zero = jnp.zeros((1, wide), FLOAT)
    total, balance = lax.fori_loop(low, block + 1, weigh, (zero, zero))
    scale = 1.0 / total
    balance = balance * scale
    ot[:inner, :] = jnp.zeros((inner, BLOCK), FLOAT)
    dqt[:inner, :] = jnp.zeros((inner, BLOCK), FLOAT)

    @pl.loop(low, block + 1)
    def _(j):
        normal = probs[span(j), :] * scale
        weight = normal.astype(LOW)
        change = (normal * (outer[span(j), :] - balance)).astype(LOW)
        dv[span(j), :] += nn(weight, om[...])
        dk[span(j), :] += nn(change, qm[...])
        for h in range(heads):
            lines = slice(h * HEAD_DIM, (h + 1) * HEAD_DIM)
            lanes = slice(h * BLOCK, (h + 1) * BLOCK)
            ot[lines, :] += nn(vt[lines, span(j)], weight[:, lanes])
            dqt[lines, :] += nn(kt[lines, span(j)], change[:, lanes])

    heads_out[...] = jnp.transpose(ot[...])[:, :inner].astype(LOW)
    dq = jnp.transpose(dqt[...])[:, :inner] * HEAD_DIM ** (-0.5)
    both = jnp.concatenate([dq, dk[span(block), :]], axis=1)
    times = 2 * inner // 128
    turned = (
        both * widen_lanes(cos[...], times)
        - pltpu.roll(both, 2 * inner - ROTARY // 2, 1) * widen_lanes(left[...], times)
        - pltpu.roll(both, ROTARY // 2, 1) * widen_lanes(right[...], times)
    )
    slope_out[...] = jnp.concatenate([turned, dv[span(block), :]], axis=1).astype(LOW)


def attention(first, q, k, v, o, start, stop, tables):
    group, inner = q.shape
    count = group // BLOCK
    heads = inner // HEAD_DIM

    def rows(s, first):
        return (count - 1 - s, 0)

    def lanes(s, first):
        return (0, count - 1 - s)

    def fixed(s, first):
        return (0, 0)

    blocked = pl.BlockSpec((BLOCK, inner), rows)
    whole = pl.BlockSpec((group, inner), fixed)
    table = pl.BlockSpec((BLOCK, 128), rows)
    side = pl.BlockSpec((1, BLOCK), lanes)
    return pl.pallas_call(
        attention_kernel,
        grid_spec=pltpu.PrefetchScalarGridSpec(
            num_scalar_prefetch=1,
            grid=(count,),
            in_specs=[blocked, whole, whole, blocked, side, side, table, table, table],
            out_specs=[blocked, pl.BlockSpec((BLOCK, 3 * inner), rows)],
            scratch_shapes=[
                pltpu.VMEM((inner, group), LOW),
                pltpu.VMEM((inner, group), LOW),
                pltpu.VMEM((heads * BLOCK, inner), LOW),
                pltpu.VMEM((heads * BLOCK, inner), LOW),
                pltpu.VMEM((group, heads * BLOCK), FLOAT),
                pltpu.VMEM((group, heads * BLOCK), FLOAT),
                pltpu.VMEM((group, inner), FLOAT),
                pltpu.VMEM((group, inner), FLOAT),
                pltpu.VMEM((BLOCK, BLOCK), FLOAT),
                pltpu.VMEM((BLOCK, BLOCK), FLOAT),
            ],
        ),
        out_shape=[
            jax.ShapeDtypeStruct((group, inner), LOW),
            jax.ShapeDtypeStruct((group, 3 * inner), LOW),
        ],
        compiler_params=pltpu.CompilerParams(vmem_limit_bytes=48 << 20),
        cost_estimate=pl.CostEstimate(
            flops=40 * group * group * inner // 2, bytes_accessed=20 * group * inner, transcendentals=0
        ),
        name="attention",
    )(first, q, k, v, o, start, stop, *tables)


def feed_kernel(
    x_ref, g_ref, gain, shift, bias, wide, narrow,
    feed_out, e_out, wide_out, narrow_out, sums_out,
):
    step = pl.program_id(0)
    unit, _ = center(x_ref[...].astype(FLOAT))
    normed = (unit * gain[...] + shift[...]).astype(LOW)
    slope = g_ref[...]
    hidden = nn(normed, wide[...]) + bias[...]
    phi = 0.5 * (1.0 + lax.erf(hidden * 0.7071067811865476))
    active = (hidden * phi).astype(LOW)
    feed_out[...] = nt(active, narrow[...]).astype(LOW)
    inside = phi + hidden * jnp.exp(-0.5 * hidden * hidden) * 0.3989422804014327
    change = (nn(slope, narrow[...]) * inside).astype(LOW)
    back = nt(change, wide[...])
    e_out[...] = (back * gain[...]).astype(LOW)
    wide_part = tn(normed, change)
    narrow_part = tn(slope, active)
    sums = jnp.concatenate(
        [
            jnp.sum(back * unit, axis=0, keepdims=True),
            jnp.sum(back, axis=0, keepdims=True),
            jnp.sum(change.astype(FLOAT), axis=0, keepdims=True),
            jnp.sum(slope.astype(FLOAT), axis=0, keepdims=True),
            jnp.zeros((4, back.shape[1]), FLOAT),
        ],
        axis=0,
    )

    @pl.when(step == 0)
    def _():
        wide_out[...] = wide_part
        narrow_out[...] = narrow_part
        sums_out[...] = sums

    @pl.when(step > 0)
    def _():
        wide_out[...] += wide_part
        narrow_out[...] += narrow_part
        sums_out[...] += sums


def feed(x, g, gain, shift, bias, wide, narrow):
    rows, width = x.shape
    units = wide.shape[1]

    def moving(s):
        return (s, 0)

    def fixed(s):
        return (0, 0)

    return pl.pallas_call(
        feed_kernel,
        grid=(rows // BLOCK,),
        in_specs=[
            pl.BlockSpec((BLOCK, width), moving),
            pl.BlockSpec((BLOCK, width), moving),
            pl.BlockSpec((1, width), fixed),
            pl.BlockSpec((1, width), fixed),
            pl.BlockSpec((1, units), fixed),
            pl.BlockSpec((width, units), fixed),
            pl.BlockSpec((width, units), fixed),
        ],
        out_specs=[
            pl.BlockSpec((BLOCK, width), moving),
            pl.BlockSpec((BLOCK, width), moving),
            pl.BlockSpec((width, units), fixed),
            pl.BlockSpec((width, units), fixed),
            pl.BlockSpec((8, width), fixed),
        ],
        out_shape=[
            jax.ShapeDtypeStruct((rows, width), LOW),
            jax.ShapeDtypeStruct((rows, width), LOW),
            jax.ShapeDtypeStruct((width, units), FLOAT),
            jax.ShapeDtypeStruct((width, units), FLOAT),
            jax.ShapeDtypeStruct((8, width), FLOAT),
        ],
        compiler_params=pltpu.CompilerParams(vmem_limit_bytes=48 << 20),
        cost_estimate=pl.CostEstimate(
            flops=12 * rows * width * units, bytes_accessed=12 * rows * width, transcendentals=0
        ),
        name="feed",
    )(x, g, gain, shift, bias, wide, narrow)


def finish_kernel(
    place, x_ref, g_ref, heads_ref, slope_ref, feed_ref, e_ref, gain, shift, weight,
    mixed_out, e_out, weight_out, sums_out,
):
    step = pl.program_id(0)
    inner = heads_ref.shape[1]
    unit, _ = center(x_ref[...].astype(FLOAT))
    normed = (unit * gain[...] + shift[...]).astype(LOW)
    mixed = heads_ref[...]
    slope = slope_ref[...]
    pad = jnp.zeros((BLOCK, 64), LOW)
    lower = jnp.concatenate([pad, mixed], axis=1)
    mixed_out[...] = (
        nt(lower, weight[:, 3 * inner - 64 :]) + feed_ref[...].astype(FLOAT)
    ).astype(LOW)
    upper = jnp.concatenate([slope, pad], axis=1)
    back = nt(upper, weight[:, : 3 * inner + 64])
    e_out[...] = (back * gain[...] + e_ref[...].astype(FLOAT)).astype(LOW)
    part = jnp.concatenate([tn(normed, upper)[:, : 3 * inner], tn(g_ref[...], mixed)], axis=1)
    width = back.shape[1]
    sums = jnp.concatenate(
        [
            jnp.sum(back * unit, axis=0, keepdims=True),
            jnp.sum(back, axis=0, keepdims=True),
            jnp.sum(jnp.concatenate([slope, jnp.zeros((BLOCK, width - 3 * inner), LOW)], axis=1).astype(FLOAT), axis=0, keepdims=True),
            jnp.zeros((5, width), FLOAT),
        ],
        axis=0,
    )

    @pl.when(step == 0)
    def _():
        weight_out[...] = part
        sums_out[...] = sums

    @pl.when(step > 0)
    def _():
        weight_out[...] += part
        sums_out[...] += sums


def finish(place, x, g, heads, slope, feed_part, e, gain, shift, weight):
    rows, width = x.shape
    inner = heads.shape[1]
    count = rows // BLOCK

    def moving(s, place):
        return (s, 0)

    def shifted(s, place):
        return (place[0] * count + s, 0)

    def fixed(s, place):
        return (0, 0)

    token = pl.BlockSpec((BLOCK, width), moving)
    line = pl.BlockSpec((1, width), fixed)
    return pl.pallas_call(
        finish_kernel,
        grid_spec=pltpu.PrefetchScalarGridSpec(
            num_scalar_prefetch=1,
            grid=(count,),
            in_specs=[
                token,
                token,
                pl.BlockSpec((BLOCK, inner), shifted),
                pl.BlockSpec((BLOCK, 3 * inner), shifted),
                token,
                token,
                line,
                line,
                pl.BlockSpec(weight.shape, fixed),
            ],
            out_specs=[
                token,
                token,
                pl.BlockSpec(weight.shape, fixed),
                pl.BlockSpec((8, width), fixed),
            ],
        ),
        out_shape=[
            jax.ShapeDtypeStruct((rows, width), LOW),
            jax.ShapeDtypeStruct((rows, width), LOW),
            jax.ShapeDtypeStruct(weight.shape, FLOAT),
            jax.ShapeDtypeStruct((8, width), FLOAT),
        ],
        compiler_params=pltpu.CompilerParams(vmem_limit_bytes=48 << 20),
        cost_estimate=pl.CostEstimate(
            flops=16 * rows * width * inner, bytes_accessed=12 * rows * width, transcendentals=0
        ),
        name="finish",
    )(place, x, g, heads, slope, feed_part, e, gain, shift, weight)


PAIR = [(0, 1), (1, 0)]


def swap(value, axis):
    return lax.ppermute(value, axis, PAIR)


def ring_gather(piece):
    n = lax.axis_size("fsdp")
    order = list(range(0, n, 2)) + list(range(n - 1, 0, -2))
    forward = [(order[i], order[(i + 1) % n]) for i in range(n)]
    backward = [(b, a) for a, b in forward]
    me = lax.axis_index("fsdp")
    spot = jnp.where(me % 2 == 0, me // 2, n - 1 - me // 2)

    def owner(position):
        position = position % n
        return jnp.where(position < n // 2, 2 * position, 2 * (n - 1 - position) + 1)

    result = jnp.zeros((n,) + piece.shape, piece.dtype)
    result = lax.dynamic_update_index_in_dim(result, piece, me, 0)
    ahead = behind = piece
    for step in range(1, n // 2 + 1):
        ahead = lax.ppermute(ahead, "fsdp", forward)
        result = lax.dynamic_update_index_in_dim(result, ahead, owner(spot - step + n), 0)
        if step < n - n // 2:
            behind = lax.ppermute(behind, "fsdp", backward)
            result = lax.dynamic_update_index_in_dim(result, behind, owner(spot + step), 0)
    return result


def scatter_sum(parts):
    n = lax.axis_size("fsdp")
    depth = n // 2
    me = lax.axis_index("fsdp")
    z, x = me // 2, me % 2
    parts = parts.reshape((depth, 2) + parts.shape[1:])
    kept = lax.dynamic_index_in_dim(parts, x, 1, keepdims=False)
    sent = lax.dynamic_index_in_dim(parts, 1 - x, 1, keepdims=False)
    got = lax.ppermute(sent, "fsdp", [(i, i ^ 1) for i in range(n)])
    both = (kept.astype(FLOAT) + got.astype(FLOAT)).astype(LOW)
    total = lax.dynamic_index_in_dim(both, z, 0, keepdims=False).astype(FLOAT)
    for step in range(1, depth):
        pairs = [(2 * a + b, 2 * ((a + step) % depth) + b) for a in range(depth) for b in range(2)]
        piece = lax.dynamic_index_in_dim(both, (z + step) % depth, 0, keepdims=False)
        total = total + lax.ppermute(piece, "fsdp", pairs).astype(FLOAT)
    return total.astype(LOW)


def ordered(own, peer, index, axis=0):
    first = jnp.where(index == 0, own, peer)
    second = jnp.where(index == 0, peer, own)
    return jnp.concatenate([first, second], axis=axis)


def take_half(value, index, axis=0):
    size = value.shape[axis] // 2
    return lax.dynamic_slice_in_dim(value, index * size, size, axis)


def split_body(
    tokens,
    pack_lengths,
    cotangent,
    projection,
    projection_bias,
    outgoing,
    outgoing_bias,
    widening,
    widening_bias,
    narrowing,
    narrowing_bias,
    first_gain,
    first_shift,
    second_gain,
    second_shift,
):
    _, local, width = tokens.shape
    n = lax.axis_size("fsdp")
    group = 2 * local
    share = width // n
    y = lax.axis_index("context")
    core = lax.axis_index("tensor")
    own_x = tokens.reshape(local, width)
    own_g = cotangent.reshape(local, width)
    inner = outgoing.shape[0] // 2
    units = narrowing.shape[0] // 2

    def exchange(value):
        mine = swap(take_half(value, core), "context")
        return ordered(mine, swap(mine, "tensor"), core)

    vectors = jnp.concatenate(
        [
            first_gain,
            first_shift,
            second_gain,
            second_shift,
            outgoing_bias,
            narrowing_bias,
            projection_bias.reshape(-1),
            widening_bias,
        ]
    )
    extra = 8 * units
    vectors = jnp.pad(vectors, (0, extra - vectors.shape[0])).reshape(8, units)
    wide_piece = jnp.concatenate([take_half(widening, y, 1), vectors], axis=0)
    narrow_piece = take_half(narrowing, y, 0).T
    attend_piece = jnp.concatenate(
        [
            take_half(projection, y, 2).reshape(share, 3 * inner),
            take_half(outgoing, y, 0).T,
        ],
        axis=1,
    )
    peer_x = exchange(own_x)
    peer_g = exchange(own_g)
    gathered = ring_gather(wide_piece)
    wide = gathered[:, :share].reshape(width, units)
    flat = gathered[:, share:].reshape(n, extra)
    narrow = ring_gather(narrow_piece).reshape(width, units)
    attend = ring_gather(attend_piece).reshape(width, 3 * inner + inner)

    def line(index):
        return flat[:, index * share : (index + 1) * share].reshape(1, width).astype(FLOAT)

    gain_one, shift_one, gain_two, shift_two, out_bias, narrow_bias = (line(i) for i in range(6))
    base = 6 * share
    third = projection_bias.shape[1]
    bias_all = flat[:, base : base + 3 * third].reshape(n, 3, third).transpose(1, 0, 2)
    bias_all = bias_all.reshape(3, n * third)
    attend_bias = take_half(bias_all, y, 1).reshape(1, 3 * inner).astype(FLOAT)
    attend_bias = jnp.pad(attend_bias, ((0, 0), (0, 64)))
    base = base + 3 * third
    unit_bias = flat[:, base : base + widening_bias.shape[0]].reshape(1, -1)
    unit_bias = take_half(unit_bias, y, 1).astype(FLOAT)

    index = jnp.arange(group, dtype=jnp.int32)
    number, position, valid = layout(pack_lengths[0], index)
    begin = index - position
    labels = jnp.arange(SEQS, dtype=jnp.int32)
    length = jnp.sum(
        jnp.where(number[:, None] == labels[None, :], pack_lengths[0][None, :], 0), axis=1
    )
    stop = jnp.minimum(index + 1, begin + length)
    start = jnp.where(number == SEQS, index, begin)
    first = jnp.min(start.reshape(group // BLOCK, BLOCK), axis=1) // BLOCK
    frequency = 10000.0 ** (-jnp.arange(0, ROTARY, 2, dtype=FLOAT) / ROTARY)
    angles = frequency[:, None] * position.astype(FLOAT)[None, :]
    cosine, sine = jnp.cos(angles).T, jnp.sin(angles).T
    ones = jnp.ones((group, HEAD_DIM - ROTARY), FLOAT)
    none = jnp.zeros((group, ROTARY // 2), FLOAT)
    blank = jnp.zeros((group, HEAD_DIM - ROTARY), FLOAT)
    tables = (
        jnp.concatenate([cosine, cosine, ones] * 2, axis=1),
        jnp.concatenate([-sine, none, blank] * 2, axis=1),
        jnp.concatenate([none, sine, blank] * 2, axis=1),
    )
    place = y.reshape(1)
    other = 1 - place

    feed_own, e_own, wide_own, narrow_own, sums_own = feed(
        own_x, own_g, gain_two, shift_two, unit_bias, wide, narrow
    )
    feed_peer, e_peer, wide_peer, narrow_peer, sums_peer = feed(
        peer_x, peer_g, gain_two, shift_two, unit_bias, wide, narrow
    )
    g_sum = jnp.where(core == 0, 1.0, 0.0) * sums_own[3]
    sums_feed = sums_own + sums_peer
    narrow_total = scatter_sum((narrow_own + narrow_peer).astype(LOW).reshape(n, share, units))
    all_units = jnp.zeros((2, units), FLOAT)
    all_units = lax.dynamic_update_index_in_dim(all_units, sums_feed[2], y, 0)
    vector = jnp.concatenate(
        [
            sums_feed[0].reshape(n, share),
            sums_feed[1].reshape(n, share),
            g_sum.reshape(n, share),
            all_units.reshape(n, 2 * units // n),
        ],
        axis=1,
    )
    vector = jnp.pad(vector, ((0, 0), (0, extra - vector.shape[1]))).reshape(n, 8, units)
    wide_total = scatter_sum(
        jnp.concatenate(
            [(wide_own + wide_peer).reshape(n, share, units), vector], axis=1
        ).astype(LOW)
    )

    q, k, v, o = prepare(
        place, own_x, peer_x, own_g, peer_g, gain_one, shift_one, attend_bias, attend, tables, inner
    )
    heads, slope = attention(
        first, q, k, v, o, start.reshape(1, group), stop.reshape(1, group), tables
    )
    mixed_peer, e_peer, part_peer, sums_peer = finish(
        other, peer_x, peer_g, heads, slope, feed_peer, e_peer, gain_one, shift_one, attend
    )
    mixed_own, e_own, part_own, sums_own = finish(
        place, own_x, own_g, heads, slope, feed_own, e_own, gain_one, shift_one, attend
    )

    def reduce(own, peer):
        far = take_half(peer, core).astype(FLOAT) + swap(take_half(peer, 1 - core), "tensor").astype(FLOAT)
        far = swap(far.astype(LOW), "context").astype(FLOAT)
        near = take_half(own, core).astype(FLOAT) + swap(take_half(own, 1 - core), "tensor").astype(FLOAT)
        mine = (near + far).astype(LOW)
        return ordered(mine, swap(mine, "tensor"), core).astype(FLOAT)

    e_total = reduce(e_own, e_peer)
    mixed_total = reduce(mixed_own, mixed_peer)
    sums_attend = sums_own + sums_peer
    all_bias = jnp.zeros((3, 2, inner), FLOAT)
    all_bias = lax.dynamic_update_index_in_dim(
        all_bias, sums_attend[2, : 3 * inner].reshape(3, inner), y, 1
    )
    vector = jnp.concatenate(
        [
            sums_attend[0].reshape(n, share),
            sums_attend[1].reshape(n, share),
            all_bias.reshape(3, n, third).transpose(1, 0, 2).reshape(n, 3 * third),
        ],
        axis=1,
    )
    columns = 4 * inner
    vector = jnp.pad(vector, ((0, 0), (0, 8 * columns - vector.shape[1]))).reshape(n, 8, columns)
    attend_total = scatter_sum(
        jnp.concatenate([(part_own + part_peer).reshape(n, share, columns), vector], axis=1).astype(LOW)
    )

    source = own_x.astype(FLOAT)
    unit, factor = center(source)
    mixed = (source + mixed_total + out_bias + narrow_bias).astype(LOW)
    tokens_gradient = own_g.astype(FLOAT) + factor * (
        e_total
        - jnp.mean(e_total, axis=-1, keepdims=True)
        - unit * jnp.mean(e_total * unit, axis=-1, keepdims=True)
    )

    narrow_other = swap(narrow_total, "context")
    wide_other = swap(wide_total, "context")
    attend_other = swap(attend_total, "context")

    def joined(own, other):
        both = own.astype(FLOAT) + other.astype(FLOAT)
        return both.reshape(-1)

    narrow_slope = ordered(narrow_total.T, narrow_other.T, y, 0).astype(FLOAT)
    wide_slope = ordered(wide_total[:share], wide_other[:share], y, 1).astype(FLOAT)
    own, far = attend_total[:share], attend_other[:share]
    projection_slope = ordered(
        own[:, : 3 * inner].reshape(share, 3, inner), far[:, : 3 * inner].reshape(share, 3, inner), y, 2
    ).astype(FLOAT)
    outgoing_slope = ordered(own[:, 3 * inner :].T, far[:, 3 * inner :].T, y, 0).astype(FLOAT)
    feed_vector = joined(wide_total[share:], wide_other[share:])
    attend_vector = joined(attend_total[share:], attend_other[share:])
    across = jnp.concatenate([feed_vector[: 3 * share], attend_vector[: 2 * share]]).astype(LOW)
    across = across.astype(FLOAT) + swap(across, "tensor").astype(FLOAT)
    gains = across.reshape(5, share)
    bias_slope = attend_vector[2 * share : 2 * share + 3 * third].reshape(3, third)
    unit_slope = feed_vector[3 * share : 3 * share + 2 * units // n]
    return (
        mixed.reshape(tokens.shape),
        tokens_gradient.reshape(tokens.shape),
        projection_slope,
        bias_slope,
        outgoing_slope,
        gains[2],
        wide_slope,
        unit_slope,
        narrow_slope,
        gains[2],
        gains[3],
        gains[4],
        gains[0],
        gains[1],
    )


def body(*arrays):
    tokens, outgoing, narrowing = arrays[0], arrays[5], arrays[9]
    fits = (
        lax.axis_size("context") == 2
        and lax.axis_size("tensor") == 2
        and tokens.shape[0] == 1
        and tokens.shape[1] % BLOCK == 0
        and outgoing.shape[0] == 6 * HEAD_DIM
    )
    return split_body(*arrays) if fits else general_body(*arrays)


def solution(mesh):
    return jax.shard_map(
        body,
        mesh=mesh,
        in_specs=(
            P("fsdp", "context", None),
            P("fsdp", None),
            P("fsdp", "context", None),
            P("fsdp", None, "tensor"),
            P(None, ("tensor", "fsdp")),
            P("tensor", "fsdp"),
            P("fsdp"),
            P("fsdp", "tensor"),
            P(("tensor", "fsdp")),
            P("tensor", "fsdp"),
            P("fsdp"),
            P("fsdp"),
            P("fsdp"),
            P("fsdp"),
            P("fsdp"),
        ),
        out_specs=(
            P("fsdp", "context", None),
            P("fsdp", "context", None),
            P("fsdp", None, "tensor"),
            P(None, ("tensor", "fsdp")),
            P("tensor", "fsdp"),
            P("fsdp"),
            P("fsdp", "tensor"),
            P(("tensor", "fsdp")),
            P("tensor", "fsdp"),
            P("fsdp"),
            P("fsdp"),
            P("fsdp"),
            P("fsdp"),
            P("fsdp"),
        ),
        check_vma=False,
    )
```

```python
import functools

import jax
import jax.numpy as jnp
import numpy as np
from jax import lax
from jax.experimental import pallas as pl
from jax.experimental.pallas import tpu as pltpu
from jax.sharding import PartitionSpec as P

HEAD_DIM = 64
ROTARY = 16
TILE = 128
SEQS = 3


epsilon = 1e-05


def layout(lengths, index):
    padded = (lengths + TILE - 1) // TILE * TILE
    labels = jnp.arange(SEQS, dtype=jnp.int32)
    finish = jnp.sum(jnp.where(labels[:, None] <= labels[None, :], padded[:, None], 0), axis=0)
    before = (index[:, None] >= finish[None, :]).astype(jnp.int32)
    number = jnp.sum(before, axis=1)
    start = jnp.sum(before * padded[None, :], axis=1)
    position = index - start
    length = jnp.sum(jnp.where(number[:, None] == labels[None, :], lengths[None, :], 0), axis=1)
    return (number, position, position < length)


def turn_tables(position):
    frequency = 10000.0 ** (-jnp.arange(0, ROTARY, 2, dtype=jnp.float32) / ROTARY)
    angles = position.astype(jnp.float32)[:, None] * frequency[None, :]
    angles = jnp.concatenate([angles, angles], axis=1)
    return (jnp.cos(angles)[:, None, :], jnp.sin(angles)[:, None, :])


def rotate(field, cosine, sine):
    half = ROTARY // 2
    front = field[..., :ROTARY]
    turned = jnp.concatenate([-front[..., half:], front[..., :half]], axis=-1)
    return jnp.concatenate([front * cosine + turned * sine, field[..., ROTARY:]], axis=-1)


def rotate_back(slope, cosine, sine):
    half = ROTARY // 2
    front = slope[..., :ROTARY]
    scaled = front * sine
    turned = jnp.concatenate([scaled[..., half:], -scaled[..., :half]], axis=-1)
    return jnp.concatenate([front * cosine + turned, slope[..., ROTARY:]], axis=-1)


def normalize(values, gain, shift):
    average = jnp.mean(values, axis=-1, keepdims=True)
    centered = values - average
    spread = jnp.mean(centered * centered, axis=-1, keepdims=True)
    factor = lax.rsqrt(spread + epsilon)
    unit = centered * factor
    return (unit, factor, unit * gain + shift)


def normalize_back(slope, unit, factor, gain):
    scaled = slope * gain
    return factor * (
        scaled
        - jnp.mean(scaled, axis=-1, keepdims=True)
        - unit * jnp.mean(scaled * unit, axis=-1, keepdims=True)
    )


def gelu_slope(values):
    return (
        0.5 * (1.0 + lax.erf(values * 0.7071067811865476))
        + values * jnp.exp(-0.5 * values * values) * 0.3989422804014327
    )


def allowed_mask(
    query_number, query_position, query_index, key_number, key_position, key_valid, key_index
):
    same = (
        (query_number[:, None] == key_number[None, :])
        & (key_position[None, :] <= query_position[:, None])
        & key_valid[None, :]
    )
    return same | (query_index[:, None] == key_index[None, :])


def general_body(
    tokens,
    pack_lengths,
    cotangent,
    projection,
    projection_bias,
    outgoing,
    outgoing_bias,
    widening,
    widening_bias,
    narrowing,
    narrowing_bias,
    first_gain,
    first_shift,
    second_gain,
    second_shift,
):
    packs, local, width = tokens.shape
    group = local * lax.axis_size("context")
    rows = packs * local
    (
        projection,
        projection_bias,
        outgoing,
        outgoing_bias,
        widening,
        widening_bias,
        narrowing,
        narrowing_bias,
        first_gain,
        first_shift,
        second_gain,
        second_shift,
    ) = (
        lax.all_gather(projection, "fsdp", axis=0, tiled=True),
        lax.all_gather(projection_bias, "fsdp", axis=1, tiled=True),
        lax.all_gather(outgoing, "fsdp", axis=1, tiled=True),
        lax.all_gather(outgoing_bias, "fsdp", axis=0, tiled=True),
        lax.all_gather(widening, "fsdp", axis=0, tiled=True),
        lax.all_gather(widening_bias, "fsdp", axis=0, tiled=True),
        lax.all_gather(narrowing, "fsdp", axis=1, tiled=True),
        lax.all_gather(narrowing_bias, "fsdp", axis=0, tiled=True),
        lax.all_gather(first_gain, "fsdp", axis=0, tiled=True),
        lax.all_gather(first_shift, "fsdp", axis=0, tiled=True),
        lax.all_gather(second_gain, "fsdp", axis=0, tiled=True),
        lax.all_gather(second_shift, "fsdp", axis=0, tiled=True),
    )
    inner = projection.shape[2]
    heads_here = inner // HEAD_DIM
    score_scale = HEAD_DIM ** (-0.5)
    gain_one = first_gain.astype(jnp.float32)
    gain_two = second_gain.astype(jnp.float32)
    source = tokens.reshape(rows, width).astype(jnp.float32)
    unit_one, factor_one, normed_one = normalize(source, gain_one, first_shift.astype(jnp.float32))
    unit_two, factor_two, normed_two = normalize(source, gain_two, second_shift.astype(jnp.float32))
    normed_one = normed_one.astype(jnp.bfloat16)
    normed_two = normed_two.astype(jnp.bfloat16)
    projected = jnp.dot(
        normed_one, projection.reshape(width, 3 * inner), preferred_element_type=jnp.float32
    ).reshape(rows, 3, inner)
    projected = projected + projection_bias.astype(jnp.float32)[None]
    query_index = lax.axis_index("context") * local + jnp.arange(local, dtype=jnp.int32)
    key_index = jnp.arange(group, dtype=jnp.int32)
    query_number, query_position, query_valid = jax.vmap(layout, in_axes=(0, None))(
        pack_lengths, query_index
    )
    key_number, key_position, key_valid = jax.vmap(layout, in_axes=(0, None))(
        pack_lengths, key_index
    )
    cosine, sine = turn_tables(query_position.reshape(rows))
    shaped = projected.reshape(rows, 3, heads_here, HEAD_DIM)
    queries = rotate(shaped[:, 0], cosine, sine).astype(jnp.bfloat16)
    keys = rotate(shaped[:, 1], cosine, sine).astype(jnp.bfloat16)
    values = shaped[:, 2].astype(jnp.bfloat16)
    all_keys, all_values = (
        lax.all_gather(keys.reshape(packs, local, inner), "context", axis=1, tiled=True),
        lax.all_gather(values.reshape(packs, local, inner), "context", axis=1, tiled=True),
    )
    query_packs = queries.reshape(packs, local, heads_here, HEAD_DIM)

    def scores_for(pack):
        key_block = all_keys[pack].reshape(group, heads_here, HEAD_DIM)
        raw = (
            jnp.einsum(
                "qhd,khd->hqk", query_packs[pack], key_block, preferred_element_type=jnp.float32
            )
            * score_scale
        )
        allowed = allowed_mask(
            query_number[pack],
            query_position[pack],
            query_index,
            key_number[pack],
            key_position[pack],
            key_valid[pack],
            key_index,
        )
        return jnp.where(allowed[None], raw, -1e30)

    pack = 0
    scores = scores_for(pack)
    top = jnp.max(scores, axis=-1, keepdims=True)
    total = jnp.log(jnp.sum(jnp.exp(scores - top), axis=-1, keepdims=True)) + top
    weights = jnp.exp(scores - total).astype(jnp.bfloat16)
    value_block = all_values[pack].reshape(group, heads_here, HEAD_DIM)
    head_blocks = [
        jnp.einsum("hqk,khd->qhd", weights, value_block, preferred_element_type=jnp.float32)
    ]
    totals = [total]
    mixed_heads = jnp.stack(head_blocks).reshape(rows, inner).astype(jnp.bfloat16)
    hidden = jnp.dot(
        normed_two, widening, preferred_element_type=jnp.float32
    ) + widening_bias.astype(jnp.float32)
    active = jax.nn.gelu(hidden, approximate=False).astype(jnp.bfloat16)
    attention_part = jnp.dot(mixed_heads, outgoing, preferred_element_type=jnp.float32)
    feed_part = jnp.dot(active, narrowing, preferred_element_type=jnp.float32)
    biases = outgoing_bias.astype(jnp.float32) + narrowing_bias.astype(jnp.float32)
    attention_sum, feed_sum = (
        lax.psum(attention_part.astype(jnp.bfloat16), "tensor").astype(jnp.float32),
        lax.psum(feed_part.astype(jnp.bfloat16), "tensor").astype(jnp.float32),
    )
    result = source + attention_sum + feed_sum + biases
    mixed = result.astype(jnp.bfloat16).reshape(packs, local, width)
    slope_out = cotangent.reshape(rows, width)
    slope_float = slope_out.astype(jnp.float32)
    outgoing_bias_slope = jnp.sum(slope_float, axis=0)
    outgoing_slope = jnp.einsum(
        "rf,rd->fd", mixed_heads, slope_out, preferred_element_type=jnp.float32
    )
    narrowing_slope = jnp.einsum("rf,rd->fd", active, slope_out, preferred_element_type=jnp.float32)
    heads_slope = jnp.einsum(
        "rd,fd->rf", slope_out, outgoing, preferred_element_type=jnp.float32
    ).astype(jnp.bfloat16)
    hidden_slope = (
        jnp.einsum("rd,fd->rf", slope_out, narrowing, preferred_element_type=jnp.float32)
        * gelu_slope(hidden)
    ).astype(jnp.bfloat16)
    widening_slope = jnp.einsum(
        "rd,rf->df", normed_two, hidden_slope, preferred_element_type=jnp.float32
    )
    widening_bias_slope = jnp.sum(hidden_slope.astype(jnp.float32), axis=0)
    second_back = jnp.einsum(
        "rf,df->rd", hidden_slope, widening, preferred_element_type=jnp.float32
    )
    heads_slope_packs = heads_slope.reshape(packs, local, heads_here, HEAD_DIM)
    balances = []
    pack = 0
    scores = scores_for(pack)
    probs = jnp.exp(scores - totals[pack])
    key_block = all_keys[pack].reshape(group, heads_here, HEAD_DIM)
    value_block = all_values[pack].reshape(group, heads_here, HEAD_DIM)
    outer = heads_slope_packs[pack]
    probs_slope = jnp.einsum("qhd,khd->hqk", outer, value_block, preferred_element_type=jnp.float32)
    balance = jnp.sum(probs * probs_slope, axis=-1, keepdims=True)
    balances.append(balance)
    score_slope = (probs * (probs_slope - balance)).astype(jnp.bfloat16)
    query_slopes = [
        jnp.einsum("hqk,khd->qhd", score_slope, key_block, preferred_element_type=jnp.float32)
        * score_scale
    ]
    weights = probs.astype(jnp.bfloat16)
    key_slopes = [
        jnp.einsum(
            "hqk,qhd->khd", score_slope, query_packs[pack], preferred_element_type=jnp.float32
        )
        * score_scale
    ]
    value_slopes = [jnp.einsum("hqk,qhd->khd", weights, outer, preferred_element_type=jnp.float32)]
    key_total, value_total = (
        lax.psum_scatter(
            jnp.stack(key_slopes).reshape(packs, group, inner).astype(jnp.bfloat16),
            "context",
            scatter_dimension=1,
            tiled=True,
        ).astype(jnp.float32),
        lax.psum_scatter(
            jnp.stack(value_slopes).reshape(packs, group, inner).astype(jnp.bfloat16),
            "context",
            scatter_dimension=1,
            tiled=True,
        ).astype(jnp.float32),
    )
    query_back = rotate_back(
        jnp.stack(query_slopes).reshape(rows, heads_here, HEAD_DIM), cosine, sine
    )
    key_back = rotate_back(key_total.reshape(rows, heads_here, HEAD_DIM), cosine, sine)
    projected_slope = jnp.stack(
        [
            query_back.reshape(rows, inner),
            key_back.reshape(rows, inner),
            value_total.reshape(rows, inner),
        ],
        axis=1,
    ).astype(jnp.bfloat16)
    projection_slope = jnp.einsum(
        "rd,rcf->dcf", normed_one, projected_slope, preferred_element_type=jnp.float32
    )
    projection_bias_slope = jnp.sum(projected_slope.astype(jnp.float32), axis=0)
    first_back = jnp.einsum(
        "rcf,dcf->rd", projected_slope, projection, preferred_element_type=jnp.float32
    )
    first_total, second_total = (
        lax.psum(first_back.astype(jnp.bfloat16), "tensor").astype(jnp.float32),
        lax.psum(second_back.astype(jnp.bfloat16), "tensor").astype(jnp.float32),
    )
    first_gain_slope = jnp.sum(first_total * unit_one, axis=0)
    first_shift_slope = jnp.sum(first_total, axis=0)
    second_gain_slope = jnp.sum(second_total * unit_two, axis=0)
    second_shift_slope = jnp.sum(second_total, axis=0)
    tokens_gradient = (
        slope_float
        + normalize_back(first_total, unit_one, factor_one, gain_one)
        + normalize_back(second_total, unit_two, factor_two, gain_two)
    )
    tokens_gradient = tokens_gradient.reshape(packs, local, width)
    owned = (
        lax.psum_scatter(
            projection_slope.astype(jnp.bfloat16), "fsdp", scatter_dimension=0, tiled=True
        ).astype(jnp.float32),
        lax.psum_scatter(
            projection_bias_slope.astype(jnp.bfloat16), "fsdp", scatter_dimension=1, tiled=True
        ).astype(jnp.float32),
        lax.psum_scatter(
            outgoing_slope.astype(jnp.bfloat16), "fsdp", scatter_dimension=1, tiled=True
        ).astype(jnp.float32),
        lax.psum_scatter(
            outgoing_bias_slope.astype(jnp.bfloat16), "fsdp", scatter_dimension=0, tiled=True
        ).astype(jnp.float32),
        lax.psum_scatter(
            widening_slope.astype(jnp.bfloat16), "fsdp", scatter_dimension=0, tiled=True
        ).astype(jnp.float32),
        lax.psum_scatter(
            widening_bias_slope.astype(jnp.bfloat16), "fsdp", scatter_dimension=0, tiled=True
        ).astype(jnp.float32),
        lax.psum_scatter(
            narrowing_slope.astype(jnp.bfloat16), "fsdp", scatter_dimension=1, tiled=True
        ).astype(jnp.float32),
        lax.psum_scatter(
            outgoing_bias_slope.astype(jnp.bfloat16), "fsdp", scatter_dimension=0, tiled=True
        ).astype(jnp.float32),
        lax.psum_scatter(
            first_gain_slope.astype(jnp.bfloat16), "fsdp", scatter_dimension=0, tiled=True
        ).astype(jnp.float32),
        lax.psum_scatter(
            first_shift_slope.astype(jnp.bfloat16), "fsdp", scatter_dimension=0, tiled=True
        ).astype(jnp.float32),
        lax.psum_scatter(
            second_gain_slope.astype(jnp.bfloat16), "fsdp", scatter_dimension=0, tiled=True
        ).astype(jnp.float32),
        lax.psum_scatter(
            second_shift_slope.astype(jnp.bfloat16), "fsdp", scatter_dimension=0, tiled=True
        ).astype(jnp.float32),
    )
    final = (
        lax.psum(owned[0].astype(jnp.bfloat16), "context").astype(jnp.float32),
        lax.psum(owned[1].astype(jnp.bfloat16), "context").astype(jnp.float32),
        lax.psum(owned[2].astype(jnp.bfloat16), "context").astype(jnp.float32),
        lax.psum(owned[3].astype(jnp.bfloat16), "context").astype(jnp.float32),
        lax.psum(owned[4].astype(jnp.bfloat16), "context").astype(jnp.float32),
        lax.psum(owned[5].astype(jnp.bfloat16), "context").astype(jnp.float32),
        lax.psum(owned[6].astype(jnp.bfloat16), "context").astype(jnp.float32),
        lax.psum(owned[7].astype(jnp.bfloat16), "context").astype(jnp.float32),
        lax.psum(owned[8].astype(jnp.bfloat16), "context").astype(jnp.float32),
        lax.psum(owned[9].astype(jnp.bfloat16), "context").astype(jnp.float32),
        lax.psum(owned[10].astype(jnp.bfloat16), "context").astype(jnp.float32),
        lax.psum(owned[11].astype(jnp.bfloat16), "context").astype(jnp.float32),
    )
    return (mixed, tokens_gradient) + tuple(final)


BLOCK = 256
FLOAT = jnp.float32
LOW = jnp.bfloat16


def nn(left, right):
    return lax.dot_general(left, right, (((1,), (0,)), ((), ())), preferred_element_type=FLOAT)


def nt(left, right):
    return lax.dot_general(left, right, (((1,), (1,)), ((), ())), preferred_element_type=FLOAT)


def tn(left, right):
    return lax.dot_general(left, right, (((0,), (0,)), ((), ())), preferred_element_type=FLOAT)


def center(values):
    average = jnp.mean(values, axis=-1, keepdims=True)
    centered = values - average
    spread = jnp.mean(centered * centered, axis=-1, keepdims=True)
    factor = lax.rsqrt(spread + epsilon)
    return centered * factor, factor


def widen_lanes(table, times):
    return jnp.concatenate([table] * times, axis=1)


def call(kernel, name, place, steps, inputs, outputs, scratch=(), flops=0):
    def fixed(rank):
        return lambda s, place: (0,) * rank

    def spec(shape, block, index):
        return pl.BlockSpec(shape if block is None else block, fixed(len(shape)) if block is None else index)

    return pl.pallas_call(
        kernel,
        grid_spec=pltpu.PrefetchScalarGridSpec(
            num_scalar_prefetch=1,
            grid=(steps,),
            in_specs=[spec(array.shape, block, index) for array, block, index in inputs],
            out_specs=[spec(shape, block, index) for shape, _, block, index in outputs],
            scratch_shapes=list(scratch),
        ),
        out_shape=[jax.ShapeDtypeStruct(shape, kind) for shape, kind, _, _ in outputs],
        compiler_params=pltpu.CompilerParams(vmem_limit_bytes=48 << 20),
        cost_estimate=pl.CostEstimate(flops=1, bytes_accessed=1, transcendentals=0),
        name=name,
    )(place, *[array for array, _, _ in inputs])


ROWS = 512


def rank_two(value):
    return value.reshape(1, -1)


def pick(index, left, right):
    return jnp.where(index == 0, left, right)


def rolled(rows, shift, width):
    return pltpu.roll(
        jnp.concatenate([rows, jnp.zeros((rows.shape[0], width - rows.shape[1]), FLOAT)], axis=1), shift, 1
    )


def stacked(rows, width):
    rows = list(rows) + [jnp.zeros((16 - len(rows), width), FLOAT)]
    return jnp.concatenate(rows, axis=0).astype(LOW)


def pack_attend_kernel(place, project, out, gain, shift, first_bias, second_bias, third, piece):
    y, me = place[0], place[12]
    share = project.shape[1]
    inner = out.shape[1] // 2
    width = piece.shape[1]
    parts = []
    for c in range(3):
        block = project[c].astype(FLOAT)
        parts.append(pick(y, block[:, :inner], block[:, inner:]))
    parts.append(pick(y, out[:, :inner].astype(FLOAT), out[:, inner:].astype(FLOAT)))
    piece[:share, :] = jnp.concatenate(parts, axis=1).astype(LOW)
    rows = [rolled(ref[...].astype(FLOAT), me * share, width) for ref in (gain, shift, first_bias, second_bias)]
    bias = rolled(third[...].astype(FLOAT), me * third.shape[1], 2 * inner)
    bias = pick(y, bias[:, :inner], bias[:, inner:])
    bias = jnp.concatenate([bias[c : c + 1] for c in range(3)] + [jnp.zeros((1, width - 3 * inner), FLOAT)], axis=1)
    piece[share:, :] = stacked([rows[0], rows[1], bias, rows[2], rows[3]], width)


def pack_feed_kernel(place, wide, narrow, gain, shift, bias, piece):
    y, me = place[0], place[12]
    share = wide.shape[0]
    units = narrow.shape[1] // 2
    width = piece.shape[1]
    piece[:share, :] = pick(y, wide[:, :units].astype(FLOAT), wide[:, units:].astype(FLOAT)).astype(LOW)
    piece[share : 2 * share, :] = pick(
        y, narrow[:, :units].astype(FLOAT), narrow[:, units:].astype(FLOAT)
    ).astype(LOW)
    rows = [rolled(ref[...].astype(FLOAT), me * share, width) for ref in (gain, shift)]
    full = rolled(bias[...].astype(FLOAT), me * bias.shape[1], 2 * units)
    rows.append(pick(y, full[:, :units], full[:, units:]))
    piece[2 * share :, :] = stacked(rows, width)


def place_pieces(place, pieces, first, target, at, share):
    for spot, piece in enumerate(pieces):
        rows = pl.ds(pl.multiple_of(at + place[spot + 2] * share, 32), share)
        target[rows, :] = piece[first : first + share, :]


def sum_rows(pieces, first):
    total = pieces[0][first:, :].astype(FLOAT)
    for piece in pieces[1:]:
        total = total + piece[first:, :].astype(FLOAT)
    return total


def prepare_kernel(place, own_x, peer_x, coarse, fine, *refs):
    pieces, (q_out, k_out, v_out, weight, lines) = refs[:-5], refs[-5:]
    inner = q_out.shape[1]
    step = pl.program_id(0)
    half = pl.num_programs(0) // 2
    share = weight.shape[0] // 8

    @pl.when(step == 0)
    def _():
        place_pieces(place, pieces, 0, weight, 0, share)
        lines[...] = sum_rows(pieces, share)

    def work(x_ref):
        unit, _ = center(x_ref[...].astype(FLOAT))
        normed = (unit * lines[0:1, :] + lines[1:2, :]).astype(LOW)
        raw = nn(normed, weight[:, : 3 * inner + 64]) + lines[2:3, : 3 * inner + 64]
        both = raw[:, : 2 * inner]
        times = 2 * inner // 128
        tiles = ROWS // TILE
        block = jnp.where(step < half, place[0] * half + step, (1 - place[0]) * half + step - half)
        cosine, left, right = turns(place, 13 + block * tiles, tiles, coarse, fine)
        turned = (
            both * widen_lanes(cosine, times)
            + pltpu.roll(both, 2 * inner - ROTARY // 2, 1) * widen_lanes(left, times)
            + pltpu.roll(both, ROTARY // 2, 1) * widen_lanes(right, times)
        )
        q_out[...] = (turned[:, :inner] * HEAD_DIM ** (-0.5)).astype(LOW)
        k_out[...] = turned[:, inner:].astype(LOW)
        v_out[...] = raw[:, 2 * inner : 3 * inner].astype(LOW)

    @pl.when(step < half)
    def _():
        work(own_x)

    @pl.when(step >= half)
    def _():
        work(peer_x)


def turning():
    lane = np.arange(128)
    rate = 10000.0 ** (-2.0 * (lane % (ROTARY // 2)) / ROTARY) * (lane % HEAD_DIM < ROTARY)
    coarse = TILE * np.arange(16)[:, None] * rate[None, :]
    fine = np.arange(TILE)[:, None] * rate[None, :]
    tables = [np.concatenate([np.cos(t), np.sin(t)], axis=1) for t in (coarse, fine)]
    return [jnp.asarray(t.astype(np.float32)) for t in tables]


def turns(scalars, at, count, coarse, fine):
    lane = lax.broadcasted_iota(jnp.int32, (1, 128), 1) % HEAD_DIM
    cosines, sines = [], []
    for tile in range(count):
        row = coarse[pl.ds(scalars[at + tile], 1), :]
        cosines.append(row[:, :128] * fine[:, :128] - row[:, 128:] * fine[:, 128:])
        sines.append(row[:, 128:] * fine[:, :128] + row[:, :128] * fine[:, 128:])
    cosine = jnp.concatenate(cosines, axis=0)
    sine = jnp.concatenate(sines, axis=0)
    left = jnp.where(lane < ROTARY // 2, -sine, 0.0)
    right = jnp.where((lane >= ROTARY // 2) & (lane < ROTARY), sine, 0.0)
    return cosine, left, right


def halves(half):
    def own(s, place):
        return (jnp.minimum(s, half - 1), 0)

    def peer(s, place):
        return (jnp.maximum(s - half, 0), 0)

    def target(s, place):
        return (jnp.where(s < half, place[0] * half + s, (1 - place[0]) * half + s - half), 0)

    return own, peer, target


def prepare(place, own_x, peer_x, tables, pieces, inner):
    rows, width = own_x.shape
    half = rows // ROWS
    own, peer, target = halves(half)
    block = (ROWS, width)
    thin = ((2 * rows, inner), LOW, (ROWS, inner), target)
    return call(
        prepare_kernel,
        "prepare",
        place,
        2 * half,
        [(own_x, block, own), (peer_x, block, peer)]
        + [(table, None, None) for table in tables]
        + [(piece, None, None) for piece in pieces],
        [thin, thin, thin, ((width, 4 * inner), LOW, None, None), ((16, width), FLOAT, None, None)],
        flops=4 * rows * width * 3 * inner,
    )


def spread(source, target, head, heads):
    rows = source.shape[0]
    for h in range(heads):
        target[h * rows : (h + 1) * rows, :] = jnp.where(head == h, source, 0.0).astype(LOW)


def span(j):
    return pl.ds(pl.multiple_of(j * BLOCK, BLOCK), BLOCK)


def diagonal(raw, block, start, stop, heads):
    key = lax.broadcasted_iota(jnp.int32, raw.shape, 0) + block * BLOCK
    itself = widen_lanes(lax.broadcasted_iota(jnp.int32, (1, BLOCK), 1) + block * BLOCK, heads)
    return jnp.where(((key >= start) & (key < stop)) | (key == itself), raw, -1e30)


def forward_kernel(
    first, q_ref, k_ref, v_ref, start_ref, stop_ref,
    heads_out, total_out, exact_out,
    vt, qm, scores, ot,
):
    inner = q_ref.shape[1]
    heads = inner // HEAD_DIM
    wide = heads * BLOCK
    step = pl.program_id(0)
    count = pl.num_programs(0)
    block = count - 1 - step

    @pl.when(step == 0)
    def _():
        ot[...] = jnp.zeros_like(ot)

        @pl.loop(0, count)
        def _(j):
            vt[:, span(j)] = jnp.transpose(v_ref[span(j), :].astype(FLOAT)).astype(LOW)

    head = lax.broadcasted_iota(jnp.int32, (BLOCK, inner), 1) // HEAD_DIM
    spread(q_ref[...].astype(FLOAT), qm, head, heads)
    start = widen_lanes(start_ref[...], heads)
    stop = widen_lanes(stop_ref[...], heads)
    low = first[block]
    row = lax.broadcasted_iota(jnp.int32, (BLOCK, wide), 0)

    def score(j, top):
        raw = nt(k_ref[span(j), :], qm[...])
        raw = jnp.where(row >= start - j * BLOCK, raw, -1e30)
        scores[span(j), :] = raw
        return jnp.maximum(top, jnp.max(raw, axis=0, keepdims=True))

    raw = diagonal(nt(k_ref[span(block), :], qm[...]), block, start, stop, heads)
    scores[span(block), :] = raw
    top = lax.fori_loop(low, block, score, jnp.max(raw, axis=0, keepdims=True))
    ot[:inner, :] = jnp.zeros((inner, BLOCK), FLOAT)

    def weigh(j, total):
        weight = jnp.exp(scores[span(j), :] - top)
        rounded = weight.astype(LOW)
        for h in range(heads):
            lines = slice(h * HEAD_DIM, (h + 1) * HEAD_DIM)
            ot[lines, :] += nn(vt[lines, span(j)], rounded[:, h * BLOCK : (h + 1) * BLOCK])
        return total + jnp.sum(weight, axis=0, keepdims=True)

    total = lax.fori_loop(low, block + 1, weigh, jnp.zeros((1, wide), FLOAT))
    total_out[...] = (jnp.log(total) + top).reshape(1, 1, wide)
    scale = 1.0 / total
    for h in range(heads):
        lines = slice(h * HEAD_DIM, (h + 1) * HEAD_DIM)
        ot[lines, :] = ot[lines, :] * scale[:, h * BLOCK : (h + 1) * BLOCK]
    exact_out[...] = ot[:inner, :]
    heads_out[...] = jnp.transpose(ot[...])[:, :inner].astype(LOW)


def forward(first, q, k, v, start, stop):
    group, inner = q.shape
    count = group // BLOCK
    wide = inner // HEAD_DIM * BLOCK

    def rows(s, first):
        return (count - 1 - s, 0)

    def lanes(s, first):
        return (0, count - 1 - s)

    def deep(s, first):
        return (count - 1 - s, 0, 0)

    thin = (BLOCK, inner)
    stat = ((count, 1, wide), FLOAT, (1, 1, wide), deep)
    return call(
        forward_kernel,
        "forward",
        first,
        count,
        [(q, thin, rows), (k, None, None), (v, None, None)]
        + [(start, (1, BLOCK), lanes), (stop, (1, BLOCK), lanes)],
        [((group, inner), LOW, thin, rows), stat, ((inner, group), FLOAT, (inner, BLOCK), lanes)],
        [
            pltpu.VMEM((inner, group), LOW),
            pltpu.VMEM((wide, inner), LOW),
            pltpu.VMEM((group, wide), FLOAT),
            pltpu.VMEM((BLOCK, BLOCK), FLOAT),
        ],
        flops=8 * group * group * inner,
    )


def backward_kernel(
    first, q_ref, k_ref, v_ref, o_ref, start_ref, stop_ref, total_ref, exact_ref, coarse, fine,
    slope_out,
    kt, qm, om, dk, dv, dqt,
):
    inner = q_ref.shape[1]
    heads = inner // HEAD_DIM
    wide = heads * BLOCK
    step = pl.program_id(0)
    count = pl.num_programs(0)
    block = count - 1 - step

    @pl.when(step == 0)
    def _():
        dk[...] = jnp.zeros_like(dk)
        dv[...] = jnp.zeros_like(dv)
        dqt[...] = jnp.zeros_like(dqt)

        @pl.loop(0, count)
        def _(j):
            kt[:, span(j)] = jnp.transpose(k_ref[span(j), :].astype(FLOAT)).astype(LOW)

    head = lax.broadcasted_iota(jnp.int32, (BLOCK, inner), 1) // HEAD_DIM
    spread(q_ref[...].astype(FLOAT), qm, head, heads)
    outer = o_ref[...].astype(FLOAT)
    spread(outer, om, head, heads)
    product = exact_ref[...] * jnp.transpose(outer)
    start = widen_lanes(start_ref[...], heads)
    stop = widen_lanes(stop_ref[...], heads)
    total = total_ref[0]
    balance = jnp.concatenate(
        [
            jnp.sum(product[h * HEAD_DIM : (h + 1) * HEAD_DIM, :], axis=0, keepdims=True)
            for h in range(heads)
        ],
        axis=1,
    )
    row = lax.broadcasted_iota(jnp.int32, (BLOCK, wide), 0)
    dqt[:inner, :] = jnp.zeros((inner, BLOCK), FLOAT)

    def spend(j, raw):
        normal = jnp.exp(raw - total)
        weight = normal.astype(LOW)
        change = (normal * (nt(v_ref[span(j), :], om[...]) - balance)).astype(LOW)
        dv[span(j), :] += nn(weight, om[...])
        dk[span(j), :] += nn(change, qm[...])
        for h in range(heads):
            lines = slice(h * HEAD_DIM, (h + 1) * HEAD_DIM)
            dqt[lines, :] += nn(kt[lines, span(j)], change[:, h * BLOCK : (h + 1) * BLOCK])

    @pl.loop(first[block], block)
    def _(j):
        raw = nt(k_ref[span(j), :], qm[...])
        spend(j, jnp.where(row >= start - j * BLOCK, raw, -1e30))

    spend(block, diagonal(nt(k_ref[span(block), :], qm[...]), block, start, stop, heads))
    dq = jnp.transpose(dqt[...])[:, :inner] * HEAD_DIM ** (-0.5)
    both = jnp.concatenate([dq, dk[span(block), :]], axis=1)
    times = 2 * inner // 128
    tiles = BLOCK // TILE
    cosine, left, right = turns(first, count + block * tiles, tiles, coarse, fine)
    turned = (
        both * widen_lanes(cosine, times)
        - pltpu.roll(both, 2 * inner - ROTARY // 2, 1) * widen_lanes(left, times)
        - pltpu.roll(both, ROTARY // 2, 1) * widen_lanes(right, times)
    )
    slope_out[...] = jnp.concatenate([turned, dv[span(block), :]], axis=1).astype(LOW)


def backward(first, q, k, v, o, start, stop, total, exact, tables):
    group, inner = q.shape
    count = group // BLOCK
    wide = inner // HEAD_DIM * BLOCK

    def rows(s, first):
        return (count - 1 - s, 0)

    def lanes(s, first):
        return (0, count - 1 - s)

    def deep(s, first):
        return (count - 1 - s, 0, 0)

    thin = (BLOCK, inner)
    return call(
        backward_kernel,
        "backward",
        first,
        count,
        [(q, thin, rows), (k, None, None), (v, None, None), (o, thin, rows)]
        + [(start, (1, BLOCK), lanes), (stop, (1, BLOCK), lanes)]
        + [(total, (1, 1, wide), deep), (exact, (inner, BLOCK), lanes)]
        + [(table, None, None) for table in tables],
        [((group, 3 * inner), LOW, (BLOCK, 3 * inner), rows)],
        [
            pltpu.VMEM((inner, group), LOW),
            pltpu.VMEM((wide, inner), LOW),
            pltpu.VMEM((wide, inner), LOW),
            pltpu.VMEM((group, inner), FLOAT),
            pltpu.VMEM((group, inner), FLOAT),
            pltpu.VMEM((BLOCK, BLOCK), FLOAT),
        ],
        flops=16 * group * group * inner,
    )[0]


def mix_kernel(place, own_g, peer_g, heads_ref, weight, o_out, own_out, peer_out, extra, outer):
    inner = heads_ref.shape[1]
    step = pl.program_id(0)
    half = pl.num_programs(0) // 2
    share = weight.shape[0] // 8

    @pl.when(step == 0)
    def _():
        outer[...] = jnp.zeros_like(outer)

    def work(g_ref, target):
        heads = heads_ref[...]
        slope = g_ref[...]
        lower = jnp.concatenate([jnp.zeros((heads.shape[0], 64), LOW), heads], axis=1)
        o_out[...] = nn(slope, weight[:, 3 * inner - 64 :])[:, 64:].astype(LOW)
        target[...] = nt(lower, weight[:, 3 * inner - 64 :]).astype(LOW)
        outer[...] += tn(slope, heads)

    @pl.when(step < half)
    def _():
        work(own_g, own_out)

    @pl.when(step >= half)
    def _():
        work(peer_g, peer_out)

    @pl.when(step == 2 * half - 1)
    def _():
        for f in range(8):
            parts = [outer[f * share + 32 * c : f * share + 32 * (c + 1), :] for c in range(3)]
            parts.append(jnp.zeros((32, extra.shape[2] - 3 * inner), FLOAT))
            extra[f] = jnp.concatenate(parts, axis=1).astype(LOW)


def mix(place, own_g, peer_g, heads, weight):
    rows, width = own_g.shape
    inner = heads.shape[1]
    half = rows // ROWS
    own, peer, target = halves(half)
    block = (ROWS, width)
    thin = (ROWS, inner)
    return call(
        mix_kernel,
        "mix",
        place,
        2 * half,
        [(own_g, block, own), (peer_g, block, peer), (heads, thin, target), (weight, None, None)],
        [
            ((2 * rows, inner), LOW, thin, target),
            ((rows, width), LOW, block, own),
            ((rows, width), LOW, block, peer),
            ((8, 32, width), LOW, None, None),
        ],
        [pltpu.VMEM((width, inner), FLOAT)],
        12 * rows * width * inner,
    )


def write_parts(x, parts, kept, sent):
    for own in range(2):

        @pl.when(x == own)
        def _(own=own):
            for f in range(8):
                target = kept if f % 2 == own else sent
                for first, value in parts(f):
                    target[f // 2, first : first + value.shape[0], : value.shape[1]] = value


def feed_kernel(closing, place, x_ref, g_ref, m_in, *refs):
    if closing:
        weight, lines, total_in, sums_in, extra = refs[:5]
        m_far, m_near, e_out, kept, sent, total, sums_all = refs[5:]
    else:
        pieces = refs[:8]
        m_far, m_near, e_out, weight, lines, total, sums_all = refs[8:]
    step = pl.program_id(0)
    width = x_ref.shape[1]
    share = width // 8

    @pl.when(step == 0)
    def _():
        if closing:
            total[...] = total_in[...]
            sums_all[...] = sums_in[...]
        else:
            place_pieces(place, pieces, 0, weight, 0, share)
            place_pieces(place, pieces, share, weight, width, share)
            lines[...] = sum_rows(pieces, 2 * share)
            total[...] = jnp.zeros_like(total)
            sums_all[...] = jnp.zeros_like(sums_all)

    gain = lines[0:1, :]
    unit, _ = center(x_ref[...].astype(FLOAT))
    normed = (unit * gain + lines[1:2, :]).astype(LOW)
    slope = g_ref[...]
    hidden = nn(normed, weight[:width, :]) + lines[2:3, :]
    phi = 0.5 * (1.0 + lax.erf(hidden * 0.7071067811865476))
    active = (hidden * phi).astype(LOW)
    fed = (nt(active, weight[width:, :]) + m_in[...].astype(FLOAT)).astype(LOW)
    inside = phi + hidden * jnp.exp(-0.5 * hidden * hidden) * 0.3989422804014327
    change = (nn(slope, weight[width:, :]) * inside).astype(LOW)
    back = nt(change, weight[:width, :])
    e_out[...] = (back * gain).astype(LOW)
    total[:width, :] += tn(normed, change)
    total[width:, :] += tn(slope, active)
    rows = [
        jnp.sum(back * unit, axis=0, keepdims=True),
        jnp.sum(back, axis=0, keepdims=True),
        jnp.sum(change.astype(FLOAT), axis=0, keepdims=True),
    ]
    if not closing:
        once = jnp.where(place[1] == 0, 1.0, 0.0)
        rows.append(jnp.sum(slope.astype(FLOAT), axis=0, keepdims=True) * once)
    rows.append(jnp.zeros((16 - len(rows), width), FLOAT))
    sums_all[...] += jnp.concatenate(rows, axis=0)

    @pl.when(step == 0)
    def _():
        m_far[...] = fed

    @pl.when(step == 1)
    def _():
        m_near[...] = fed
        if closing:
            vectors = sums_all[...].astype(LOW)

            def parts(f):
                lines_of = slice(f * share, (f + 1) * share)
                later = slice(width + f * share, width + (f + 1) * share)
                return [
                    (0, total[lines_of, :].astype(LOW)),
                    (share, total[later, :].astype(LOW)),
                    (2 * share, vectors),
                    (2 * share + 16, extra[f]),
                ]

            write_parts(place[10], parts, kept, sent)


def crossed(s, place):
    return (jnp.where(s == 0, 1 - place[1], place[1]), 0)


def feed(place, x, g, m, pieces=None, weight=None, lines=None, sums=None, extra=None):
    rows, width = x.shape
    block = (ROWS, width)
    closing = sums is not None
    inputs = [(x, block, crossed), (g, block, crossed), (m, block, crossed)]
    outputs = [((ROWS, width), LOW, None, None)] * 2 + [((rows, width), LOW, block, crossed)]
    scratch = []
    if closing:
        inputs += [(array, None, None) for array in (weight, lines) + sums + (extra,)]
        outputs += [((4, width // 4 + 48, width), LOW, None, None)] * 2
        scratch = [pltpu.VMEM((2 * width, width), FLOAT), pltpu.VMEM((16, width), FLOAT)]
    else:
        inputs += [(piece, None, None) for piece in pieces]
        outputs += [
            ((2 * width, width), LOW, None, None),
            ((16, width), FLOAT, None, None),
            ((2 * width, width), FLOAT, None, None),
            ((16, width), FLOAT, None, None),
        ]
    kernel = functools.partial(feed_kernel, closing)
    return call(kernel, "feed", place, 2, inputs, outputs, scratch, 12 * rows * width * width)


def finish_kernel(
    place, own_x, peer_x, own_e, peer_e, slope_ref, lines, weight,
    peer_far, peer_near, own_far, own_near, kept, sent,
    total, sums_all,
):
    step = pl.program_id(0)
    half = pl.num_programs(0) // 2
    width, size = total.shape
    share = width // 8

    @pl.when(step == 0)
    def _():
        total[...] = jnp.zeros_like(total)
        sums_all[...] = jnp.zeros_like(sums_all)

    slope = jnp.concatenate([slope_ref[...], jnp.zeros((slope_ref.shape[0], 64), LOW)], axis=1)

    def work(x_ref, e_ref, targets):
        unit, _ = center(x_ref[...].astype(FLOAT))
        total[...] += tn(unit.astype(LOW), slope)
        sums_all[0:1, :] += jnp.sum(slope.astype(FLOAT), axis=0, keepdims=True)
        back = nt(slope, weight[:, :size])
        value = (back * lines[0:1, :] + e_ref[...].astype(FLOAT)).astype(LOW)
        for spot, target in enumerate(targets):

            @pl.when(step % half == spot)
            def _(target=target):
                target[...] = value

    @pl.when(step < half)
    def _():
        work(peer_x, peer_e, (peer_far, peer_near))

    @pl.when(step >= half)
    def _():
        work(own_x, own_e, (own_far, own_near))

    @pl.when(step == 2 * half - 1)
    def _():
        column = jnp.transpose(jnp.concatenate([lines[...], jnp.zeros((112, width), FLOAT)], axis=0))
        flat = sums_all[0:1, :]
        part = weight[:, :size].astype(FLOAT)
        lane = lax.broadcasted_iota(jnp.int32, (1, size), 1)
        part = jnp.where(lane < size - 64, part, 0.0)
        gain_part = jnp.sum(part * total[...], axis=1, keepdims=True)
        shift_part = jnp.sum(part * flat, axis=1, keepdims=True)
        both = jnp.concatenate([gain_part, shift_part, jnp.zeros((width, 126), FLOAT)], axis=1)
        both = jnp.transpose(both)
        middle = width // 2
        none = jnp.zeros((1, size - middle), FLOAT)
        vectors = [
            jnp.concatenate([both[line : line + 1, a : a + middle], none], axis=1)
            for line in range(2)
            for a in (0, middle)
        ]
        vectors = stacked(vectors + [flat], size)
        total[...] = total[...] * column[:, 0:1] + column[:, 1:2] * flat

        def parts(f):
            return [(0, total[f * share : (f + 1) * share, :].astype(LOW)), (share, vectors)]

        write_parts(place[10], parts, kept, sent)


def finish(place, own_x, peer_x, own_e, peer_e, slope, lines, weight):
    rows, width = own_x.shape
    size = slope.shape[1] + 64
    block = (ROWS, width)

    def peer(s, place):
        return (jnp.where(s == 0, 1 - place[1], place[1]), 0)

    def own(s, place):
        return (jnp.where(s < 3, 1 - place[1], place[1]), 0)

    def target(s, place):
        side = jnp.where(s < 2, 1 - place[0], place[0])
        return (2 * side + jnp.where(s % 2 == 0, 1 - place[1], place[1]), 0)

    return call(
        finish_kernel,
        "finish",
        place,
        4,
        [(own_x, block, own), (peer_x, block, peer), (own_e, block, own), (peer_e, block, peer)]
        + [(slope, (ROWS, slope.shape[1]), target), (lines, None, None), (weight, None, None)],
        [((ROWS, width), LOW, None, None)] * 4 + [((4, width // 8 + 16, size), LOW, None, None)] * 2,
        [pltpu.VMEM((width, size), FLOAT), pltpu.VMEM((8, size), FLOAT)],
    )


def cross_kernel(place, kept, got, own, *sent):
    for step, target in enumerate((own,) + sent):
        spot = lax.rem(place[11] + step, 4)
        target[...] = (kept[spot].astype(FLOAT) + got[spot].astype(FLOAT)).astype(LOW)


def cross(place, kept, got):
    return call(
        cross_kernel,
        "cross",
        place,
        1,
        [(kept, None, None), (got, None, None)],
        [(kept.shape[1:], LOW, None, None)] * 4,
    )


def last_feed_kernel(place, own, far, wide, narrow, out, sums, units):
    y = place[0]
    width = own.shape[1]
    share = width // 8
    inner = out.shape[1] // 2

    def both(first, count):
        mine = own[first : first + count, :].astype(FLOAT)
        theirs = far[first : first + count, :].astype(FLOAT)
        return mine, theirs, pick(y, mine, theirs), pick(y, theirs, mine)

    _, _, low, high = both(0, share)
    wide[...] = jnp.concatenate([low, high], axis=1)
    _, _, low, high = both(share, share)
    narrow[...] = jnp.concatenate([low, high], axis=1)
    mine, theirs, low, high = both(2 * share, 16)
    sums[...] = mine + theirs
    units[...] = jnp.concatenate([low[2:3, :], high[2:3, :]], axis=1)
    _, _, low, high = both(2 * share + 16, 32)

    def column(value):
        return jnp.concatenate([value[:, c * inner : (c + 1) * inner] for c in range(3)], axis=0)

    out[...] = jnp.concatenate([column(low), column(high)], axis=1)


def last_feed(place, own, far, inner):
    width = own.shape[1]
    share = width // 8
    return call(
        last_feed_kernel,
        "last_feed",
        place,
        1,
        [(own, None, None), (far, None, None)],
        [
            ((share, 2 * width), FLOAT, None, None),
            ((share, 2 * width), FLOAT, None, None),
            ((share, 2 * inner), FLOAT, None, None),
            ((16, width), FLOAT, None, None),
            ((1, 2 * width), FLOAT, None, None),
        ],
    )


def last_attend_kernel(place, own, far, project, sums, bias):
    y = place[0]
    _, share, double = project.shape
    inner = double // 2
    mine = own[:share, :].astype(FLOAT)
    theirs = far[:share, :].astype(FLOAT)
    low, high = pick(y, mine, theirs), pick(y, theirs, mine)
    for c in range(3):
        lanes = slice(c * inner, (c + 1) * inner)
        project[c] = jnp.concatenate([low[:, lanes], high[:, lanes]], axis=1)
    mine = own[share:, :].astype(FLOAT)
    theirs = far[share:, :].astype(FLOAT)
    sums[...] = mine + theirs
    low, high = pick(y, mine, theirs), pick(y, theirs, mine)
    rows = []
    for c in range(3):
        lanes = slice(c * inner, (c + 1) * inner)
        rows.append(jnp.concatenate([low[4:5, lanes], high[4:5, lanes]], axis=1))
    bias[...] = jnp.concatenate(rows, axis=0)


def last_attend(place, own, far, inner):
    share = own.shape[0] - 16
    return call(
        last_attend_kernel,
        "last_attend",
        place,
        1,
        [(own, None, None), (far, None, None)],
        [
            ((3, share, 2 * inner), FLOAT, None, None),
            ((16, own.shape[1]), FLOAT, None, None),
            ((3, 2 * inner), FLOAT, None, None),
        ],
    )


def settle_kernel(slope, place, x_ref, other_ref, mine, theirs, out):
    step = pl.program_id(0)
    source = x_ref[...].astype(FLOAT)

    def work(total):
        if slope:
            unit, factor = center(source)
            change = (
                total
                - jnp.mean(total, axis=-1, keepdims=True)
                - unit * jnp.mean(total * unit, axis=-1, keepdims=True)
            )
            out[...] = other_ref[...].astype(FLOAT) + factor * change
        else:
            out[...] = (source + total + (other_ref[3:4, :] + other_ref[4:5, :])).astype(LOW)

    @pl.when(step == place[1])
    def _():
        work(mine[...].astype(FLOAT))

    @pl.when(step != place[1])
    def _():
        work(theirs[...].astype(FLOAT))


def settle(place, slope, x, other, mine, theirs):
    rows, width = x.shape
    block = (ROWS, width)

    def moving(s, place):
        return (s, 0)

    return call(
        functools.partial(settle_kernel, slope),
        "settle",
        place,
        2,
        [(x, block, moving), (other, block, moving) if slope else (other, None, None)]
        + [(mine, None, None), (theirs, None, None)],
        [((rows, width), FLOAT if slope else LOW, block, moving)],
    )[0]


PAIR = [(0, 1), (1, 0)]


def swap(value, axis):
    return lax.ppermute(value, axis, PAIR)


def ring_order():
    return list(range(0, 8, 2)) + list(range(7, 0, -2))


def ring_owners(me):
    spot = jnp.where(me % 2 == 0, me // 2, 7 - me // 2)
    offsets = [0, -1, 1, -2, 2, -3, 3, -4]
    positions = [(spot + offset + 8) % 8 for offset in offsets]
    return [jnp.where(p < 4, 2 * p, 15 - 2 * p) for p in positions]


class Ring:
    def __init__(self, piece):
        self.pieces = [piece]
        self.ends = [piece, piece]
        order = ring_order()
        forward = [(order[i], order[(i + 1) % 8]) for i in range(8)]
        self.ways = [forward, [(b, a) for a, b in forward]]

    def step(self):
        ways = self.ways[: 8 - len(self.pieces)]
        self.ends = [lax.ppermute(end, "fsdp", way) for end, way in zip(self.ends, ways)]
        self.pieces += self.ends

    def newest(self):
        return tuple(self.ends)


def send_along(pieces):
    got = []
    for step, piece in enumerate(pieces, 1):
        pairs = [(2 * a + b, 2 * ((a + step) % 4) + b) for a in range(4) for b in range(2)]
        got.append(lax.ppermute(piece, "fsdp", pairs))
    return got


def add_along(own, got):
    total = own.astype(FLOAT)
    for piece in got:
        total = total + piece.astype(FLOAT)
    return total.astype(LOW)


def swap_x(value):
    return lax.ppermute(value, "fsdp", [(i, i ^ 1) for i in range(8)])


def after(values, *earlier):
    return lax.optimization_barrier((values, earlier))[0]


def add(*values):
    total = values[0].astype(FLOAT)
    for value in values[1:]:
        total = total + value.astype(FLOAT)
    return total.astype(LOW)


def ordered(own, peer, index, axis=0):
    first = jnp.where(index == 0, own, peer)
    second = jnp.where(index == 0, peer, own)
    return jnp.concatenate([first, second], axis=axis)


def take_half(value, index, axis=0):
    size = value.shape[axis] // 2
    return lax.dynamic_slice_in_dim(value, index * size, size, axis)


def split_body(
    tokens,
    pack_lengths,
    cotangent,
    projection,
    projection_bias,
    outgoing,
    outgoing_bias,
    widening,
    widening_bias,
    narrowing,
    narrowing_bias,
    first_gain,
    first_shift,
    second_gain,
    second_shift,
):
    _, local, width = tokens.shape
    group = 2 * local
    share = width // 8
    y = lax.axis_index("context")
    core = lax.axis_index("tensor")
    me = lax.axis_index("fsdp")
    own_x = tokens.reshape(local, width)
    own_g = cotangent.reshape(local, width)
    inner = outgoing.shape[0] // 2
    third = projection_bias.shape[1]
    owners = ring_owners(me)
    place = jnp.stack([y, core] + owners + [me % 2, me // 2, me])
    other = jnp.stack([1 - y, core] + owners + [me % 2, me // 2, me])

    def whole(*arrays):
        return [(array if array.ndim > 1 else rank_two(array), None, None) for array in arrays]

    attend_piece = call(
        pack_attend_kernel,
        "pack_attend",
        place,
        1,
        whole(projection.transpose(1, 0, 2), outgoing.T, first_gain, first_shift, outgoing_bias, narrowing_bias)
        + whole(projection_bias),
        [((share + 16, width), LOW, None, None)],
    )[0]
    index = jnp.arange(group, dtype=jnp.int32)
    number, position, valid = layout(pack_lengths[0], index)
    begin = index - position
    labels = jnp.arange(SEQS, dtype=jnp.int32)
    length = jnp.sum(
        jnp.where(number[:, None] == labels[None, :], pack_lengths[0][None, :], 0), axis=1
    )
    stop = jnp.minimum(index + 1, begin + length).reshape(1, group)
    start = jnp.where(number == SEQS, index, begin)
    first = jnp.min(start.reshape(group // BLOCK, BLOCK), axis=1) // BLOCK
    start = start.reshape(1, group)
    tiles = position.reshape(group // TILE, TILE)[:, 0] // TILE
    first = jnp.concatenate([first, tiles])
    tables = turning()
    place = jnp.concatenate([place, tiles])

    far_x = swap(take_half(own_x, core), "context")
    attend_ring = Ring(attend_piece)
    attend_ring.step()
    attend_ring.step()
    feed_piece = call(
        pack_feed_kernel,
        "pack_feed",
        place,
        1,
        whole(widening, narrowing.T, second_gain, second_shift, widening_bias),
        [((2 * share + 16, width), LOW, None, None)],
    )[0]
    feed_ring = Ring(after(feed_piece, attend_ring.newest()))
    attend_ring.step()
    far_x = after(far_x, attend_ring.newest())
    far_g = swap(after(take_half(own_g, core), far_x), "context")
    peer_x = ordered(far_x, swap(far_x, "tensor"), core)
    feed_ring.step()
    attend_ring.step()
    peer_x = after(peer_x, feed_ring.newest())
    feed_ring.step()
    q, k, v, attend_weight, attend_lines = prepare(place, own_x, peer_x, tables, attend_ring.pieces, inner)
    q, far_g = after((q, far_g), feed_ring.newest())
    feed_ring.step()
    near_g = swap(far_g, "tensor")
    heads, total, exact = forward(first, q, k, v, start, stop)
    heads, near_g, feed_ring.ends = after((heads, near_g, feed_ring.ends))
    feed_ring.step()
    peer_g = ordered(far_g, near_g, core)
    o, mixed_own, mixed_peer, extra = mix(place, own_g, peer_g, heads, attend_weight)

    own_far, own_near, e_own, weight, lines, totals, sums = feed(place, own_x, own_g, mixed_own, pieces=feed_ring.pieces)
    peer_far, peer_near, e_peer, kept, sent = feed(
        place, peer_x, peer_g, mixed_peer, weight=weight, lines=lines, sums=(totals, sums), extra=extra
    )
    got = swap_x(sent)
    gone = add(peer_near, swap(peer_far, "tensor"))
    mixed_far = swap(gone, "context")
    own_got = swap(own_far, "tensor")

    o = after(o, gone, own_got)
    slope = backward(first, q, k, v, o, start, stop, total, exact, tables)
    slope, got, mixed_far = after((slope, got, mixed_far))
    feed_cross = cross(place, kept, got)
    slope = after(slope, feed_cross)
    feed_got = send_along(feed_cross[1:])
    peer_far, peer_near, far_own, near_own, kept, sent = finish(
        place, own_x, peer_x, own_e=e_own, peer_e=e_peer, slope=slope, lines=attend_lines, weight=attend_weight
    )
    attend_got = swap_x(sent)
    peer_got = swap(peer_far, "tensor")
    e_got_own = swap(far_own, "tensor")
    gone = add(peer_near, peer_got)
    e_far = swap(gone, "context")
    feed_got = after(feed_got, gone)
    feed_sum = add_along(feed_cross[0], feed_got)
    feed_far = swap(feed_sum, "context")
    own_near = after(own_near, feed_sum)
    mine = add(own_near, own_got, mixed_far)
    mixed = settle(place, False, own_x, attend_lines, mine, swap(mine, "tensor"))
    attend_got = after(attend_got, feed_sum)
    attend_cross = cross(place, kept, attend_got)
    attend_along = send_along(attend_cross[1:])
    e_far = after(e_far, attend_cross[0])
    mine = add(near_own, e_got_own, e_far)
    attend_along = after(attend_along, mine)
    attend_sum = add_along(attend_cross[0], attend_along)
    attend_far = swap(attend_sum, "context")
    tokens_gradient = settle(place, True, own_x, own_g, mine, swap(mine, "tensor"))

    wide_slope, narrow_slope, outgoing_slope, feed_sums, unit_slope = last_feed(place, feed_sum, feed_far, inner)
    projection_slope, attend_sums, bias_slope = last_attend(place, attend_sum, attend_far, inner)

    def across(rows):
        part = lax.dynamic_slice_in_dim(rows.astype(LOW), me * share, share, 1)
        return part.astype(FLOAT) + swap(part, "tensor").astype(FLOAT)

    feed_lines = across(feed_sums[:8])
    attend_slopes = across(attend_sums[:4, : width // 2].reshape(2, width))
    unit_slope = lax.dynamic_slice_in_dim(unit_slope[0], me * (width // 4), width // 4)
    bias_slope = lax.dynamic_slice_in_dim(bias_slope, me * third, third, 1)
    return (
        mixed.reshape(tokens.shape),
        tokens_gradient.reshape(tokens.shape),
        projection_slope.transpose(1, 0, 2),
        bias_slope,
        outgoing_slope.T,
        feed_lines[3],
        wide_slope,
        unit_slope,
        narrow_slope.T,
        feed_lines[3],
        attend_slopes[0],
        attend_slopes[1],
        feed_lines[0],
        feed_lines[1],
    )


def body(*arrays):
    tokens, outgoing, narrowing = arrays[0], arrays[5], arrays[9]
    fits = (
        lax.axis_size("fsdp") == 8
        and lax.axis_size("context") == 2
        and lax.axis_size("tensor") == 2
        and tokens.shape[0] == 1
        and tokens.shape[1] == 2 * ROWS
        and outgoing.shape[0] == 6 * HEAD_DIM
        and tokens.shape[2] * 2 == narrowing.shape[0]
    )
    return split_body(*arrays) if fits else general_body(*arrays)


def solution(mesh):
    return jax.shard_map(
        body,
        mesh=mesh,
        in_specs=(
            P("fsdp", "context", None),
            P("fsdp", None),
            P("fsdp", "context", None),
            P("fsdp", None, "tensor"),
            P(None, ("tensor", "fsdp")),
            P("tensor", "fsdp"),
            P("fsdp"),
            P("fsdp", "tensor"),
            P(("tensor", "fsdp")),
            P("tensor", "fsdp"),
            P("fsdp"),
            P("fsdp"),
            P("fsdp"),
            P("fsdp"),
            P("fsdp"),
        ),
        out_specs=(
            P("fsdp", "context", None),
            P("fsdp", "context", None),
            P("fsdp", None, "tensor"),
            P(None, ("tensor", "fsdp")),
            P("tensor", "fsdp"),
            P("fsdp"),
            P("fsdp", "tensor"),
            P(("tensor", "fsdp")),
            P("tensor", "fsdp"),
            P("fsdp"),
            P("fsdp"),
            P("fsdp"),
            P("fsdp"),
            P("fsdp"),
        ),
        check_vma=False,
    )
```

```python
import functools

import jax
import jax.numpy as jnp
import numpy as np
from jax import lax
from jax.experimental import pallas as pl
from jax.experimental.pallas import tpu as pltpu
from jax.sharding import PartitionSpec as P

HEAD_DIM = 64
ROTARY = 16
TILE = 128
SEQS = 3


epsilon = 1e-05


def layout(lengths, index):
    padded = (lengths + TILE - 1) // TILE * TILE
    labels = jnp.arange(SEQS, dtype=jnp.int32)
    finish = jnp.sum(jnp.where(labels[:, None] <= labels[None, :], padded[:, None], 0), axis=0)
    before = (index[:, None] >= finish[None, :]).astype(jnp.int32)
    number = jnp.sum(before, axis=1)
    start = jnp.sum(before * padded[None, :], axis=1)
    position = index - start
    length = jnp.sum(jnp.where(number[:, None] == labels[None, :], lengths[None, :], 0), axis=1)
    return (number, position, position < length)


def turn_tables(position):
    frequency = 10000.0 ** (-jnp.arange(0, ROTARY, 2, dtype=jnp.float32) / ROTARY)
    angles = position.astype(jnp.float32)[:, None] * frequency[None, :]
    angles = jnp.concatenate([angles, angles], axis=1)
    return (jnp.cos(angles)[:, None, :], jnp.sin(angles)[:, None, :])


def rotate(field, cosine, sine):
    half = ROTARY // 2
    front = field[..., :ROTARY]
    turned = jnp.concatenate([-front[..., half:], front[..., :half]], axis=-1)
    return jnp.concatenate([front * cosine + turned * sine, field[..., ROTARY:]], axis=-1)


def rotate_back(slope, cosine, sine):
    half = ROTARY // 2
    front = slope[..., :ROTARY]
    scaled = front * sine
    turned = jnp.concatenate([scaled[..., half:], -scaled[..., :half]], axis=-1)
    return jnp.concatenate([front * cosine + turned, slope[..., ROTARY:]], axis=-1)


def normalize(values, gain, shift):
    average = jnp.mean(values, axis=-1, keepdims=True)
    centered = values - average
    spread = jnp.mean(centered * centered, axis=-1, keepdims=True)
    factor = lax.rsqrt(spread + epsilon)
    unit = centered * factor
    return (unit, factor, unit * gain + shift)


def normalize_back(slope, unit, factor, gain):
    scaled = slope * gain
    return factor * (
        scaled
        - jnp.mean(scaled, axis=-1, keepdims=True)
        - unit * jnp.mean(scaled * unit, axis=-1, keepdims=True)
    )


def gelu_slope(values):
    return (
        0.5 * (1.0 + lax.erf(values * 0.7071067811865476))
        + values * jnp.exp(-0.5 * values * values) * 0.3989422804014327
    )


def allowed_mask(
    query_number, query_position, query_index, key_number, key_position, key_valid, key_index
):
    same = (
        (query_number[:, None] == key_number[None, :])
        & (key_position[None, :] <= query_position[:, None])
        & key_valid[None, :]
    )
    return same | (query_index[:, None] == key_index[None, :])


def general_body(
    tokens,
    pack_lengths,
    cotangent,
    projection,
    projection_bias,
    outgoing,
    outgoing_bias,
    widening,
    widening_bias,
    narrowing,
    narrowing_bias,
    first_gain,
    first_shift,
    second_gain,
    second_shift,
):
    packs, local, width = tokens.shape
    group = local * lax.axis_size("context")
    rows = packs * local
    (
        projection,
        projection_bias,
        outgoing,
        outgoing_bias,
        widening,
        widening_bias,
        narrowing,
        narrowing_bias,
        first_gain,
        first_shift,
        second_gain,
        second_shift,
    ) = (
        lax.all_gather(projection, "fsdp", axis=0, tiled=True),
        lax.all_gather(projection_bias, "fsdp", axis=1, tiled=True),
        lax.all_gather(outgoing, "fsdp", axis=1, tiled=True),
        lax.all_gather(outgoing_bias, "fsdp", axis=0, tiled=True),
        lax.all_gather(widening, "fsdp", axis=0, tiled=True),
        lax.all_gather(widening_bias, "fsdp", axis=0, tiled=True),
        lax.all_gather(narrowing, "fsdp", axis=1, tiled=True),
        lax.all_gather(narrowing_bias, "fsdp", axis=0, tiled=True),
        lax.all_gather(first_gain, "fsdp", axis=0, tiled=True),
        lax.all_gather(first_shift, "fsdp", axis=0, tiled=True),
        lax.all_gather(second_gain, "fsdp", axis=0, tiled=True),
        lax.all_gather(second_shift, "fsdp", axis=0, tiled=True),
    )
    inner = projection.shape[2]
    heads_here = inner // HEAD_DIM
    score_scale = HEAD_DIM ** (-0.5)
    gain_one = first_gain.astype(jnp.float32)
    gain_two = second_gain.astype(jnp.float32)
    source = tokens.reshape(rows, width).astype(jnp.float32)
    unit_one, factor_one, normed_one = normalize(source, gain_one, first_shift.astype(jnp.float32))
    unit_two, factor_two, normed_two = normalize(source, gain_two, second_shift.astype(jnp.float32))
    normed_one = normed_one.astype(jnp.bfloat16)
    normed_two = normed_two.astype(jnp.bfloat16)
    projected = jnp.dot(
        normed_one, projection.reshape(width, 3 * inner), preferred_element_type=jnp.float32
    ).reshape(rows, 3, inner)
    projected = projected + projection_bias.astype(jnp.float32)[None]
    query_index = lax.axis_index("context") * local + jnp.arange(local, dtype=jnp.int32)
    key_index = jnp.arange(group, dtype=jnp.int32)
    query_number, query_position, query_valid = jax.vmap(layout, in_axes=(0, None))(
        pack_lengths, query_index
    )
    key_number, key_position, key_valid = jax.vmap(layout, in_axes=(0, None))(
        pack_lengths, key_index
    )
    cosine, sine = turn_tables(query_position.reshape(rows))
    shaped = projected.reshape(rows, 3, heads_here, HEAD_DIM)
    queries = rotate(shaped[:, 0], cosine, sine).astype(jnp.bfloat16)
    keys = rotate(shaped[:, 1], cosine, sine).astype(jnp.bfloat16)
    values = shaped[:, 2].astype(jnp.bfloat16)
    all_keys, all_values = (
        lax.all_gather(keys.reshape(packs, local, inner), "context", axis=1, tiled=True),
        lax.all_gather(values.reshape(packs, local, inner), "context", axis=1, tiled=True),
    )
    query_packs = queries.reshape(packs, local, heads_here, HEAD_DIM)

    def scores_for(pack):
        key_block = all_keys[pack].reshape(group, heads_here, HEAD_DIM)
        raw = (
            jnp.einsum(
                "qhd,khd->hqk", query_packs[pack], key_block, preferred_element_type=jnp.float32
            )
            * score_scale
        )
        allowed = allowed_mask(
            query_number[pack],
            query_position[pack],
            query_index,
            key_number[pack],
            key_position[pack],
            key_valid[pack],
            key_index,
        )
        return jnp.where(allowed[None], raw, -1e30)

    pack = 0
    scores = scores_for(pack)
    top = jnp.max(scores, axis=-1, keepdims=True)
    total = jnp.log(jnp.sum(jnp.exp(scores - top), axis=-1, keepdims=True)) + top
    weights = jnp.exp(scores - total).astype(jnp.bfloat16)
    value_block = all_values[pack].reshape(group, heads_here, HEAD_DIM)
    head_blocks = [
        jnp.einsum("hqk,khd->qhd", weights, value_block, preferred_element_type=jnp.float32)
    ]
    totals = [total]
    mixed_heads = jnp.stack(head_blocks).reshape(rows, inner).astype(jnp.bfloat16)
    hidden = jnp.dot(
        normed_two, widening, preferred_element_type=jnp.float32
    ) + widening_bias.astype(jnp.float32)
    active = jax.nn.gelu(hidden, approximate=False).astype(jnp.bfloat16)
    attention_part = jnp.dot(mixed_heads, outgoing, preferred_element_type=jnp.float32)
    feed_part = jnp.dot(active, narrowing, preferred_element_type=jnp.float32)
    biases = outgoing_bias.astype(jnp.float32) + narrowing_bias.astype(jnp.float32)
    attention_sum, feed_sum = (
        lax.psum(attention_part.astype(jnp.bfloat16), "tensor").astype(jnp.float32),
        lax.psum(feed_part.astype(jnp.bfloat16), "tensor").astype(jnp.float32),
    )
    result = source + attention_sum + feed_sum + biases
    mixed = result.astype(jnp.bfloat16).reshape(packs, local, width)
    slope_out = cotangent.reshape(rows, width)
    slope_float = slope_out.astype(jnp.float32)
    outgoing_bias_slope = jnp.sum(slope_float, axis=0)
    outgoing_slope = jnp.einsum(
        "rf,rd->fd", mixed_heads, slope_out, preferred_element_type=jnp.float32
    )
    narrowing_slope = jnp.einsum("rf,rd->fd", active, slope_out, preferred_element_type=jnp.float32)
    heads_slope = jnp.einsum(
        "rd,fd->rf", slope_out, outgoing, preferred_element_type=jnp.float32
    ).astype(jnp.bfloat16)
    hidden_slope = (
        jnp.einsum("rd,fd->rf", slope_out, narrowing, preferred_element_type=jnp.float32)
        * gelu_slope(hidden)
    ).astype(jnp.bfloat16)
    widening_slope = jnp.einsum(
        "rd,rf->df", normed_two, hidden_slope, preferred_element_type=jnp.float32
    )
    widening_bias_slope = jnp.sum(hidden_slope.astype(jnp.float32), axis=0)
    second_back = jnp.einsum(
        "rf,df->rd", hidden_slope, widening, preferred_element_type=jnp.float32
    )
    heads_slope_packs = heads_slope.reshape(packs, local, heads_here, HEAD_DIM)
    balances = []
    pack = 0
    scores = scores_for(pack)
    probs = jnp.exp(scores - totals[pack])
    key_block = all_keys[pack].reshape(group, heads_here, HEAD_DIM)
    value_block = all_values[pack].reshape(group, heads_here, HEAD_DIM)
    outer = heads_slope_packs[pack]
    probs_slope = jnp.einsum("qhd,khd->hqk", outer, value_block, preferred_element_type=jnp.float32)
    balance = jnp.sum(probs * probs_slope, axis=-1, keepdims=True)
    balances.append(balance)
    score_slope = (probs * (probs_slope - balance)).astype(jnp.bfloat16)
    query_slopes = [
        jnp.einsum("hqk,khd->qhd", score_slope, key_block, preferred_element_type=jnp.float32)
        * score_scale
    ]
    weights = probs.astype(jnp.bfloat16)
    key_slopes = [
        jnp.einsum(
            "hqk,qhd->khd", score_slope, query_packs[pack], preferred_element_type=jnp.float32
        )
        * score_scale
    ]
    value_slopes = [jnp.einsum("hqk,qhd->khd", weights, outer, preferred_element_type=jnp.float32)]
    key_total, value_total = (
        lax.psum_scatter(
            jnp.stack(key_slopes).reshape(packs, group, inner).astype(jnp.bfloat16),
            "context",
            scatter_dimension=1,
            tiled=True,
        ).astype(jnp.float32),
        lax.psum_scatter(
            jnp.stack(value_slopes).reshape(packs, group, inner).astype(jnp.bfloat16),
            "context",
            scatter_dimension=1,
            tiled=True,
        ).astype(jnp.float32),
    )
    query_back = rotate_back(
        jnp.stack(query_slopes).reshape(rows, heads_here, HEAD_DIM), cosine, sine
    )
    key_back = rotate_back(key_total.reshape(rows, heads_here, HEAD_DIM), cosine, sine)
    projected_slope = jnp.stack(
        [
            query_back.reshape(rows, inner),
            key_back.reshape(rows, inner),
            value_total.reshape(rows, inner),
        ],
        axis=1,
    ).astype(jnp.bfloat16)
    projection_slope = jnp.einsum(
        "rd,rcf->dcf", normed_one, projected_slope, preferred_element_type=jnp.float32
    )
    projection_bias_slope = jnp.sum(projected_slope.astype(jnp.float32), axis=0)
    first_back = jnp.einsum(
        "rcf,dcf->rd", projected_slope, projection, preferred_element_type=jnp.float32
    )
    first_total, second_total = (
        lax.psum(first_back.astype(jnp.bfloat16), "tensor").astype(jnp.float32),
        lax.psum(second_back.astype(jnp.bfloat16), "tensor").astype(jnp.float32),
    )
    first_gain_slope = jnp.sum(first_total * unit_one, axis=0)
    first_shift_slope = jnp.sum(first_total, axis=0)
    second_gain_slope = jnp.sum(second_total * unit_two, axis=0)
    second_shift_slope = jnp.sum(second_total, axis=0)
    tokens_gradient = (
        slope_float
        + normalize_back(first_total, unit_one, factor_one, gain_one)
        + normalize_back(second_total, unit_two, factor_two, gain_two)
    )
    tokens_gradient = tokens_gradient.reshape(packs, local, width)
    owned = (
        lax.psum_scatter(
            projection_slope.astype(jnp.bfloat16), "fsdp", scatter_dimension=0, tiled=True
        ).astype(jnp.float32),
        lax.psum_scatter(
            projection_bias_slope.astype(jnp.bfloat16), "fsdp", scatter_dimension=1, tiled=True
        ).astype(jnp.float32),
        lax.psum_scatter(
            outgoing_slope.astype(jnp.bfloat16), "fsdp", scatter_dimension=1, tiled=True
        ).astype(jnp.float32),
        lax.psum_scatter(
            outgoing_bias_slope.astype(jnp.bfloat16), "fsdp", scatter_dimension=0, tiled=True
        ).astype(jnp.float32),
        lax.psum_scatter(
            widening_slope.astype(jnp.bfloat16), "fsdp", scatter_dimension=0, tiled=True
        ).astype(jnp.float32),
        lax.psum_scatter(
            widening_bias_slope.astype(jnp.bfloat16), "fsdp", scatter_dimension=0, tiled=True
        ).astype(jnp.float32),
        lax.psum_scatter(
            narrowing_slope.astype(jnp.bfloat16), "fsdp", scatter_dimension=1, tiled=True
        ).astype(jnp.float32),
        lax.psum_scatter(
            outgoing_bias_slope.astype(jnp.bfloat16), "fsdp", scatter_dimension=0, tiled=True
        ).astype(jnp.float32),
        lax.psum_scatter(
            first_gain_slope.astype(jnp.bfloat16), "fsdp", scatter_dimension=0, tiled=True
        ).astype(jnp.float32),
        lax.psum_scatter(
            first_shift_slope.astype(jnp.bfloat16), "fsdp", scatter_dimension=0, tiled=True
        ).astype(jnp.float32),
        lax.psum_scatter(
            second_gain_slope.astype(jnp.bfloat16), "fsdp", scatter_dimension=0, tiled=True
        ).astype(jnp.float32),
        lax.psum_scatter(
            second_shift_slope.astype(jnp.bfloat16), "fsdp", scatter_dimension=0, tiled=True
        ).astype(jnp.float32),
    )
    final = (
        lax.psum(owned[0].astype(jnp.bfloat16), "context").astype(jnp.float32),
        lax.psum(owned[1].astype(jnp.bfloat16), "context").astype(jnp.float32),
        lax.psum(owned[2].astype(jnp.bfloat16), "context").astype(jnp.float32),
        lax.psum(owned[3].astype(jnp.bfloat16), "context").astype(jnp.float32),
        lax.psum(owned[4].astype(jnp.bfloat16), "context").astype(jnp.float32),
        lax.psum(owned[5].astype(jnp.bfloat16), "context").astype(jnp.float32),
        lax.psum(owned[6].astype(jnp.bfloat16), "context").astype(jnp.float32),
        lax.psum(owned[7].astype(jnp.bfloat16), "context").astype(jnp.float32),
        lax.psum(owned[8].astype(jnp.bfloat16), "context").astype(jnp.float32),
        lax.psum(owned[9].astype(jnp.bfloat16), "context").astype(jnp.float32),
        lax.psum(owned[10].astype(jnp.bfloat16), "context").astype(jnp.float32),
        lax.psum(owned[11].astype(jnp.bfloat16), "context").astype(jnp.float32),
    )
    return (mixed, tokens_gradient) + tuple(final)


BLOCK = 256
FLOAT = jnp.float32
LOW = jnp.bfloat16


def nn(left, right):
    return lax.dot_general(left, right, (((1,), (0,)), ((), ())), preferred_element_type=FLOAT)


def nt(left, right):
    return lax.dot_general(left, right, (((1,), (1,)), ((), ())), preferred_element_type=FLOAT)


def tn(left, right):
    return lax.dot_general(left, right, (((0,), (0,)), ((), ())), preferred_element_type=FLOAT)


def center(values):
    average = jnp.mean(values, axis=-1, keepdims=True)
    centered = values - average
    spread = jnp.mean(centered * centered, axis=-1, keepdims=True)
    factor = lax.rsqrt(spread + epsilon)
    return centered * factor, factor


def widen_lanes(table, times):
    return jnp.concatenate([table] * times, axis=1)


def call(kernel, name, place, steps, inputs, outputs, scratch=(), flops=0):
    def fixed(rank):
        return lambda s, place: (0,) * rank

    def spec(shape, block, index):
        return pl.BlockSpec(shape if block is None else block, fixed(len(shape)) if block is None else index)

    return pl.pallas_call(
        kernel,
        grid_spec=pltpu.PrefetchScalarGridSpec(
            num_scalar_prefetch=1,
            grid=(steps,),
            in_specs=[spec(array.shape, block, index) for array, block, index in inputs],
            out_specs=[spec(shape, block, index) for shape, _, block, index in outputs],
            scratch_shapes=list(scratch),
        ),
        out_shape=[jax.ShapeDtypeStruct(shape, kind) for shape, kind, _, _ in outputs],
        compiler_params=pltpu.CompilerParams(vmem_limit_bytes=48 << 20),
        cost_estimate=pl.CostEstimate(flops=1, bytes_accessed=1, transcendentals=0),
        name=name,
    )(place, *[array for array, _, _ in inputs])


ROWS = 512


def rank_two(value):
    return value.reshape(1, -1)


def pick(index, left, right):
    return jnp.where(index == 0, left, right)


def rolled(rows, shift, width):
    return pltpu.roll(
        jnp.concatenate([rows, jnp.zeros((rows.shape[0], width - rows.shape[1]), FLOAT)], axis=1), shift, 1
    )


def stacked(rows, width):
    rows = list(rows) + [jnp.zeros((16 - len(rows), width), FLOAT)]
    return jnp.concatenate(rows, axis=0).astype(LOW)


def pack_attend_kernel(place, project, out, gain, shift, first_bias, second_bias, third, piece):
    y, me = place[0], place[12]
    share = project.shape[1]
    inner = out.shape[1] // 2
    width = piece.shape[1]
    parts = []
    for c in range(3):
        block = project[c].astype(FLOAT)
        parts.append(pick(y, block[:, :inner], block[:, inner:]))
    parts.append(pick(y, out[:, :inner].astype(FLOAT), out[:, inner:].astype(FLOAT)))
    piece[:share, :] = jnp.concatenate(parts, axis=1).astype(LOW)
    rows = [rolled(ref[...].astype(FLOAT), me * share, width) for ref in (gain, shift, first_bias, second_bias)]
    bias = rolled(third[...].astype(FLOAT), me * third.shape[1], 2 * inner)
    bias = pick(y, bias[:, :inner], bias[:, inner:])
    bias = jnp.concatenate([bias[c : c + 1] for c in range(3)] + [jnp.zeros((1, width - 3 * inner), FLOAT)], axis=1)
    piece[share:, :] = stacked([rows[0], rows[1], bias, rows[2], rows[3]], width)


def pack_feed_kernel(place, wide, narrow, gain, shift, bias, piece):
    y, me = place[0], place[12]
    share = wide.shape[0]
    units = narrow.shape[1] // 2
    width = piece.shape[1]
    piece[:share, :] = pick(y, wide[:, :units].astype(FLOAT), wide[:, units:].astype(FLOAT)).astype(LOW)
    piece[share : 2 * share, :] = pick(
        y, narrow[:, :units].astype(FLOAT), narrow[:, units:].astype(FLOAT)
    ).astype(LOW)
    rows = [rolled(ref[...].astype(FLOAT), me * share, width) for ref in (gain, shift)]
    full = rolled(bias[...].astype(FLOAT), me * bias.shape[1], 2 * units)
    rows.append(pick(y, full[:, :units], full[:, units:]))
    piece[2 * share :, :] = stacked(rows, width)


def place_pieces(place, pieces, first, target, at, share):
    for spot, piece in enumerate(pieces):
        rows = pl.ds(pl.multiple_of(at + place[spot + 2] * share, 32), share)
        target[rows, :] = piece[first : first + share, :]


def sum_rows(pieces, first):
    total = pieces[0][first:, :].astype(FLOAT)
    for piece in pieces[1:]:
        total = total + piece[first:, :].astype(FLOAT)
    return total


def prepare_kernel(place, own_x, peer_x, coarse, fine, *refs):
    pieces, (q_out, k_out, v_out, weight, lines) = refs[:-5], refs[-5:]
    inner = q_out.shape[1]
    step = pl.program_id(0)
    half = pl.num_programs(0) // 2
    share = weight.shape[0] // 8

    @pl.when(step == 0)
    def _():
        place_pieces(place, pieces, 0, weight, 0, share)
        lines[...] = sum_rows(pieces, share)

    def work(x_ref):
        unit, _ = center(x_ref[...].astype(FLOAT))
        normed = (unit * lines[0:1, :] + lines[1:2, :]).astype(LOW)
        raw = nn(normed, weight[:, : 3 * inner + 64]) + lines[2:3, : 3 * inner + 64]
        both = raw[:, : 2 * inner]
        times = 2 * inner // 128
        tiles = ROWS // TILE
        block = jnp.where(step < half, place[0] * half + step, (1 - place[0]) * half + step - half)
        cosine, left, right = turns(place, 13 + block * tiles, tiles, coarse, fine)
        turned = (
            both * widen_lanes(cosine, times)
            + pltpu.roll(both, 2 * inner - ROTARY // 2, 1) * widen_lanes(left, times)
            + pltpu.roll(both, ROTARY // 2, 1) * widen_lanes(right, times)
        )
        q_out[...] = (turned[:, :inner] * HEAD_DIM ** (-0.5)).astype(LOW)
        k_out[...] = turned[:, inner:].astype(LOW)
        v_out[...] = raw[:, 2 * inner : 3 * inner].astype(LOW)

    @pl.when(step < half)
    def _():
        work(own_x)

    @pl.when(step >= half)
    def _():
        work(peer_x)


def turning():
    lane = np.arange(128)
    rate = 10000.0 ** (-2.0 * (lane % (ROTARY // 2)) / ROTARY) * (lane % HEAD_DIM < ROTARY)
    coarse = TILE * np.arange(16)[:, None] * rate[None, :]
    fine = np.arange(TILE)[:, None] * rate[None, :]
    tables = [np.concatenate([np.cos(t), np.sin(t)], axis=1) for t in (coarse, fine)]
    return [jnp.asarray(t.astype(np.float32)) for t in tables]


def turns(scalars, at, count, coarse, fine):
    lane = lax.broadcasted_iota(jnp.int32, (1, 128), 1) % HEAD_DIM
    cosines, sines = [], []
    for tile in range(count):
        row = coarse[pl.ds(scalars[at + tile], 1), :]
        cosines.append(row[:, :128] * fine[:, :128] - row[:, 128:] * fine[:, 128:])
        sines.append(row[:, 128:] * fine[:, :128] + row[:, :128] * fine[:, 128:])
    cosine = jnp.concatenate(cosines, axis=0)
    sine = jnp.concatenate(sines, axis=0)
    left = jnp.where(lane < ROTARY // 2, -sine, 0.0)
    right = jnp.where((lane >= ROTARY // 2) & (lane < ROTARY), sine, 0.0)
    return cosine, left, right


def halves(half):
    def own(s, place):
        return (jnp.minimum(s, half - 1), 0)

    def peer(s, place):
        return (jnp.maximum(s - half, 0), 0)

    def target(s, place):
        return (jnp.where(s < half, place[0] * half + s, (1 - place[0]) * half + s - half), 0)

    return own, peer, target


def prepare(place, own_x, peer_x, tables, pieces, inner):
    rows, width = own_x.shape
    half = rows // ROWS
    own, peer, target = halves(half)
    block = (ROWS, width)
    thin = ((2 * rows, inner), LOW, (ROWS, inner), target)
    return call(
        prepare_kernel,
        "prepare",
        place,
        2 * half,
        [(own_x, block, own), (peer_x, block, peer)]
        + [(table, None, None) for table in tables]
        + [(piece, None, None) for piece in pieces],
        [thin, thin, thin, ((width, 4 * inner), LOW, None, None), ((16, width), FLOAT, None, None)],
        flops=4 * rows * width * 3 * inner,
    )


def spread(source, target, head, heads):
    rows = source.shape[0]
    for h in range(heads):
        target[h * rows : (h + 1) * rows, :] = jnp.where(head == h, source, 0.0).astype(LOW)


def span(j, size=1):
    return pl.ds(pl.multiple_of(j * BLOCK, BLOCK), size * BLOCK)


def sweep(first, last, work, carry):
    pairs = (last - first) // 2
    carry = lax.fori_loop(0, pairs, lambda i, kept: work(2, first + 2 * i, kept), carry)
    return lax.fori_loop(first + 2 * pairs, last, lambda j, kept: work(1, j, kept), carry)


def diagonal(raw, block, start, stop, heads):
    key = lax.broadcasted_iota(jnp.int32, raw.shape, 0) + block * BLOCK
    itself = widen_lanes(lax.broadcasted_iota(jnp.int32, (1, BLOCK), 1) + block * BLOCK, heads)
    return jnp.where(((key >= start) & (key < stop)) | (key == itself), raw, -1e30)


def forward_kernel(
    first, q_ref, k_ref, v_ref, start_ref, stop_ref,
    heads_out, total_out, exact_out,
    vt, qm, scores, ot,
):
    inner = q_ref.shape[1]
    heads = inner // HEAD_DIM
    wide = heads * BLOCK
    step = pl.program_id(0)
    count = pl.num_programs(0)
    block = count - 1 - step

    @pl.when(step == 0)
    def _():
        ot[...] = jnp.zeros_like(ot)

        @pl.loop(0, count)
        def _(j):
            vt[:, span(j)] = jnp.transpose(v_ref[span(j), :].astype(FLOAT)).astype(LOW)

    head = lax.broadcasted_iota(jnp.int32, (BLOCK, inner), 1) // HEAD_DIM
    spread(q_ref[...].astype(FLOAT), qm, head, heads)
    start = widen_lanes(start_ref[...], heads)
    stop = widen_lanes(stop_ref[...], heads)
    low = first[block]
    row = lax.broadcasted_iota(jnp.int32, (BLOCK, wide), 0)

    def score(masked, size, j, top):
        raw = nt(k_ref[span(j, size), :], qm[...])
        if masked:
            raw = jnp.where(row >= start - j * BLOCK, raw, -1e30)
        scores[span(j, size), :] = raw
        return jnp.maximum(top, jnp.max(raw, axis=0, keepdims=True))

    raw = diagonal(nt(k_ref[span(block), :], qm[...]), block, start, stop, heads)
    scores[span(block), :] = raw
    clear = first[count + count * (BLOCK // TILE) + block]
    top = jnp.max(raw, axis=0, keepdims=True)
    top = lax.fori_loop(low, clear, functools.partial(score, True, 1), top)
    top = sweep(clear, block, functools.partial(score, False), top)
    ot[:inner, :] = jnp.zeros((inner, BLOCK), FLOAT)

    def weigh(size, j, total):
        weight = jnp.exp(scores[span(j, size), :] - top)
        rounded = weight.astype(LOW)
        for h in range(heads):
            lines = slice(h * HEAD_DIM, (h + 1) * HEAD_DIM)
            ot[lines, :] += nn(vt[lines, span(j, size)], rounded[:, h * BLOCK : (h + 1) * BLOCK])
        return total + jnp.sum(weight, axis=0, keepdims=True)

    total = sweep(low, block + 1, weigh, jnp.zeros((1, wide), FLOAT))
    total_out[...] = (jnp.log(total) + top).reshape(1, 1, wide)
    scale = 1.0 / total
    for h in range(heads):
        lines = slice(h * HEAD_DIM, (h + 1) * HEAD_DIM)
        ot[lines, :] = ot[lines, :] * scale[:, h * BLOCK : (h + 1) * BLOCK]
    exact_out[...] = ot[:inner, :]
    heads_out[...] = jnp.transpose(ot[...])[:, :inner].astype(LOW)


def forward(first, q, k, v, start, stop):
    group, inner = q.shape
    count = group // BLOCK
    wide = inner // HEAD_DIM * BLOCK

    def rows(s, first):
        return (count - 1 - s, 0)

    def lanes(s, first):
        return (0, count - 1 - s)

    def deep(s, first):
        return (count - 1 - s, 0, 0)

    thin = (BLOCK, inner)
    stat = ((count, 1, wide), FLOAT, (1, 1, wide), deep)
    return call(
        forward_kernel,
        "forward",
        first,
        count,
        [(q, thin, rows), (k, None, None), (v, None, None)]
        + [(start, (1, BLOCK), lanes), (stop, (1, BLOCK), lanes)],
        [((group, inner), LOW, thin, rows), stat, ((inner, group), FLOAT, (inner, BLOCK), lanes)],
        [
            pltpu.VMEM((inner, group), LOW),
            pltpu.VMEM((wide, inner), LOW),
            pltpu.VMEM((group, wide), FLOAT),
            pltpu.VMEM((BLOCK, BLOCK), FLOAT),
        ],
        flops=8 * group * group * inner,
    )


def backward_kernel(
    first, q_ref, k_ref, v_ref, o_ref, start_ref, stop_ref, total_ref, exact_ref, coarse, fine,
    slope_out,
    kt, qm, om, dk, dv, dqt,
):
    inner = q_ref.shape[1]
    heads = inner // HEAD_DIM
    wide = heads * BLOCK
    step = pl.program_id(0)
    count = pl.num_programs(0)
    block = count - 1 - step

    @pl.when(step == 0)
    def _():
        dk[...] = jnp.zeros_like(dk)
        dv[...] = jnp.zeros_like(dv)
        dqt[...] = jnp.zeros_like(dqt)

        @pl.loop(0, count)
        def _(j):
            kt[:, span(j)] = jnp.transpose(k_ref[span(j), :].astype(FLOAT)).astype(LOW)

    head = lax.broadcasted_iota(jnp.int32, (BLOCK, inner), 1) // HEAD_DIM
    spread(q_ref[...].astype(FLOAT), qm, head, heads)
    outer = o_ref[...].astype(FLOAT)
    spread(outer, om, head, heads)
    product = exact_ref[...] * jnp.transpose(outer)
    start = widen_lanes(start_ref[...], heads)
    stop = widen_lanes(stop_ref[...], heads)
    total = total_ref[0]
    balance = jnp.concatenate(
        [
            jnp.sum(product[h * HEAD_DIM : (h + 1) * HEAD_DIM, :], axis=0, keepdims=True)
            for h in range(heads)
        ],
        axis=1,
    )
    row = lax.broadcasted_iota(jnp.int32, (BLOCK, wide), 0)
    dqt[:inner, :] = jnp.zeros((inner, BLOCK), FLOAT)

    def spend(j, raw, size=1):
        normal = jnp.exp(raw - total)
        weight = normal.astype(LOW)
        change = (normal * (nt(v_ref[span(j, size), :], om[...]) - balance)).astype(LOW)
        dv[span(j, size), :] += nn(weight, om[...])
        dk[span(j, size), :] += nn(change, qm[...])
        for h in range(heads):
            lines = slice(h * HEAD_DIM, (h + 1) * HEAD_DIM)
            dqt[lines, :] += nn(kt[lines, span(j, size)], change[:, h * BLOCK : (h + 1) * BLOCK])

    clear = first[count + count * (BLOCK // TILE) + block]

    @pl.loop(first[block], clear)
    def _(j):
        raw = nt(k_ref[span(j), :], qm[...])
        spend(j, jnp.where(row >= start - j * BLOCK, raw, -1e30))

    def plain(size, j, carry):
        spend(j, nt(k_ref[span(j, size), :], qm[...]), size)
        return carry

    sweep(clear, block, plain, 0)

    spend(block, diagonal(nt(k_ref[span(block), :], qm[...]), block, start, stop, heads))
    dq = jnp.transpose(dqt[...])[:, :inner] * HEAD_DIM ** (-0.5)
    both = jnp.concatenate([dq, dk[span(block), :]], axis=1)
    times = 2 * inner // 128
    tiles = BLOCK // TILE
    cosine, left, right = turns(first, count + block * tiles, tiles, coarse, fine)
    turned = (
        both * widen_lanes(cosine, times)
        - pltpu.roll(both, 2 * inner - ROTARY // 2, 1) * widen_lanes(left, times)
        - pltpu.roll(both, ROTARY // 2, 1) * widen_lanes(right, times)
    )
    slope_out[...] = jnp.concatenate([turned, dv[span(block), :]], axis=1).astype(LOW)


def backward(first, q, k, v, o, start, stop, total, exact, tables):
    group, inner = q.shape
    count = group // BLOCK
    wide = inner // HEAD_DIM * BLOCK

    def rows(s, first):
        return (count - 1 - s, 0)

    def lanes(s, first):
        return (0, count - 1 - s)

    def deep(s, first):
        return (count - 1 - s, 0, 0)

    thin = (BLOCK, inner)
    return call(
        backward_kernel,
        "backward",
        first,
        count,
        [(q, thin, rows), (k, None, None), (v, None, None), (o, thin, rows)]
        + [(start, (1, BLOCK), lanes), (stop, (1, BLOCK), lanes)]
        + [(total, (1, 1, wide), deep), (exact, (inner, BLOCK), lanes)]
        + [(table, None, None) for table in tables],
        [((group, 3 * inner), LOW, (BLOCK, 3 * inner), rows)],
        [
            pltpu.VMEM((inner, group), LOW),
            pltpu.VMEM((wide, inner), LOW),
            pltpu.VMEM((wide, inner), LOW),
            pltpu.VMEM((group, inner), FLOAT),
            pltpu.VMEM((group, inner), FLOAT),
            pltpu.VMEM((BLOCK, BLOCK), FLOAT),
        ],
        flops=16 * group * group * inner,
    )[0]


def mix_kernel(place, own_g, peer_g, heads_ref, weight, o_out, own_out, peer_out, extra, outer):
    inner = heads_ref.shape[1]
    step = pl.program_id(0)
    half = pl.num_programs(0) // 2
    share = weight.shape[0] // 8

    @pl.when(step == 0)
    def _():
        outer[...] = jnp.zeros_like(outer)

    def work(g_ref, target):
        heads = heads_ref[...]
        slope = g_ref[...]
        lower = jnp.concatenate([jnp.zeros((heads.shape[0], 64), LOW), heads], axis=1)
        o_out[...] = nn(slope, weight[:, 3 * inner - 64 :])[:, 64:].astype(LOW)
        target[...] = nt(lower, weight[:, 3 * inner - 64 :]).astype(LOW)
        outer[...] += tn(slope, heads)

    @pl.when(step < half)
    def _():
        work(own_g, own_out)

    @pl.when(step >= half)
    def _():
        work(peer_g, peer_out)

    @pl.when(step == 2 * half - 1)
    def _():
        for f in range(8):
            parts = [outer[f * share + 32 * c : f * share + 32 * (c + 1), :] for c in range(3)]
            parts.append(jnp.zeros((32, extra.shape[2] - 3 * inner), FLOAT))
            extra[f] = jnp.concatenate(parts, axis=1).astype(LOW)


def mix(place, own_g, peer_g, heads, weight):
    rows, width = own_g.shape
    inner = heads.shape[1]
    half = rows // ROWS
    own, peer, target = halves(half)
    block = (ROWS, width)
    thin = (ROWS, inner)
    return call(
        mix_kernel,
        "mix",
        place,
        2 * half,
        [(own_g, block, own), (peer_g, block, peer), (heads, thin, target), (weight, None, None)],
        [
            ((2 * rows, inner), LOW, thin, target),
            ((rows, width), LOW, block, own),
            ((rows, width), LOW, block, peer),
            ((8, 32, width), LOW, None, None),
        ],
        [pltpu.VMEM((width, inner), FLOAT)],
        12 * rows * width * inner,
    )


def write_parts(x, parts, kept, sent):
    for own in range(2):

        @pl.when(x == own)
        def _(own=own):
            for f in range(8):
                target = kept if f % 2 == own else sent
                for first, value in parts(f):
                    target[f // 2, first : first + value.shape[0], : value.shape[1]] = value


def feed_kernel(place, own_x, peer_x, own_g, peer_g, own_m, peer_m, *refs):
    pieces, extra, refs = refs[:8], refs[8], refs[9:]
    own_far, own_near, peer_far, peer_near, own_e, peer_e, kept, sent, *later, weight, lines, total, sums_all = refs
    step = pl.program_id(0)
    half = pl.num_programs(0) // 2
    width = own_x.shape[1]
    share = width // 8

    @pl.when(step == 0)
    def _():
        place_pieces(place, pieces, 0, weight, 0, share)
        place_pieces(place, pieces, share, weight, width, share)
        lines[...] = sum_rows(pieces, 2 * share)
        total[...] = jnp.zeros_like(total)
        sums_all[...] = jnp.zeros_like(sums_all)

    def work(x_ref, g_ref, m_ref, e_out, targets, once):
        gain = lines[0:1, :]
        unit, _ = center(x_ref[...].astype(FLOAT))
        normed = (unit * gain + lines[1:2, :]).astype(LOW)
        slope = g_ref[...]
        hidden = nn(normed, weight[:width, :]) + lines[2:3, :]
        phi = 0.5 * (1.0 + lax.erf(hidden * 0.7071067811865476))
        active = (hidden * phi).astype(LOW)
        fed = (nt(active, weight[width:, :]) + m_ref[...].astype(FLOAT)).astype(LOW)
        inside = phi + hidden * jnp.exp(-0.5 * hidden * hidden) * 0.3989422804014327
        change = (nn(slope, weight[width:, :]) * inside).astype(LOW)
        back = nt(change, weight[:width, :])
        e_out[...] = (back * gain).astype(LOW)
        total[:width, :] += tn(normed, change)
        total[width:, :] += tn(slope, active)
        rows = [
            jnp.sum(back * unit, axis=0, keepdims=True),
            jnp.sum(back, axis=0, keepdims=True),
            jnp.sum(change.astype(FLOAT), axis=0, keepdims=True),
            jnp.sum(slope.astype(FLOAT), axis=0, keepdims=True) * once,
            jnp.zeros((12, width), FLOAT),
        ]
        sums_all[...] += jnp.concatenate(rows, axis=0)
        for spot, target in enumerate(targets):

            @pl.when(step % half == spot)
            def _(target=target):
                target[...] = fed

    @pl.when(step < half)
    def _():
        work(own_x, own_g, own_m, own_e, (own_far, own_near), jnp.where(place[1] == 0, 1.0, 0.0))

    @pl.when(step >= half)
    def _():
        work(peer_x, peer_g, peer_m, peer_e, (peer_far, peer_near), 0.0)

    @pl.when(step == 2 * half - 1)
    def _():
        vectors = sums_all[...].astype(LOW)

        def parts(f):
            return [(0, total[f * share : (f + 1) * share, :].astype(LOW)), (share, vectors)]

        write_parts(place[10], parts, kept, sent)
        for ahead, target in enumerate(later):
            depth = lax.rem(place[11] + ahead, 4)
            for side in range(2):
                f = 2 * depth + side
                target[side, :share, :] = total[pl.ds(pl.multiple_of(width + f * share, 32), share), :].astype(LOW)
                target[side, share:, :] = extra[f]


def crossed(first):
    def index(s, place):
        return (jnp.where(s <= first, 1 - place[1], place[1]), 0)

    return index


def feed(place, own_x, peer_x, own_g, peer_g, own_m, peer_m, pieces, extra):
    rows, width = own_x.shape
    block = (ROWS, width)
    own, peer = crossed(0), crossed(2)
    half = ((ROWS, width), LOW, None, None)
    return call(
        feed_kernel,
        "feed",
        place,
        4,
        [(own_x, block, own), (peer_x, block, peer), (own_g, block, own), (peer_g, block, peer)]
        + [(own_m, block, own), (peer_m, block, peer)]
        + [(array, None, None) for array in (*pieces, extra)],
        [half] * 4
        + [((rows, width), LOW, block, own), ((rows, width), LOW, block, peer)]
        + [((4, width // 8 + 16, width), LOW, None, None)] * 2
        + [((2, width // 8 + 32, width), LOW, None, None)] * 4,
        [
            pltpu.VMEM((2 * width, width), LOW),
            pltpu.VMEM((16, width), FLOAT),
            pltpu.VMEM((2 * width, width), FLOAT),
            pltpu.VMEM((16, width), FLOAT),
        ],
    )


def finish_kernel(
    place, own_x, peer_x, own_e, peer_e, slope_ref, lines, weight,
    peer_far, peer_near, own_far, own_near, kept, sent,
    total, sums_all,
):
    step = pl.program_id(0)
    half = pl.num_programs(0) // 2
    width, size = total.shape
    share = width // 8

    @pl.when(step == 0)
    def _():
        total[...] = jnp.zeros_like(total)
        sums_all[...] = jnp.zeros_like(sums_all)

    slope = jnp.concatenate([slope_ref[...], jnp.zeros((slope_ref.shape[0], 64), LOW)], axis=1)

    def work(x_ref, e_ref, targets):
        unit, _ = center(x_ref[...].astype(FLOAT))
        total[...] += tn(unit.astype(LOW), slope)
        sums_all[0:1, :] += jnp.sum(slope.astype(FLOAT), axis=0, keepdims=True)
        back = nt(slope, weight[:, :size])
        value = (back * lines[0:1, :] + e_ref[...].astype(FLOAT)).astype(LOW)
        for spot, target in enumerate(targets):

            @pl.when(step % half == spot)
            def _(target=target):
                target[...] = value

    @pl.when(step < half)
    def _():
        work(peer_x, peer_e, (peer_far, peer_near))

    @pl.when(step >= half)
    def _():
        work(own_x, own_e, (own_far, own_near))

    @pl.when(step == 2 * half - 1)
    def _():
        column = jnp.transpose(jnp.concatenate([lines[...], jnp.zeros((112, width), FLOAT)], axis=0))
        flat = sums_all[0:1, :]
        part = weight[:, :size].astype(FLOAT)
        lane = lax.broadcasted_iota(jnp.int32, (1, size), 1)
        part = jnp.where(lane < size - 64, part, 0.0)
        gain_part = jnp.sum(part * total[...], axis=1, keepdims=True)
        shift_part = jnp.sum(part * flat, axis=1, keepdims=True)
        both = jnp.concatenate([gain_part, shift_part, jnp.zeros((width, 126), FLOAT)], axis=1)
        both = jnp.transpose(both)
        middle = width // 2
        none = jnp.zeros((1, size - middle), FLOAT)
        vectors = [
            jnp.concatenate([both[line : line + 1, a : a + middle], none], axis=1)
            for line in range(2)
            for a in (0, middle)
        ]
        vectors = stacked(vectors + [flat], size)
        total[...] = total[...] * column[:, 0:1] + column[:, 1:2] * flat

        def parts(f):
            return [(0, total[f * share : (f + 1) * share, :].astype(LOW)), (share, vectors)]

        write_parts(place[10], parts, kept, sent)


def finish(place, own_x, peer_x, own_e, peer_e, slope, lines, weight):
    rows, width = own_x.shape
    size = slope.shape[1] + 64
    block = (ROWS, width)

    def peer(s, place):
        return (jnp.where(s == 0, 1 - place[1], place[1]), 0)

    def own(s, place):
        return (jnp.where(s < 3, 1 - place[1], place[1]), 0)

    def target(s, place):
        side = jnp.where(s < 2, 1 - place[0], place[0])
        return (2 * side + jnp.where(s % 2 == 0, 1 - place[1], place[1]), 0)

    return call(
        finish_kernel,
        "finish",
        place,
        4,
        [(own_x, block, own), (peer_x, block, peer), (own_e, block, own), (peer_e, block, peer)]
        + [(slope, (ROWS, slope.shape[1]), target), (lines, None, None), (weight, None, None)],
        [((ROWS, width), LOW, None, None)] * 4 + [((4, width // 8 + 16, size), LOW, None, None)] * 2,
        [pltpu.VMEM((width, size), FLOAT), pltpu.VMEM((8, size), FLOAT)],
    )


def cross_kernel(place, kept, got, own, *sent):
    for step, target in enumerate((own,) + sent):
        spot = lax.rem(place[11] + step, 4)
        target[...] = (kept[spot].astype(FLOAT) + got[spot].astype(FLOAT)).astype(LOW)


def cross(place, kept, got):
    return call(
        cross_kernel,
        "cross",
        place,
        1,
        [(kept, None, None), (got, None, None)],
        [(kept.shape[1:], LOW, None, None)] * 4,
    )


def cross_feed_kernel(place, kept, got, mine, *refs):
    later, (own, one, two, three, own_late, sent_late) = refs[:3], refs[3:]
    cross_kernel(place, kept, got, own, one, two, three)
    for target, side in ((own_late, place[10]), (sent_late, 1 - place[10])):
        total = mine[side].astype(FLOAT)
        for part in later:
            total = total + part[side].astype(FLOAT)
        target[...] = total.astype(LOW)


def cross_feed(place, kept, got, mine, later):
    return call(
        cross_feed_kernel,
        "cross_feed",
        place,
        1,
        [(array, None, None) for array in (kept, got, mine, *later)],
        [(kept.shape[1:], LOW, None, None)] * 4 + [(mine.shape[1:], LOW, None, None)] * 2,
    )


def join_kernel(place, own, one, two, three, own_late, got_late, out):
    first = own.shape[0]
    total = own[...].astype(FLOAT) + one[...].astype(FLOAT) + two[...].astype(FLOAT) + three[...].astype(FLOAT)
    out[:first, :] = total.astype(LOW)
    out[first:, :] = (own_late[...].astype(FLOAT) + got_late[...].astype(FLOAT)).astype(LOW)


def join(place, own, got, own_late, got_late):
    rows = own.shape[0] + own_late.shape[0]
    return call(
        join_kernel,
        "join",
        place,
        1,
        [(array, None, None) for array in (own, *got, own_late, got_late)],
        [((rows, own.shape[1]), LOW, None, None)],
    )[0]


def last_feed_kernel(place, own, far, wide, narrow, out, sums, units):
    y = place[0]
    width = own.shape[1]
    share = width // 8
    inner = out.shape[1] // 2

    def both(first, count):
        mine = own[first : first + count, :].astype(FLOAT)
        theirs = far[first : first + count, :].astype(FLOAT)
        return mine, theirs, pick(y, mine, theirs), pick(y, theirs, mine)

    _, _, low, high = both(0, share)
    wide[...] = jnp.concatenate([low, high], axis=1)
    _, _, low, high = both(share + 16, share)
    narrow[...] = jnp.concatenate([low, high], axis=1)
    mine, theirs, low, high = both(share, 16)
    sums[...] = mine + theirs
    units[...] = jnp.concatenate([low[2:3, :], high[2:3, :]], axis=1)
    _, _, low, high = both(2 * share + 16, 32)

    def column(value):
        return jnp.concatenate([value[:, c * inner : (c + 1) * inner] for c in range(3)], axis=0)

    out[...] = jnp.concatenate([column(low), column(high)], axis=1)


def last_feed(place, own, far, inner):
    width = own.shape[1]
    share = width // 8
    return call(
        last_feed_kernel,
        "last_feed",
        place,
        1,
        [(own, None, None), (far, None, None)],
        [
            ((share, 2 * width), FLOAT, None, None),
            ((share, 2 * width), FLOAT, None, None),
            ((share, 2 * inner), FLOAT, None, None),
            ((16, width), FLOAT, None, None),
            ((1, 2 * width), FLOAT, None, None),
        ],
    )


def last_attend_kernel(place, own, far, project, sums, bias):
    y = place[0]
    _, share, double = project.shape
    inner = double // 2
    mine = own[:share, :].astype(FLOAT)
    theirs = far[:share, :].astype(FLOAT)
    low, high = pick(y, mine, theirs), pick(y, theirs, mine)
    for c in range(3):
        lanes = slice(c * inner, (c + 1) * inner)
        project[c] = jnp.concatenate([low[:, lanes], high[:, lanes]], axis=1)
    mine = own[share:, :].astype(FLOAT)
    theirs = far[share:, :].astype(FLOAT)
    sums[...] = mine + theirs
    low, high = pick(y, mine, theirs), pick(y, theirs, mine)
    rows = []
    for c in range(3):
        lanes = slice(c * inner, (c + 1) * inner)
        rows.append(jnp.concatenate([low[4:5, lanes], high[4:5, lanes]], axis=1))
    bias[...] = jnp.concatenate(rows, axis=0)


def last_attend(place, own, far, inner):
    share = own.shape[0] - 16
    return call(
        last_attend_kernel,
        "last_attend",
        place,
        1,
        [(own, None, None), (far, None, None)],
        [
            ((3, share, 2 * inner), FLOAT, None, None),
            ((16, own.shape[1]), FLOAT, None, None),
            ((3, 2 * inner), FLOAT, None, None),
        ],
    )


def settle_kernel(slope, place, x_ref, other_ref, mine, theirs, out):
    step = pl.program_id(0)
    source = x_ref[...].astype(FLOAT)

    def work(total):
        if slope:
            unit, factor = center(source)
            change = (
                total
                - jnp.mean(total, axis=-1, keepdims=True)
                - unit * jnp.mean(total * unit, axis=-1, keepdims=True)
            )
            out[...] = other_ref[...].astype(FLOAT) + factor * change
        else:
            out[...] = (source + total + (other_ref[3:4, :] + other_ref[4:5, :])).astype(LOW)

    @pl.when(step == place[1])
    def _():
        work(mine[...].astype(FLOAT))

    @pl.when(step != place[1])
    def _():
        work(theirs[...].astype(FLOAT))


def settle(place, slope, x, other, mine, theirs):
    rows, width = x.shape
    block = (ROWS, width)

    def moving(s, place):
        return (s, 0)

    return call(
        functools.partial(settle_kernel, slope),
        "settle",
        place,
        2,
        [(x, block, moving), (other, block, moving) if slope else (other, None, None)]
        + [(mine, None, None), (theirs, None, None)],
        [((rows, width), FLOAT if slope else LOW, block, moving)],
    )[0]


PAIR = [(0, 1), (1, 0)]


def swap(value, axis):
    return lax.ppermute(value, axis, PAIR)


def ring_order():
    return list(range(0, 8, 2)) + list(range(7, 0, -2))


def ring_owners(me):
    spot = jnp.where(me % 2 == 0, me // 2, 7 - me // 2)
    offsets = [0, -1, 1, -2, 2, -3, 3, -4]
    positions = [(spot + offset + 8) % 8 for offset in offsets]
    return [jnp.where(p < 4, 2 * p, 15 - 2 * p) for p in positions]


class Ring:
    def __init__(self, piece):
        self.pieces = [piece]
        self.ends = [piece, piece]
        order = ring_order()
        forward = [(order[i], order[(i + 1) % 8]) for i in range(8)]
        self.ways = [forward, [(b, a) for a, b in forward]]

    def step(self):
        ways = self.ways[: 8 - len(self.pieces)]
        self.ends = [lax.ppermute(end, "fsdp", way) for end, way in zip(self.ends, ways)]
        self.pieces += self.ends

    def newest(self):
        return tuple(self.ends)


def send_along(pieces):
    got = []
    for step, piece in enumerate(pieces, 1):
        pairs = [(2 * a + b, 2 * ((a + step) % 4) + b) for a in range(4) for b in range(2)]
        got.append(lax.ppermute(piece, "fsdp", pairs))
    return got


def add_along(own, got):
    total = own.astype(FLOAT)
    for piece in got:
        total = total + piece.astype(FLOAT)
    return total.astype(LOW)


def swap_x(value):
    return lax.ppermute(value, "fsdp", [(i, i ^ 1) for i in range(8)])


def after(values, *earlier):
    return lax.optimization_barrier((values, earlier))[0]


def add(*values):
    total = values[0].astype(FLOAT)
    for value in values[1:]:
        total = total + value.astype(FLOAT)
    return total.astype(LOW)


def ordered(own, peer, index, axis=0):
    first = jnp.where(index == 0, own, peer)
    second = jnp.where(index == 0, peer, own)
    return jnp.concatenate([first, second], axis=axis)


def take_half(value, index, axis=0):
    size = value.shape[axis] // 2
    return lax.dynamic_slice_in_dim(value, index * size, size, axis)


def split_body(
    tokens,
    pack_lengths,
    cotangent,
    projection,
    projection_bias,
    outgoing,
    outgoing_bias,
    widening,
    widening_bias,
    narrowing,
    narrowing_bias,
    first_gain,
    first_shift,
    second_gain,
    second_shift,
):
    _, local, width = tokens.shape
    group = 2 * local
    share = width // 8
    y = lax.axis_index("context")
    core = lax.axis_index("tensor")
    me = lax.axis_index("fsdp")
    own_x = tokens.reshape(local, width)
    own_g = cotangent.reshape(local, width)
    inner = outgoing.shape[0] // 2
    third = projection_bias.shape[1]
    owners = ring_owners(me)
    place = jnp.stack([y, core] + owners + [me % 2, me // 2, me])
    other = jnp.stack([1 - y, core] + owners + [me % 2, me // 2, me])

    def whole(*arrays):
        return [(array if array.ndim > 1 else rank_two(array), None, None) for array in arrays]

    attend_piece = call(
        pack_attend_kernel,
        "pack_attend",
        place,
        1,
        whole(projection.transpose(1, 0, 2), outgoing.T, first_gain, first_shift, outgoing_bias, narrowing_bias)
        + whole(projection_bias),
        [((share + 16, width), LOW, None, None)],
    )[0]
    index = jnp.arange(group, dtype=jnp.int32)
    number, position, valid = layout(pack_lengths[0], index)
    begin = index - position
    labels = jnp.arange(SEQS, dtype=jnp.int32)
    length = jnp.sum(
        jnp.where(number[:, None] == labels[None, :], pack_lengths[0][None, :], 0), axis=1
    )
    stop = jnp.minimum(index + 1, begin + length).reshape(1, group)
    start = jnp.where(number == SEQS, index, begin)
    blocks = start.reshape(group // BLOCK, BLOCK)
    first = jnp.min(blocks, axis=1) // BLOCK
    clear = (jnp.max(blocks, axis=1) + BLOCK - 1) // BLOCK
    clear = jnp.minimum(jnp.maximum(clear, first), jnp.arange(group // BLOCK, dtype=jnp.int32))
    start = start.reshape(1, group)
    tiles = position.reshape(group // TILE, TILE)[:, 0] // TILE
    first = jnp.concatenate([first, tiles, clear])
    tables = turning()
    place = jnp.concatenate([place, tiles])

    far_x = swap(take_half(own_x, core), "context")
    attend_ring = Ring(attend_piece)
    attend_ring.step()
    attend_ring.step()
    feed_piece = call(
        pack_feed_kernel,
        "pack_feed",
        place,
        1,
        whole(widening, narrowing.T, second_gain, second_shift, widening_bias),
        [((2 * share + 16, width), LOW, None, None)],
    )[0]
    feed_ring = Ring(after(feed_piece, attend_ring.newest()))
    attend_ring.step()
    far_x = after(far_x, attend_ring.newest())
    far_g = swap(after(take_half(own_g, core), far_x), "context")
    peer_x = ordered(far_x, swap(far_x, "tensor"), core)
    feed_ring.step()
    attend_ring.step()
    peer_x, feed_ring.ends = after((peer_x, feed_ring.ends))
    feed_ring.step()
    q, k, v, attend_weight, attend_lines = prepare(place, own_x, peer_x, tables, attend_ring.pieces, inner)
    q, far_g = after((q, far_g), feed_ring.newest())
    feed_ring.step()
    near_g = swap(far_g, "tensor")
    heads, total, exact = forward(first, q, k, v, start, stop)
    heads, near_g, feed_ring.ends = after((heads, near_g, feed_ring.ends))
    feed_ring.step()
    peer_g = ordered(far_g, near_g, core)
    o, mixed_own, mixed_peer, extra = mix(place, own_g, peer_g, heads, attend_weight)

    own_far, own_near, peer_far, peer_near, e_own, e_peer, kept, sent, *late = feed(
        place, own_x, peer_x, own_g, peer_g, mixed_own, mixed_peer, feed_ring.pieces, extra
    )
    got = swap_x(sent)
    late_got = send_along(late[1:])
    gone = add(peer_near, swap(peer_far, "tensor"))
    mixed_far = swap(gone, "context")
    own_got = swap(own_far, "tensor")

    o = after(o, gone, own_got)
    slope = backward(first, q, k, v, o, start, stop, total, exact, tables)
    slope, got, late_got, mixed_far = after((slope, got, late_got, mixed_far))
    feed_cross = cross_feed(place, kept, got, late[0], late_got)
    slope = after(slope, feed_cross)
    feed_got = send_along(feed_cross[1:4])
    late_got = swap_x(feed_cross[5])
    peer_far, peer_near, far_own, near_own, kept, sent = finish(
        place, own_x, peer_x, own_e=e_own, peer_e=e_peer, slope=slope, lines=attend_lines, weight=attend_weight
    )
    sent, peer_far, far_own, feed_got, late_got = after((sent, peer_far, far_own, feed_got, late_got))
    attend_got = swap_x(sent)
    peer_got = swap(peer_far, "tensor")
    e_got_own = swap(far_own, "tensor")
    gone = add(peer_near, peer_got)
    e_far = swap(gone, "context")
    feed_got, own_near = after((feed_got, own_near), gone)
    feed_sum = join(place, feed_cross[0], feed_got, feed_cross[4], late_got)
    mine = add(own_near, own_got, mixed_far)
    theirs = swap(mine, "tensor")
    mixed = settle(place, False, own_x, attend_lines, mine, theirs)
    attend_got = after(attend_got, mixed)
    attend_cross = cross(place, kept, attend_got)
    attend_along = send_along(attend_cross[1:])
    e_far = after(e_far, attend_cross[0])
    mine = add(near_own, e_got_own, e_far)
    feed_far = swap(after(feed_sum, e_far), "context")
    tokens_gradient = settle(place, True, own_x, own_g, mine, swap(mine, "tensor"))
    attend_along = after(attend_along, tokens_gradient)
    attend_sum = add_along(attend_cross[0], attend_along)
    attend_far = swap(attend_sum, "context")

    wide_slope, narrow_slope, outgoing_slope, feed_sums, unit_slope = last_feed(place, feed_sum, feed_far, inner)
    projection_slope, attend_sums, bias_slope = last_attend(place, attend_sum, attend_far, inner)

    def across(rows):
        part = lax.dynamic_slice_in_dim(rows.astype(LOW), me * share, share, 1)
        return part.astype(FLOAT) + swap(part, "tensor").astype(FLOAT)

    feed_lines = across(feed_sums[:8])
    attend_slopes = across(attend_sums[:4, : width // 2].reshape(2, width))
    unit_slope = lax.dynamic_slice_in_dim(unit_slope[0], me * (width // 4), width // 4)
    bias_slope = lax.dynamic_slice_in_dim(bias_slope, me * third, third, 1)
    return (
        mixed.reshape(tokens.shape),
        tokens_gradient.reshape(tokens.shape),
        projection_slope.transpose(1, 0, 2),
        bias_slope,
        outgoing_slope.T,
        feed_lines[3],
        wide_slope,
        unit_slope,
        narrow_slope.T,
        feed_lines[3],
        attend_slopes[0],
        attend_slopes[1],
        feed_lines[0],
        feed_lines[1],
    )


def body(*arrays):
    tokens, outgoing, narrowing = arrays[0], arrays[5], arrays[9]
    fits = (
        lax.axis_size("fsdp") == 8
        and lax.axis_size("context") == 2
        and lax.axis_size("tensor") == 2
        and tokens.shape[0] == 1
        and tokens.shape[1] == 2 * ROWS
        and outgoing.shape[0] == 6 * HEAD_DIM
        and tokens.shape[2] * 2 == narrowing.shape[0]
    )
    return split_body(*arrays) if fits else general_body(*arrays)


def solution(mesh):
    return jax.shard_map(
        body,
        mesh=mesh,
        in_specs=(
            P("fsdp", "context", None),
            P("fsdp", None),
            P("fsdp", "context", None),
            P("fsdp", None, "tensor"),
            P(None, ("tensor", "fsdp")),
            P("tensor", "fsdp"),
            P("fsdp"),
            P("fsdp", "tensor"),
            P(("tensor", "fsdp")),
            P("tensor", "fsdp"),
            P("fsdp"),
            P("fsdp"),
            P("fsdp"),
            P("fsdp"),
            P("fsdp"),
        ),
        out_specs=(
            P("fsdp", "context", None),
            P("fsdp", "context", None),
            P("fsdp", None, "tensor"),
            P(None, ("tensor", "fsdp")),
            P("tensor", "fsdp"),
            P("fsdp"),
            P("fsdp", "tensor"),
            P(("tensor", "fsdp")),
            P("tensor", "fsdp"),
            P("fsdp"),
            P("fsdp"),
            P("fsdp"),
            P("fsdp"),
            P("fsdp"),
        ),
        check_vma=False,
    )
```

```python
import functools

import jax
import jax.numpy as jnp
import numpy as np
from jax import lax
from jax.experimental import pallas as pl
from jax.experimental.pallas import tpu as pltpu
from jax.sharding import PartitionSpec as P

HEAD_DIM = 64
ROTARY = 16
TILE = 128
SEQS = 3


epsilon = 1e-05


def layout(lengths, index):
    padded = (lengths + TILE - 1) // TILE * TILE
    labels = jnp.arange(SEQS, dtype=jnp.int32)
    finish = jnp.sum(jnp.where(labels[:, None] <= labels[None, :], padded[:, None], 0), axis=0)
    before = (index[:, None] >= finish[None, :]).astype(jnp.int32)
    number = jnp.sum(before, axis=1)
    start = jnp.sum(before * padded[None, :], axis=1)
    position = index - start
    length = jnp.sum(jnp.where(number[:, None] == labels[None, :], lengths[None, :], 0), axis=1)
    return (number, position, position < length)


def turn_tables(position):
    frequency = 10000.0 ** (-jnp.arange(0, ROTARY, 2, dtype=jnp.float32) / ROTARY)
    angles = position.astype(jnp.float32)[:, None] * frequency[None, :]
    angles = jnp.concatenate([angles, angles], axis=1)
    return (jnp.cos(angles)[:, None, :], jnp.sin(angles)[:, None, :])


def rotate(field, cosine, sine):
    half = ROTARY // 2
    front = field[..., :ROTARY]
    turned = jnp.concatenate([-front[..., half:], front[..., :half]], axis=-1)
    return jnp.concatenate([front * cosine + turned * sine, field[..., ROTARY:]], axis=-1)


def rotate_back(slope, cosine, sine):
    half = ROTARY // 2
    front = slope[..., :ROTARY]
    scaled = front * sine
    turned = jnp.concatenate([scaled[..., half:], -scaled[..., :half]], axis=-1)
    return jnp.concatenate([front * cosine + turned, slope[..., ROTARY:]], axis=-1)


def normalize(values, gain, shift):
    average = jnp.mean(values, axis=-1, keepdims=True)
    centered = values - average
    spread = jnp.mean(centered * centered, axis=-1, keepdims=True)
    factor = lax.rsqrt(spread + epsilon)
    unit = centered * factor
    return (unit, factor, unit * gain + shift)


def normalize_back(slope, unit, factor, gain):
    scaled = slope * gain
    return factor * (
        scaled
        - jnp.mean(scaled, axis=-1, keepdims=True)
        - unit * jnp.mean(scaled * unit, axis=-1, keepdims=True)
    )


def gelu_slope(values):
    return (
        0.5 * (1.0 + lax.erf(values * 0.7071067811865476))
        + values * jnp.exp(-0.5 * values * values) * 0.3989422804014327
    )


def allowed_mask(
    query_number, query_position, query_index, key_number, key_position, key_valid, key_index
):
    same = (
        (query_number[:, None] == key_number[None, :])
        & (key_position[None, :] <= query_position[:, None])
        & key_valid[None, :]
    )
    return same | (query_index[:, None] == key_index[None, :])


def general_body(
    tokens,
    pack_lengths,
    cotangent,
    projection,
    projection_bias,
    outgoing,
    outgoing_bias,
    widening,
    widening_bias,
    narrowing,
    narrowing_bias,
    first_gain,
    first_shift,
    second_gain,
    second_shift,
):
    packs, local, width = tokens.shape
    group = local * lax.axis_size("context")
    rows = packs * local
    (
        projection,
        projection_bias,
        outgoing,
        outgoing_bias,
        widening,
        widening_bias,
        narrowing,
        narrowing_bias,
        first_gain,
        first_shift,
        second_gain,
        second_shift,
    ) = (
        lax.all_gather(projection, "fsdp", axis=0, tiled=True),
        lax.all_gather(projection_bias, "fsdp", axis=1, tiled=True),
        lax.all_gather(outgoing, "fsdp", axis=1, tiled=True),
        lax.all_gather(outgoing_bias, "fsdp", axis=0, tiled=True),
        lax.all_gather(widening, "fsdp", axis=0, tiled=True),
        lax.all_gather(widening_bias, "fsdp", axis=0, tiled=True),
        lax.all_gather(narrowing, "fsdp", axis=1, tiled=True),
        lax.all_gather(narrowing_bias, "fsdp", axis=0, tiled=True),
        lax.all_gather(first_gain, "fsdp", axis=0, tiled=True),
        lax.all_gather(first_shift, "fsdp", axis=0, tiled=True),
        lax.all_gather(second_gain, "fsdp", axis=0, tiled=True),
        lax.all_gather(second_shift, "fsdp", axis=0, tiled=True),
    )
    inner = projection.shape[2]
    heads_here = inner // HEAD_DIM
    score_scale = HEAD_DIM ** (-0.5)
    gain_one = first_gain.astype(jnp.float32)
    gain_two = second_gain.astype(jnp.float32)
    source = tokens.reshape(rows, width).astype(jnp.float32)
    unit_one, factor_one, normed_one = normalize(source, gain_one, first_shift.astype(jnp.float32))
    unit_two, factor_two, normed_two = normalize(source, gain_two, second_shift.astype(jnp.float32))
    normed_one = normed_one.astype(jnp.bfloat16)
    normed_two = normed_two.astype(jnp.bfloat16)
    projected = jnp.dot(
        normed_one, projection.reshape(width, 3 * inner), preferred_element_type=jnp.float32
    ).reshape(rows, 3, inner)
    projected = projected + projection_bias.astype(jnp.float32)[None]
    query_index = lax.axis_index("context") * local + jnp.arange(local, dtype=jnp.int32)
    key_index = jnp.arange(group, dtype=jnp.int32)
    query_number, query_position, query_valid = jax.vmap(layout, in_axes=(0, None))(
        pack_lengths, query_index
    )
    key_number, key_position, key_valid = jax.vmap(layout, in_axes=(0, None))(
        pack_lengths, key_index
    )
    cosine, sine = turn_tables(query_position.reshape(rows))
    shaped = projected.reshape(rows, 3, heads_here, HEAD_DIM)
    queries = rotate(shaped[:, 0], cosine, sine).astype(jnp.bfloat16)
    keys = rotate(shaped[:, 1], cosine, sine).astype(jnp.bfloat16)
    values = shaped[:, 2].astype(jnp.bfloat16)
    all_keys, all_values = (
        lax.all_gather(keys.reshape(packs, local, inner), "context", axis=1, tiled=True),
        lax.all_gather(values.reshape(packs, local, inner), "context", axis=1, tiled=True),
    )
    query_packs = queries.reshape(packs, local, heads_here, HEAD_DIM)

    def scores_for(pack):
        key_block = all_keys[pack].reshape(group, heads_here, HEAD_DIM)
        raw = (
            jnp.einsum(
                "qhd,khd->hqk", query_packs[pack], key_block, preferred_element_type=jnp.float32
            )
            * score_scale
        )
        allowed = allowed_mask(
            query_number[pack],
            query_position[pack],
            query_index,
            key_number[pack],
            key_position[pack],
            key_valid[pack],
            key_index,
        )
        return jnp.where(allowed[None], raw, -1e30)

    pack = 0
    scores = scores_for(pack)
    top = jnp.max(scores, axis=-1, keepdims=True)
    total = jnp.log(jnp.sum(jnp.exp(scores - top), axis=-1, keepdims=True)) + top
    weights = jnp.exp(scores - total).astype(jnp.bfloat16)
    value_block = all_values[pack].reshape(group, heads_here, HEAD_DIM)
    head_blocks = [
        jnp.einsum("hqk,khd->qhd", weights, value_block, preferred_element_type=jnp.float32)
    ]
    totals = [total]
    mixed_heads = jnp.stack(head_blocks).reshape(rows, inner).astype(jnp.bfloat16)
    hidden = jnp.dot(
        normed_two, widening, preferred_element_type=jnp.float32
    ) + widening_bias.astype(jnp.float32)
    active = jax.nn.gelu(hidden, approximate=False).astype(jnp.bfloat16)
    attention_part = jnp.dot(mixed_heads, outgoing, preferred_element_type=jnp.float32)
    feed_part = jnp.dot(active, narrowing, preferred_element_type=jnp.float32)
    biases = outgoing_bias.astype(jnp.float32) + narrowing_bias.astype(jnp.float32)
    attention_sum, feed_sum = (
        lax.psum(attention_part.astype(jnp.bfloat16), "tensor").astype(jnp.float32),
        lax.psum(feed_part.astype(jnp.bfloat16), "tensor").astype(jnp.float32),
    )
    result = source + attention_sum + feed_sum + biases
    mixed = result.astype(jnp.bfloat16).reshape(packs, local, width)
    slope_out = cotangent.reshape(rows, width)
    slope_float = slope_out.astype(jnp.float32)
    outgoing_bias_slope = jnp.sum(slope_float, axis=0)
    outgoing_slope = jnp.einsum(
        "rf,rd->fd", mixed_heads, slope_out, preferred_element_type=jnp.float32
    )
    narrowing_slope = jnp.einsum("rf,rd->fd", active, slope_out, preferred_element_type=jnp.float32)
    heads_slope = jnp.einsum(
        "rd,fd->rf", slope_out, outgoing, preferred_element_type=jnp.float32
    ).astype(jnp.bfloat16)
    hidden_slope = (
        jnp.einsum("rd,fd->rf", slope_out, narrowing, preferred_element_type=jnp.float32)
        * gelu_slope(hidden)
    ).astype(jnp.bfloat16)
    widening_slope = jnp.einsum(
        "rd,rf->df", normed_two, hidden_slope, preferred_element_type=jnp.float32
    )
    widening_bias_slope = jnp.sum(hidden_slope.astype(jnp.float32), axis=0)
    second_back = jnp.einsum(
        "rf,df->rd", hidden_slope, widening, preferred_element_type=jnp.float32
    )
    heads_slope_packs = heads_slope.reshape(packs, local, heads_here, HEAD_DIM)
    balances = []
    pack = 0
    scores = scores_for(pack)
    probs = jnp.exp(scores - totals[pack])
    key_block = all_keys[pack].reshape(group, heads_here, HEAD_DIM)
    value_block = all_values[pack].reshape(group, heads_here, HEAD_DIM)
    outer = heads_slope_packs[pack]
    probs_slope = jnp.einsum("qhd,khd->hqk", outer, value_block, preferred_element_type=jnp.float32)
    balance = jnp.sum(probs * probs_slope, axis=-1, keepdims=True)
    balances.append(balance)
    score_slope = (probs * (probs_slope - balance)).astype(jnp.bfloat16)
    query_slopes = [
        jnp.einsum("hqk,khd->qhd", score_slope, key_block, preferred_element_type=jnp.float32)
        * score_scale
    ]
    weights = probs.astype(jnp.bfloat16)
    key_slopes = [
        jnp.einsum(
            "hqk,qhd->khd", score_slope, query_packs[pack], preferred_element_type=jnp.float32
        )
        * score_scale
    ]
    value_slopes = [jnp.einsum("hqk,qhd->khd", weights, outer, preferred_element_type=jnp.float32)]
    key_total, value_total = (
        lax.psum_scatter(
            jnp.stack(key_slopes).reshape(packs, group, inner).astype(jnp.bfloat16),
            "context",
            scatter_dimension=1,
            tiled=True,
        ).astype(jnp.float32),
        lax.psum_scatter(
            jnp.stack(value_slopes).reshape(packs, group, inner).astype(jnp.bfloat16),
            "context",
            scatter_dimension=1,
            tiled=True,
        ).astype(jnp.float32),
    )
    query_back = rotate_back(
        jnp.stack(query_slopes).reshape(rows, heads_here, HEAD_DIM), cosine, sine
    )
    key_back = rotate_back(key_total.reshape(rows, heads_here, HEAD_DIM), cosine, sine)
    projected_slope = jnp.stack(
        [
            query_back.reshape(rows, inner),
            key_back.reshape(rows, inner),
            value_total.reshape(rows, inner),
        ],
        axis=1,
    ).astype(jnp.bfloat16)
    projection_slope = jnp.einsum(
        "rd,rcf->dcf", normed_one, projected_slope, preferred_element_type=jnp.float32
    )
    projection_bias_slope = jnp.sum(projected_slope.astype(jnp.float32), axis=0)
    first_back = jnp.einsum(
        "rcf,dcf->rd", projected_slope, projection, preferred_element_type=jnp.float32
    )
    first_total, second_total = (
        lax.psum(first_back.astype(jnp.bfloat16), "tensor").astype(jnp.float32),
        lax.psum(second_back.astype(jnp.bfloat16), "tensor").astype(jnp.float32),
    )
    first_gain_slope = jnp.sum(first_total * unit_one, axis=0)
    first_shift_slope = jnp.sum(first_total, axis=0)
    second_gain_slope = jnp.sum(second_total * unit_two, axis=0)
    second_shift_slope = jnp.sum(second_total, axis=0)
    tokens_gradient = (
        slope_float
        + normalize_back(first_total, unit_one, factor_one, gain_one)
        + normalize_back(second_total, unit_two, factor_two, gain_two)
    )
    tokens_gradient = tokens_gradient.reshape(packs, local, width)
    owned = (
        lax.psum_scatter(
            projection_slope.astype(jnp.bfloat16), "fsdp", scatter_dimension=0, tiled=True
        ).astype(jnp.float32),
        lax.psum_scatter(
            projection_bias_slope.astype(jnp.bfloat16), "fsdp", scatter_dimension=1, tiled=True
        ).astype(jnp.float32),
        lax.psum_scatter(
            outgoing_slope.astype(jnp.bfloat16), "fsdp", scatter_dimension=1, tiled=True
        ).astype(jnp.float32),
        lax.psum_scatter(
            outgoing_bias_slope.astype(jnp.bfloat16), "fsdp", scatter_dimension=0, tiled=True
        ).astype(jnp.float32),
        lax.psum_scatter(
            widening_slope.astype(jnp.bfloat16), "fsdp", scatter_dimension=0, tiled=True
        ).astype(jnp.float32),
        lax.psum_scatter(
            widening_bias_slope.astype(jnp.bfloat16), "fsdp", scatter_dimension=0, tiled=True
        ).astype(jnp.float32),
        lax.psum_scatter(
            narrowing_slope.astype(jnp.bfloat16), "fsdp", scatter_dimension=1, tiled=True
        ).astype(jnp.float32),
        lax.psum_scatter(
            outgoing_bias_slope.astype(jnp.bfloat16), "fsdp", scatter_dimension=0, tiled=True
        ).astype(jnp.float32),
        lax.psum_scatter(
            first_gain_slope.astype(jnp.bfloat16), "fsdp", scatter_dimension=0, tiled=True
        ).astype(jnp.float32),
        lax.psum_scatter(
            first_shift_slope.astype(jnp.bfloat16), "fsdp", scatter_dimension=0, tiled=True
        ).astype(jnp.float32),
        lax.psum_scatter(
            second_gain_slope.astype(jnp.bfloat16), "fsdp", scatter_dimension=0, tiled=True
        ).astype(jnp.float32),
        lax.psum_scatter(
            second_shift_slope.astype(jnp.bfloat16), "fsdp", scatter_dimension=0, tiled=True
        ).astype(jnp.float32),
    )
    final = (
        lax.psum(owned[0].astype(jnp.bfloat16), "context").astype(jnp.float32),
        lax.psum(owned[1].astype(jnp.bfloat16), "context").astype(jnp.float32),
        lax.psum(owned[2].astype(jnp.bfloat16), "context").astype(jnp.float32),
        lax.psum(owned[3].astype(jnp.bfloat16), "context").astype(jnp.float32),
        lax.psum(owned[4].astype(jnp.bfloat16), "context").astype(jnp.float32),
        lax.psum(owned[5].astype(jnp.bfloat16), "context").astype(jnp.float32),
        lax.psum(owned[6].astype(jnp.bfloat16), "context").astype(jnp.float32),
        lax.psum(owned[7].astype(jnp.bfloat16), "context").astype(jnp.float32),
        lax.psum(owned[8].astype(jnp.bfloat16), "context").astype(jnp.float32),
        lax.psum(owned[9].astype(jnp.bfloat16), "context").astype(jnp.float32),
        lax.psum(owned[10].astype(jnp.bfloat16), "context").astype(jnp.float32),
        lax.psum(owned[11].astype(jnp.bfloat16), "context").astype(jnp.float32),
    )
    return (mixed, tokens_gradient) + tuple(final)


BLOCK = 256
FLOAT = jnp.float32
LOW = jnp.bfloat16


def nn(left, right):
    return lax.dot_general(left, right, (((1,), (0,)), ((), ())), preferred_element_type=FLOAT)


def nt(left, right):
    return lax.dot_general(left, right, (((1,), (1,)), ((), ())), preferred_element_type=FLOAT)


def tn(left, right):
    return lax.dot_general(left, right, (((0,), (0,)), ((), ())), preferred_element_type=FLOAT)


def center(values):
    average = jnp.mean(values, axis=-1, keepdims=True)
    centered = values - average
    spread = jnp.mean(centered * centered, axis=-1, keepdims=True)
    factor = lax.rsqrt(spread + epsilon)
    return centered * factor, factor


def widen_lanes(table, times):
    return jnp.concatenate([table] * times, axis=1)


def call(kernel, name, place, steps, inputs, outputs, scratch=(), flops=0):
    def fixed(rank):
        return lambda s, place: (0,) * rank

    def spec(shape, block, index):
        return pl.BlockSpec(shape if block is None else block, fixed(len(shape)) if block is None else index)

    return pl.pallas_call(
        kernel,
        grid_spec=pltpu.PrefetchScalarGridSpec(
            num_scalar_prefetch=1,
            grid=(steps,),
            in_specs=[spec(array.shape, block, index) for array, block, index in inputs],
            out_specs=[spec(shape, block, index) for shape, _, block, index in outputs],
            scratch_shapes=list(scratch),
        ),
        out_shape=[jax.ShapeDtypeStruct(shape, kind) for shape, kind, _, _ in outputs],
        compiler_params=pltpu.CompilerParams(vmem_limit_bytes=48 << 20),
        cost_estimate=pl.CostEstimate(flops=1, bytes_accessed=1, transcendentals=0),
        name=name,
    )(place, *[array for array, _, _ in inputs])


ROWS = 512


def rank_two(value):
    return value.reshape(1, -1)


def pick(index, left, right):
    return jnp.where(index == 0, left, right)


def rolled(rows, shift, width):
    return pltpu.roll(
        jnp.concatenate([rows, jnp.zeros((rows.shape[0], width - rows.shape[1]), FLOAT)], axis=1), shift, 1
    )


def stacked(rows, width):
    rows = list(rows) + [jnp.zeros((16 - len(rows), width), FLOAT)]
    return jnp.concatenate(rows, axis=0).astype(LOW)


def pack_attend_kernel(place, project, out, gain, shift, first_bias, second_bias, third, piece):
    y, me = place[0], place[12]
    share = project.shape[1]
    inner = out.shape[1] // 2
    width = piece.shape[1]
    parts = []
    for c in range(3):
        block = project[c].astype(FLOAT)
        parts.append(pick(y, block[:, :inner], block[:, inner:]))
    parts.append(pick(y, out[:, :inner].astype(FLOAT), out[:, inner:].astype(FLOAT)))
    piece[:share, :] = jnp.concatenate(parts, axis=1).astype(LOW)
    rows = [rolled(ref[...].astype(FLOAT), me * share, width) for ref in (gain, shift, first_bias, second_bias)]
    bias = rolled(third[...].astype(FLOAT), me * third.shape[1], 2 * inner)
    bias = pick(y, bias[:, :inner], bias[:, inner:])
    bias = jnp.concatenate([bias[c : c + 1] for c in range(3)] + [jnp.zeros((1, width - 3 * inner), FLOAT)], axis=1)
    piece[share:, :] = stacked([rows[0], rows[1], bias, rows[2], rows[3]], width)


def pack_feed_kernel(place, wide, narrow, gain, shift, bias, piece):
    y, me = place[0], place[12]
    share = wide.shape[0]
    units = narrow.shape[1] // 2
    width = piece.shape[1]
    piece[:share, :] = pick(y, wide[:, :units].astype(FLOAT), wide[:, units:].astype(FLOAT)).astype(LOW)
    piece[share : 2 * share, :] = pick(
        y, narrow[:, :units].astype(FLOAT), narrow[:, units:].astype(FLOAT)
    ).astype(LOW)
    rows = [rolled(ref[...].astype(FLOAT), me * share, width) for ref in (gain, shift)]
    full = rolled(bias[...].astype(FLOAT), me * bias.shape[1], 2 * units)
    rows.append(pick(y, full[:, :units], full[:, units:]))
    piece[2 * share :, :] = stacked(rows, width)


def place_pieces(place, pieces, first, target, at, share):
    for spot, piece in enumerate(pieces):
        rows = pl.ds(pl.multiple_of(at + place[spot + 2] * share, 32), share)
        target[rows, :] = piece[first : first + share, :]


def sum_rows(pieces, first):
    total = pieces[0][first:, :].astype(FLOAT)
    for piece in pieces[1:]:
        total = total + piece[first:, :].astype(FLOAT)
    return total


def prepare_kernel(place, own_x, peer_x, coarse, fine, *refs):
    pieces, (q_out, k_out, v_out, weight, lines) = refs[:-5], refs[-5:]
    inner = q_out.shape[1]
    step = pl.program_id(0)
    half = pl.num_programs(0) // 2
    share = weight.shape[0] // 8

    @pl.when(step == 0)
    def _():
        place_pieces(place, pieces, 0, weight, 0, share)
        lines[...] = sum_rows(pieces, share)

    def work(x_ref):
        unit, _ = center(x_ref[...].astype(FLOAT))
        normed = (unit * lines[0:1, :] + lines[1:2, :]).astype(LOW)
        raw = nn(normed, weight[:, : 3 * inner + 64]) + lines[2:3, : 3 * inner + 64]
        both = raw[:, : 2 * inner]
        times = 2 * inner // 128
        tiles = ROWS // TILE
        block = jnp.where(step < half, place[0] * half + step, (1 - place[0]) * half + step - half)
        cosine, left, right = turns(place, 13 + block * tiles, tiles, coarse, fine)
        turned = (
            both * widen_lanes(cosine, times)
            + pltpu.roll(both, 2 * inner - ROTARY // 2, 1) * widen_lanes(left, times)
            + pltpu.roll(both, ROTARY // 2, 1) * widen_lanes(right, times)
        )
        q_out[...] = (turned[:, :inner] * HEAD_DIM ** (-0.5)).astype(LOW)
        k_out[...] = turned[:, inner:].astype(LOW)
        v_out[...] = raw[:, 2 * inner : 3 * inner].astype(LOW)

    @pl.when(step < half)
    def _():
        work(own_x)

    @pl.when(step >= half)
    def _():
        work(peer_x)


def turning():
    lane = np.arange(128)
    rate = 10000.0 ** (-2.0 * (lane % (ROTARY // 2)) / ROTARY) * (lane % HEAD_DIM < ROTARY)
    coarse = TILE * np.arange(16)[:, None] * rate[None, :]
    fine = np.arange(TILE)[:, None] * rate[None, :]
    tables = [np.concatenate([np.cos(t), np.sin(t)], axis=1) for t in (coarse, fine)]
    return [jnp.asarray(t.astype(np.float32)) for t in tables]


def turns(scalars, at, count, coarse, fine):
    lane = lax.broadcasted_iota(jnp.int32, (1, 128), 1) % HEAD_DIM
    cosines, sines = [], []
    for tile in range(count):
        row = coarse[pl.ds(scalars[at + tile], 1), :]
        cosines.append(row[:, :128] * fine[:, :128] - row[:, 128:] * fine[:, 128:])
        sines.append(row[:, 128:] * fine[:, :128] + row[:, :128] * fine[:, 128:])
    cosine = jnp.concatenate(cosines, axis=0)
    sine = jnp.concatenate(sines, axis=0)
    left = jnp.where(lane < ROTARY // 2, -sine, 0.0)
    right = jnp.where((lane >= ROTARY // 2) & (lane < ROTARY), sine, 0.0)
    return cosine, left, right


def halves(half):
    def own(s, place):
        return (jnp.minimum(s, half - 1), 0)

    def peer(s, place):
        return (jnp.maximum(s - half, 0), 0)

    def target(s, place):
        return (jnp.where(s < half, place[0] * half + s, (1 - place[0]) * half + s - half), 0)

    return own, peer, target


def prepare(place, own_x, peer_x, tables, pieces, inner):
    rows, width = own_x.shape
    half = rows // ROWS
    own, peer, target = halves(half)
    block = (ROWS, width)
    thin = ((2 * rows, inner), LOW, (ROWS, inner), target)
    return call(
        prepare_kernel,
        "prepare",
        place,
        2 * half,
        [(own_x, block, own), (peer_x, block, peer)]
        + [(table, None, None) for table in tables]
        + [(piece, None, None) for piece in pieces],
        [thin, thin, thin, ((width, 4 * inner), LOW, None, None), ((16, width), FLOAT, None, None)],
        flops=4 * rows * width * 3 * inner,
    )


def spread(source, target, head, heads):
    rows = source.shape[0]
    for h in range(heads):
        target[h * rows : (h + 1) * rows, :] = jnp.where(head == h, source, 0.0).astype(LOW)


def span(j, size=1):
    return pl.ds(pl.multiple_of(j * BLOCK, BLOCK), size * BLOCK)


def sweep(first, last, work, carry):
    pairs = (last - first) // 2
    carry = lax.fori_loop(0, pairs, lambda i, kept: work(2, first + 2 * i, kept), carry)
    return lax.fori_loop(first + 2 * pairs, last, lambda j, kept: work(1, j, kept), carry)


def diagonal(raw, block, start, stop, heads):
    key = lax.broadcasted_iota(jnp.int32, raw.shape, 0) + block * BLOCK
    itself = widen_lanes(lax.broadcasted_iota(jnp.int32, (1, BLOCK), 1) + block * BLOCK, heads)
    return jnp.where(((key >= start) & (key < stop)) | (key == itself), raw, -1e30)


def forward_kernel(
    first, q_ref, k_ref, v_ref, start_ref, stop_ref,
    heads_out, total_out, exact_out,
    vt, qm, scores, ot,
):
    inner = q_ref.shape[1]
    heads = inner // HEAD_DIM
    wide = heads * BLOCK
    step = pl.program_id(0)
    count = pl.num_programs(0)
    block = count - 1 - step

    @pl.when(step == 0)
    def _():
        ot[...] = jnp.zeros_like(ot)

        @pl.loop(0, count)
        def _(j):
            vt[:, span(j)] = jnp.transpose(v_ref[span(j), :].astype(FLOAT)).astype(LOW)

    head = lax.broadcasted_iota(jnp.int32, (BLOCK, inner), 1) // HEAD_DIM
    spread(q_ref[...].astype(FLOAT), qm, head, heads)
    start = widen_lanes(start_ref[...], heads)
    stop = widen_lanes(stop_ref[...], heads)
    low = first[block]
    row = lax.broadcasted_iota(jnp.int32, (BLOCK, wide), 0)

    def score(masked, size, j, top):
        raw = nt(k_ref[span(j, size), :], qm[...])
        if masked:
            raw = jnp.where(row >= start - j * BLOCK, raw, -1e30)
        scores[span(j, size), :] = raw
        return jnp.maximum(top, jnp.max(raw, axis=0, keepdims=True))

    raw = diagonal(nt(k_ref[span(block), :], qm[...]), block, start, stop, heads)
    scores[span(block), :] = raw
    clear = first[count + count * (BLOCK // TILE) + block]
    top = jnp.max(raw, axis=0, keepdims=True)
    top = lax.fori_loop(low, clear, functools.partial(score, True, 1), top)
    top = sweep(clear, block, functools.partial(score, False), top)
    ot[:inner, :] = jnp.zeros((inner, BLOCK), FLOAT)

    def weigh(size, j, total):
        weight = jnp.exp(scores[span(j, size), :] - top)
        rounded = weight.astype(LOW)
        for h in range(heads):
            lines = slice(h * HEAD_DIM, (h + 1) * HEAD_DIM)
            ot[lines, :] += nn(vt[lines, span(j, size)], rounded[:, h * BLOCK : (h + 1) * BLOCK])
        return total + jnp.sum(weight, axis=0, keepdims=True)

    total = sweep(low, block + 1, weigh, jnp.zeros((1, wide), FLOAT))
    total_out[...] = (jnp.log(total) + top).reshape(1, 1, wide)
    scale = 1.0 / total
    for h in range(heads):
        lines = slice(h * HEAD_DIM, (h + 1) * HEAD_DIM)
        ot[lines, :] = ot[lines, :] * scale[:, h * BLOCK : (h + 1) * BLOCK]
    exact_out[...] = ot[:inner, :]
    heads_out[...] = jnp.transpose(ot[...])[:, :inner].astype(LOW)


def forward(first, q, k, v, start, stop):
    group, inner = q.shape
    count = group // BLOCK
    wide = inner // HEAD_DIM * BLOCK

    def rows(s, first):
        return (count - 1 - s, 0)

    def lanes(s, first):
        return (0, count - 1 - s)

    def deep(s, first):
        return (count - 1 - s, 0, 0)

    thin = (BLOCK, inner)
    stat = ((count, 1, wide), FLOAT, (1, 1, wide), deep)
    return call(
        forward_kernel,
        "forward",
        first,
        count,
        [(q, thin, rows), (k, None, None), (v, None, None)]
        + [(start, (1, BLOCK), lanes), (stop, (1, BLOCK), lanes)],
        [((group, inner), LOW, thin, rows), stat, ((inner, group), FLOAT, (inner, BLOCK), lanes)],
        [
            pltpu.VMEM((inner, group), LOW),
            pltpu.VMEM((wide, inner), LOW),
            pltpu.VMEM((group, wide), FLOAT),
            pltpu.VMEM((BLOCK, BLOCK), FLOAT),
        ],
        flops=8 * group * group * inner,
    )


def backward_kernel(
    first, q_ref, k_ref, v_ref, o_ref, start_ref, stop_ref, total_ref, exact_ref, coarse, fine,
    slope_out,
    kt, qm, om, dk, dv, dqt,
):
    inner = q_ref.shape[1]
    heads = inner // HEAD_DIM
    wide = heads * BLOCK
    step = pl.program_id(0)
    count = pl.num_programs(0)
    block = count - 1 - step

    @pl.when(step == 0)
    def _():
        dk[...] = jnp.zeros_like(dk)
        dv[...] = jnp.zeros_like(dv)
        dqt[...] = jnp.zeros_like(dqt)

        @pl.loop(0, count)
        def _(j):
            kt[:, span(j)] = jnp.transpose(k_ref[span(j), :].astype(FLOAT)).astype(LOW)

    head = lax.broadcasted_iota(jnp.int32, (BLOCK, inner), 1) // HEAD_DIM
    spread(q_ref[...].astype(FLOAT), qm, head, heads)
    outer = o_ref[...].astype(FLOAT)
    spread(outer, om, head, heads)
    product = exact_ref[...] * jnp.transpose(outer)
    start = widen_lanes(start_ref[...], heads)
    stop = widen_lanes(stop_ref[...], heads)
    total = total_ref[0]
    balance = jnp.concatenate(
        [
            jnp.sum(product[h * HEAD_DIM : (h + 1) * HEAD_DIM, :], axis=0, keepdims=True)
            for h in range(heads)
        ],
        axis=1,
    )
    row = lax.broadcasted_iota(jnp.int32, (BLOCK, wide), 0)
    dqt[:inner, :] = jnp.zeros((inner, BLOCK), FLOAT)

    def spend(j, raw, size=1):
        normal = jnp.exp(raw - total)
        weight = normal.astype(LOW)
        change = (normal * (nt(v_ref[span(j, size), :], om[...]) - balance)).astype(LOW)
        dv[span(j, size), :] += nn(weight, om[...])
        dk[span(j, size), :] += nn(change, qm[...])
        for h in range(heads):
            lines = slice(h * HEAD_DIM, (h + 1) * HEAD_DIM)
            dqt[lines, :] += nn(kt[lines, span(j, size)], change[:, h * BLOCK : (h + 1) * BLOCK])

    clear = first[count + count * (BLOCK // TILE) + block]

    @pl.loop(first[block], clear)
    def _(j):
        raw = nt(k_ref[span(j), :], qm[...])
        spend(j, jnp.where(row >= start - j * BLOCK, raw, -1e30))

    def plain(size, j, carry):
        spend(j, nt(k_ref[span(j, size), :], qm[...]), size)
        return carry

    sweep(clear, block, plain, 0)

    spend(block, diagonal(nt(k_ref[span(block), :], qm[...]), block, start, stop, heads))
    dq = jnp.transpose(dqt[...])[:, :inner] * HEAD_DIM ** (-0.5)
    both = jnp.concatenate([dq, dk[span(block), :]], axis=1)
    times = 2 * inner // 128
    tiles = BLOCK // TILE
    cosine, left, right = turns(first, count + block * tiles, tiles, coarse, fine)
    turned = (
        both * widen_lanes(cosine, times)
        - pltpu.roll(both, 2 * inner - ROTARY // 2, 1) * widen_lanes(left, times)
        - pltpu.roll(both, ROTARY // 2, 1) * widen_lanes(right, times)
    )
    slope_out[...] = jnp.concatenate([turned, dv[span(block), :]], axis=1).astype(LOW)


def backward(first, q, k, v, o, start, stop, total, exact, tables):
    group, inner = q.shape
    count = group // BLOCK
    wide = inner // HEAD_DIM * BLOCK

    def rows(s, first):
        return (count - 1 - s, 0)

    def lanes(s, first):
        return (0, count - 1 - s)

    def deep(s, first):
        return (count - 1 - s, 0, 0)

    thin = (BLOCK, inner)
    return call(
        backward_kernel,
        "backward",
        first,
        count,
        [(q, thin, rows), (k, None, None), (v, None, None), (o, thin, rows)]
        + [(start, (1, BLOCK), lanes), (stop, (1, BLOCK), lanes)]
        + [(total, (1, 1, wide), deep), (exact, (inner, BLOCK), lanes)]
        + [(table, None, None) for table in tables],
        [((group, 3 * inner), LOW, (BLOCK, 3 * inner), rows)],
        [
            pltpu.VMEM((inner, group), LOW),
            pltpu.VMEM((wide, inner), LOW),
            pltpu.VMEM((wide, inner), LOW),
            pltpu.VMEM((group, inner), FLOAT),
            pltpu.VMEM((group, inner), FLOAT),
            pltpu.VMEM((BLOCK, BLOCK), FLOAT),
        ],
        flops=16 * group * group * inner,
    )[0]


def mix_kernel(place, own_g, peer_g, heads_ref, weight, o_out, own_out, peer_out, extra, outer):
    inner = heads_ref.shape[1]
    step = pl.program_id(0)
    half = pl.num_programs(0) // 2
    share = weight.shape[0] // 8

    @pl.when(step == 0)
    def _():
        outer[...] = jnp.zeros_like(outer)

    def work(g_ref, target):
        heads = heads_ref[...]
        slope = g_ref[...]
        lower = jnp.concatenate([jnp.zeros((heads.shape[0], 64), LOW), heads], axis=1)
        o_out[...] = nn(slope, weight[:, 3 * inner - 64 :])[:, 64:].astype(LOW)
        target[...] = nt(lower, weight[:, 3 * inner - 64 :]).astype(LOW)
        outer[...] += tn(slope, heads)

    @pl.when(step < half)
    def _():
        work(own_g, own_out)

    @pl.when(step >= half)
    def _():
        work(peer_g, peer_out)

    @pl.when(step == 2 * half - 1)
    def _():
        for f in range(8):
            parts = [outer[f * share + 32 * c : f * share + 32 * (c + 1), :] for c in range(3)]
            parts.append(jnp.zeros((32, extra.shape[2] - 3 * inner), FLOAT))
            extra[f] = jnp.concatenate(parts, axis=1).astype(LOW)


def mix(place, own_g, peer_g, heads, weight):
    rows, width = own_g.shape
    inner = heads.shape[1]
    half = rows // ROWS
    own, peer, target = halves(half)
    block = (ROWS, width)
    thin = (ROWS, inner)
    return call(
        mix_kernel,
        "mix",
        place,
        2 * half,
        [(own_g, block, own), (peer_g, block, peer), (heads, thin, target), (weight, None, None)],
        [
            ((2 * rows, inner), LOW, thin, target),
            ((rows, width), LOW, block, own),
            ((rows, width), LOW, block, peer),
            ((8, 32, width), LOW, None, None),
        ],
        [pltpu.VMEM((width, inner), FLOAT)],
        12 * rows * width * inner,
    )


def write_parts(x, parts, kept, sent):
    for own in range(2):

        @pl.when(x == own)
        def _(own=own):
            for f in range(8):
                target = kept if f % 2 == own else sent
                for first, value in parts(f):
                    target[f // 2, first : first + value.shape[0], : value.shape[1]] = value


def feed_kernel(place, own_x, peer_x, own_g, peer_g, own_m, peer_m, *refs):
    pieces, extra, refs = refs[:8], refs[8], refs[9:]
    own_far, own_near, peer_far, peer_near, own_e, peer_e, kept, sent, *later, weight, lines, total, sums_all = refs
    step = pl.program_id(0)
    half = pl.num_programs(0) // 2
    width = own_x.shape[1]
    share = width // 8

    @pl.when(step == 0)
    def _():
        place_pieces(place, pieces, 0, weight, 0, share)
        place_pieces(place, pieces, share, weight, width, share)
        lines[...] = sum_rows(pieces, 2 * share)
        total[...] = jnp.zeros_like(total)
        sums_all[...] = jnp.zeros_like(sums_all)

    def work(x_ref, g_ref, m_ref, e_out, targets, once):
        gain = lines[0:1, :]
        unit, _ = center(x_ref[...].astype(FLOAT))
        normed = (unit * gain + lines[1:2, :]).astype(LOW)
        slope = g_ref[...]
        hidden = nn(normed, weight[:width, :]) + lines[2:3, :]
        phi = 0.5 * (1.0 + lax.erf(hidden * 0.7071067811865476))
        active = (hidden * phi).astype(LOW)
        fed = (nt(active, weight[width:, :]) + m_ref[...].astype(FLOAT)).astype(LOW)
        inside = phi + hidden * jnp.exp(-0.5 * hidden * hidden) * 0.3989422804014327
        change = (nn(slope, weight[width:, :]) * inside).astype(LOW)
        back = nt(change, weight[:width, :])
        e_out[...] = (back * gain).astype(LOW)
        total[:width, :] += tn(normed, change)
        total[width:, :] += tn(slope, active)
        rows = [
            jnp.sum(back * unit, axis=0, keepdims=True),
            jnp.sum(back, axis=0, keepdims=True),
            jnp.sum(change.astype(FLOAT), axis=0, keepdims=True),
            jnp.sum(slope.astype(FLOAT), axis=0, keepdims=True) * once,
            jnp.zeros((12, width), FLOAT),
        ]
        sums_all[...] += jnp.concatenate(rows, axis=0)
        for spot, target in enumerate(targets):

            @pl.when(step % half == spot)
            def _(target=target):
                target[...] = fed

    @pl.when(step < half)
    def _():
        work(own_x, own_g, own_m, own_e, (own_far, own_near), jnp.where(place[1] == 0, 1.0, 0.0))

    @pl.when(step >= half)
    def _():
        work(peer_x, peer_g, peer_m, peer_e, (peer_far, peer_near), 0.0)

    @pl.when(step == 2 * half - 1)
    def _():
        vectors = sums_all[...].astype(LOW)

        def parts(f):
            later_rows = slice(width + f * share, width + (f + 1) * share)
            return [(0, total[later_rows, :].astype(LOW)), (share, extra[f])]

        write_parts(place[10], parts, kept, sent)
        for ahead, target in enumerate(later):
            depth = lax.rem(place[11] + ahead, 4)
            for side in range(2):
                f = 2 * depth + side
                target[side, :share, :] = total[pl.ds(pl.multiple_of(f * share, 32), share), :].astype(LOW)
                target[side, share:, :] = vectors


def crossed(first):
    def index(s, place):
        return (jnp.where(s <= first, 1 - place[1], place[1]), 0)

    return index


def feed(place, own_x, peer_x, own_g, peer_g, own_m, peer_m, pieces, extra):
    rows, width = own_x.shape
    block = (ROWS, width)
    own, peer = crossed(0), crossed(2)
    half = ((ROWS, width), LOW, None, None)
    return call(
        feed_kernel,
        "feed",
        place,
        4,
        [(own_x, block, own), (peer_x, block, peer), (own_g, block, own), (peer_g, block, peer)]
        + [(own_m, block, own), (peer_m, block, peer)]
        + [(array, None, None) for array in (*pieces, extra)],
        [half] * 4
        + [((rows, width), LOW, block, own), ((rows, width), LOW, block, peer)]
        + [((4, width // 8 + 32, width), LOW, None, None)] * 2
        + [((2, width // 8 + 16, width), LOW, None, None)] * 4,
        [
            pltpu.VMEM((2 * width, width), LOW),
            pltpu.VMEM((16, width), FLOAT),
            pltpu.VMEM((2 * width, width), FLOAT),
            pltpu.VMEM((16, width), FLOAT),
        ],
    )


def finish_kernel(
    place, own_x, peer_x, own_e, peer_e, slope_ref, lines, weight,
    peer_far, peer_near, own_far, own_near, kept, sent,
    total, sums_all,
):
    step = pl.program_id(0)
    half = pl.num_programs(0) // 2
    width, size = total.shape
    share = width // 8

    @pl.when(step == 0)
    def _():
        total[...] = jnp.zeros_like(total)
        sums_all[...] = jnp.zeros_like(sums_all)

    slope = jnp.concatenate([slope_ref[...], jnp.zeros((slope_ref.shape[0], 64), LOW)], axis=1)

    def work(x_ref, e_ref, targets):
        unit, _ = center(x_ref[...].astype(FLOAT))
        total[...] += tn(unit.astype(LOW), slope)
        sums_all[0:1, :] += jnp.sum(slope.astype(FLOAT), axis=0, keepdims=True)
        back = nt(slope, weight[:, :size])
        value = (back * lines[0:1, :] + e_ref[...].astype(FLOAT)).astype(LOW)
        for spot, target in enumerate(targets):

            @pl.when(step % half == spot)
            def _(target=target):
                target[...] = value

    @pl.when(step < half)
    def _():
        work(peer_x, peer_e, (peer_far, peer_near))

    @pl.when(step >= half)
    def _():
        work(own_x, own_e, (own_far, own_near))

    @pl.when(step == 2 * half - 1)
    def _():
        column = jnp.transpose(jnp.concatenate([lines[...], jnp.zeros((112, width), FLOAT)], axis=0))
        flat = sums_all[0:1, :]
        part = weight[:, :size].astype(FLOAT)
        lane = lax.broadcasted_iota(jnp.int32, (1, size), 1)
        part = jnp.where(lane < size - 64, part, 0.0)
        gain_part = jnp.sum(part * total[...], axis=1, keepdims=True)
        shift_part = jnp.sum(part * flat, axis=1, keepdims=True)
        both = jnp.concatenate([gain_part, shift_part, jnp.zeros((width, 126), FLOAT)], axis=1)
        both = jnp.transpose(both)
        middle = width // 2
        none = jnp.zeros((1, size - middle), FLOAT)
        vectors = [
            jnp.concatenate([both[line : line + 1, a : a + middle], none], axis=1)
            for line in range(2)
            for a in (0, middle)
        ]
        vectors = stacked(vectors + [flat], size)
        total[...] = total[...] * column[:, 0:1] + column[:, 1:2] * flat

        def parts(f):
            return [(0, total[f * share : (f + 1) * share, :].astype(LOW)), (share, vectors)]

        write_parts(place[10], parts, kept, sent)


def finish(place, own_x, peer_x, own_e, peer_e, slope, lines, weight):
    rows, width = own_x.shape
    size = slope.shape[1] + 64
    block = (ROWS, width)

    def peer(s, place):
        return (jnp.where(s == 0, 1 - place[1], place[1]), 0)

    def own(s, place):
        return (jnp.where(s < 3, 1 - place[1], place[1]), 0)

    def target(s, place):
        side = jnp.where(s < 2, 1 - place[0], place[0])
        return (2 * side + jnp.where(s % 2 == 0, 1 - place[1], place[1]), 0)

    return call(
        finish_kernel,
        "finish",
        place,
        4,
        [(own_x, block, own), (peer_x, block, peer), (own_e, block, own), (peer_e, block, peer)]
        + [(slope, (ROWS, slope.shape[1]), target), (lines, None, None), (weight, None, None)],
        [((ROWS, width), LOW, None, None)] * 4 + [((4, width // 8 + 16, size), LOW, None, None)] * 2,
        [pltpu.VMEM((width, size), FLOAT), pltpu.VMEM((8, size), FLOAT)],
    )


def cross_kernel(place, kept, got, own, *sent):
    for step, target in enumerate((own,) + sent):
        spot = lax.rem(place[11] + step, 4)
        target[...] = (kept[spot].astype(FLOAT) + got[spot].astype(FLOAT)).astype(LOW)


def cross(place, kept, got):
    return call(
        cross_kernel,
        "cross",
        place,
        1,
        [(kept, None, None), (got, None, None)],
        [(kept.shape[1:], LOW, None, None)] * 4,
    )


def cross_feed_kernel(place, kept, got, mine, *refs):
    later, (own, one, two, three, own_late, sent_late) = refs[:3], refs[3:]
    cross_kernel(place, kept, got, own, one, two, three)
    for target, side in ((own_late, place[10]), (sent_late, 1 - place[10])):
        total = mine[side].astype(FLOAT)
        for part in later:
            total = total + part[side].astype(FLOAT)
        target[...] = total.astype(LOW)


def cross_feed(place, kept, got, mine, later):
    return call(
        cross_feed_kernel,
        "cross_feed",
        place,
        1,
        [(array, None, None) for array in (kept, got, mine, *later)],
        [(kept.shape[1:], LOW, None, None)] * 4 + [(mine.shape[1:], LOW, None, None)] * 2,
    )


def join_kernel(place, own, one, two, three, own_late, got_late, out):
    first = own.shape[0]
    total = own[...].astype(FLOAT) + one[...].astype(FLOAT) + two[...].astype(FLOAT) + three[...].astype(FLOAT)
    out[:first, :] = total.astype(LOW)
    out[first:, :] = (own_late[...].astype(FLOAT) + got_late[...].astype(FLOAT)).astype(LOW)


def join(place, own, got, own_late, got_late):
    rows = own.shape[0] + own_late.shape[0]
    return call(
        join_kernel,
        "join",
        place,
        1,
        [(array, None, None) for array in (own, *got, own_late, got_late)],
        [((rows, own.shape[1]), LOW, None, None)],
    )[0]


def last_feed_kernel(place, own, far, wide, narrow, out, sums, units):
    y = place[0]
    width = own.shape[1]
    share = width // 8
    inner = out.shape[1] // 2

    def both(first, count):
        mine = own[first : first + count, :].astype(FLOAT)
        theirs = far[first : first + count, :].astype(FLOAT)
        return mine, theirs, pick(y, mine, theirs), pick(y, theirs, mine)

    _, _, low, high = both(share + 32, share)
    wide[...] = jnp.concatenate([low, high], axis=1)
    _, _, low, high = both(0, share)
    narrow[...] = jnp.concatenate([low, high], axis=1)
    mine, theirs, low, high = both(2 * share + 32, 16)
    sums[...] = mine + theirs
    units[...] = jnp.concatenate([low[2:3, :], high[2:3, :]], axis=1)
    _, _, low, high = both(share, 32)

    def column(value):
        return jnp.concatenate([value[:, c * inner : (c + 1) * inner] for c in range(3)], axis=0)

    out[...] = jnp.concatenate([column(low), column(high)], axis=1)


def last_feed(place, own, far, inner):
    width = own.shape[1]
    share = width // 8
    return call(
        last_feed_kernel,
        "last_feed",
        place,
        1,
        [(own, None, None), (far, None, None)],
        [
            ((share, 2 * width), FLOAT, None, None),
            ((share, 2 * width), FLOAT, None, None),
            ((share, 2 * inner), FLOAT, None, None),
            ((16, width), FLOAT, None, None),
            ((1, 2 * width), FLOAT, None, None),
        ],
    )


def last_attend_kernel(place, own, far, project, sums, bias):
    y = place[0]
    _, share, double = project.shape
    inner = double // 2
    mine = own[:share, :].astype(FLOAT)
    theirs = far[:share, :].astype(FLOAT)
    low, high = pick(y, mine, theirs), pick(y, theirs, mine)
    for c in range(3):
        lanes = slice(c * inner, (c + 1) * inner)
        project[c] = jnp.concatenate([low[:, lanes], high[:, lanes]], axis=1)
    mine = own[share:, :].astype(FLOAT)
    theirs = far[share:, :].astype(FLOAT)
    sums[...] = mine + theirs
    low, high = pick(y, mine, theirs), pick(y, theirs, mine)
    rows = []
    for c in range(3):
        lanes = slice(c * inner, (c + 1) * inner)
        rows.append(jnp.concatenate([low[4:5, lanes], high[4:5, lanes]], axis=1))
    bias[...] = jnp.concatenate(rows, axis=0)


def last_attend(place, own, far, inner):
    share = own.shape[0] - 16
    return call(
        last_attend_kernel,
        "last_attend",
        place,
        1,
        [(own, None, None), (far, None, None)],
        [
            ((3, share, 2 * inner), FLOAT, None, None),
            ((16, own.shape[1]), FLOAT, None, None),
            ((3, 2 * inner), FLOAT, None, None),
        ],
    )


def settle_kernel(slope, place, x_ref, other_ref, mine, theirs, out):
    step = pl.program_id(0)
    source = x_ref[...].astype(FLOAT)

    def work(total):
        if slope:
            unit, factor = center(source)
            change = (
                total
                - jnp.mean(total, axis=-1, keepdims=True)
                - unit * jnp.mean(total * unit, axis=-1, keepdims=True)
            )
            out[...] = other_ref[...].astype(FLOAT) + factor * change
        else:
            out[...] = (source + total + (other_ref[3:4, :] + other_ref[4:5, :])).astype(LOW)

    @pl.when(step == place[1])
    def _():
        work(mine[...].astype(FLOAT))

    @pl.when(step != place[1])
    def _():
        work(theirs[...].astype(FLOAT))


def settle(place, slope, x, other, mine, theirs):
    rows, width = x.shape
    block = (ROWS, width)

    def moving(s, place):
        return (s, 0)

    return call(
        functools.partial(settle_kernel, slope),
        "settle",
        place,
        2,
        [(x, block, moving), (other, block, moving) if slope else (other, None, None)]
        + [(mine, None, None), (theirs, None, None)],
        [((rows, width), FLOAT if slope else LOW, block, moving)],
    )[0]


PAIR = [(0, 1), (1, 0)]


def swap(value, axis):
    return lax.ppermute(value, axis, PAIR)


def ring_order():
    return list(range(0, 8, 2)) + list(range(7, 0, -2))


def ring_owners(me):
    spot = jnp.where(me % 2 == 0, me // 2, 7 - me // 2)
    offsets = [0, -1, 1, -2, 2, -3, 3, -4]
    positions = [(spot + offset + 8) % 8 for offset in offsets]
    return [jnp.where(p < 4, 2 * p, 15 - 2 * p) for p in positions]


class Ring:
    def __init__(self, piece):
        self.pieces = [piece]
        self.ends = [piece, piece]
        order = ring_order()
        forward = [(order[i], order[(i + 1) % 8]) for i in range(8)]
        self.ways = [forward, [(b, a) for a, b in forward]]

    def step(self):
        ways = self.ways[: 8 - len(self.pieces)]
        self.ends = [lax.ppermute(end, "fsdp", way) for end, way in zip(self.ends, ways)]
        self.pieces += self.ends

    def newest(self):
        return tuple(self.ends)


def send_along(pieces):
    got = []
    for step, piece in enumerate(pieces, 1):
        pairs = [(2 * a + b, 2 * ((a + step) % 4) + b) for a in range(4) for b in range(2)]
        got.append(lax.ppermute(piece, "fsdp", pairs))
    return got


def add_along(own, got):
    total = own.astype(FLOAT)
    for piece in got:
        total = total + piece.astype(FLOAT)
    return total.astype(LOW)


def swap_x(value):
    return lax.ppermute(value, "fsdp", [(i, i ^ 1) for i in range(8)])


def after(values, *earlier):
    return lax.optimization_barrier((values, earlier))[0]


def add(*values):
    total = values[0].astype(FLOAT)
    for value in values[1:]:
        total = total + value.astype(FLOAT)
    return total.astype(LOW)


def ordered(own, peer, index, axis=0):
    first = jnp.where(index == 0, own, peer)
    second = jnp.where(index == 0, peer, own)
    return jnp.concatenate([first, second], axis=axis)


def take_half(value, index, axis=0):
    size = value.shape[axis] // 2
    return lax.dynamic_slice_in_dim(value, index * size, size, axis)


def split_body(
    tokens,
    pack_lengths,
    cotangent,
    projection,
    projection_bias,
    outgoing,
    outgoing_bias,
    widening,
    widening_bias,
    narrowing,
    narrowing_bias,
    first_gain,
    first_shift,
    second_gain,
    second_shift,
):
    _, local, width = tokens.shape
    group = 2 * local
    share = width // 8
    y = lax.axis_index("context")
    core = lax.axis_index("tensor")
    me = lax.axis_index("fsdp")
    own_x = tokens.reshape(local, width)
    own_g = cotangent.reshape(local, width)
    inner = outgoing.shape[0] // 2
    third = projection_bias.shape[1]
    owners = ring_owners(me)
    place = jnp.stack([y, core] + owners + [me % 2, me // 2, me])
    other = jnp.stack([1 - y, core] + owners + [me % 2, me // 2, me])

    def whole(*arrays):
        return [(array if array.ndim > 1 else rank_two(array), None, None) for array in arrays]

    attend_piece = call(
        pack_attend_kernel,
        "pack_attend",
        place,
        1,
        whole(projection.transpose(1, 0, 2), outgoing.T, first_gain, first_shift, outgoing_bias, narrowing_bias)
        + whole(projection_bias),
        [((share + 16, width), LOW, None, None)],
    )[0]
    index = jnp.arange(group, dtype=jnp.int32)
    number, position, valid = layout(pack_lengths[0], index)
    begin = index - position
    labels = jnp.arange(SEQS, dtype=jnp.int32)
    length = jnp.sum(
        jnp.where(number[:, None] == labels[None, :], pack_lengths[0][None, :], 0), axis=1
    )
    stop = jnp.minimum(index + 1, begin + length).reshape(1, group)
    start = jnp.where(number == SEQS, index, begin)
    blocks = start.reshape(group // BLOCK, BLOCK)
    first = jnp.min(blocks, axis=1) // BLOCK
    clear = (jnp.max(blocks, axis=1) + BLOCK - 1) // BLOCK
    clear = jnp.minimum(jnp.maximum(clear, first), jnp.arange(group // BLOCK, dtype=jnp.int32))
    start = start.reshape(1, group)
    tiles = position.reshape(group // TILE, TILE)[:, 0] // TILE
    first = jnp.concatenate([first, tiles, clear])
    tables = turning()
    place = jnp.concatenate([place, tiles])

    far_x = swap(take_half(own_x, core), "context")
    attend_ring = Ring(attend_piece)
    attend_ring.step()
    attend_ring.step()
    feed_piece = call(
        pack_feed_kernel,
        "pack_feed",
        place,
        1,
        whole(widening, narrowing.T, second_gain, second_shift, widening_bias),
        [((2 * share + 16, width), LOW, None, None)],
    )[0]
    feed_ring = Ring(after(feed_piece, attend_ring.newest()))
    attend_ring.step()
    far_x = after(far_x, attend_ring.newest())
    far_g = swap(after(take_half(own_g, core), far_x), "context")
    peer_x = ordered(far_x, swap(far_x, "tensor"), core)
    feed_ring.step()
    attend_ring.step()
    peer_x, feed_ring.ends = after((peer_x, feed_ring.ends))
    feed_ring.step()
    q, k, v, attend_weight, attend_lines = prepare(place, own_x, peer_x, tables, attend_ring.pieces, inner)
    q, far_g = after((q, far_g), feed_ring.newest())
    feed_ring.step()
    near_g = swap(far_g, "tensor")
    heads, total, exact = forward(first, q, k, v, start, stop)
    heads, near_g, feed_ring.ends = after((heads, near_g, feed_ring.ends))
    feed_ring.step()
    peer_g = ordered(far_g, near_g, core)
    o, mixed_own, mixed_peer, extra = mix(place, own_g, peer_g, heads, attend_weight)

    own_far, own_near, peer_far, peer_near, e_own, e_peer, kept, sent, *late = feed(
        place, own_x, peer_x, own_g, peer_g, mixed_own, mixed_peer, feed_ring.pieces, extra
    )
    got = swap_x(sent)
    late_got = send_along(late[1:])
    gone = add(peer_near, swap(peer_far, "tensor"))
    mixed_far = swap(gone, "context")
    own_got = swap(own_far, "tensor")

    o = after(o, gone, own_got)
    slope = backward(first, q, k, v, o, start, stop, total, exact, tables)
    slope, got, late_got, mixed_far = after((slope, got, late_got, mixed_far))
    feed_cross = cross_feed(place, kept, got, late[0], late_got)
    slope = after(slope, feed_cross)
    feed_got = send_along(feed_cross[1:4])
    late_got = swap_x(feed_cross[5])
    peer_far, peer_near, far_own, near_own, kept, sent = finish(
        place, own_x, peer_x, own_e=e_own, peer_e=e_peer, slope=slope, lines=attend_lines, weight=attend_weight
    )
    sent, peer_far, far_own, feed_got, late_got = after((sent, peer_far, far_own, feed_got, late_got))
    attend_got = swap_x(sent)
    peer_got = swap(peer_far, "tensor")
    e_got_own = swap(far_own, "tensor")
    gone = add(peer_near, peer_got)
    e_far = swap(gone, "context")
    feed_got, own_near = after((feed_got, own_near), gone)
    feed_sum = join(place, feed_cross[0], feed_got, feed_cross[4], late_got)
    mine = add(own_near, own_got, mixed_far)
    theirs = swap(mine, "tensor")
    mixed = settle(place, False, own_x, attend_lines, mine, theirs)
    attend_got = after(attend_got, mixed)
    attend_cross = cross(place, kept, attend_got)
    attend_along = send_along(attend_cross[1:])
    e_far = after(e_far, attend_cross[0])
    mine = add(near_own, e_got_own, e_far)
    feed_far = swap(after(feed_sum, e_far), "context")
    tokens_gradient = settle(place, True, own_x, own_g, mine, swap(mine, "tensor"))
    attend_along = after(attend_along, tokens_gradient)
    attend_sum = add_along(attend_cross[0], attend_along)
    attend_far = swap(attend_sum, "context")

    wide_slope, narrow_slope, outgoing_slope, feed_sums, unit_slope = last_feed(place, feed_sum, feed_far, inner)
    projection_slope, attend_sums, bias_slope = last_attend(place, attend_sum, attend_far, inner)

    def across(rows):
        part = lax.dynamic_slice_in_dim(rows.astype(LOW), me * share, share, 1)
        return part.astype(FLOAT) + swap(part, "tensor").astype(FLOAT)

    feed_lines = across(feed_sums[:8])
    attend_slopes = across(attend_sums[:4, : width // 2].reshape(2, width))
    unit_slope = lax.dynamic_slice_in_dim(unit_slope[0], me * (width // 4), width // 4)
    bias_slope = lax.dynamic_slice_in_dim(bias_slope, me * third, third, 1)
    return (
        mixed.reshape(tokens.shape),
        tokens_gradient.reshape(tokens.shape),
        projection_slope.transpose(1, 0, 2),
        bias_slope,
        outgoing_slope.T,
        feed_lines[3],
        wide_slope,
        unit_slope,
        narrow_slope.T,
        feed_lines[3],
        attend_slopes[0],
        attend_slopes[1],
        feed_lines[0],
        feed_lines[1],
    )


def body(*arrays):
    tokens, outgoing, narrowing = arrays[0], arrays[5], arrays[9]
    fits = (
        lax.axis_size("fsdp") == 8
        and lax.axis_size("context") == 2
        and lax.axis_size("tensor") == 2
        and tokens.shape[0] == 1
        and tokens.shape[1] == 2 * ROWS
        and outgoing.shape[0] == 6 * HEAD_DIM
        and tokens.shape[2] * 2 == narrowing.shape[0]
    )
    return split_body(*arrays) if fits else general_body(*arrays)


def solution(mesh):
    return jax.shard_map(
        body,
        mesh=mesh,
        in_specs=(
            P("fsdp", "context", None),
            P("fsdp", None),
            P("fsdp", "context", None),
            P("fsdp", None, "tensor"),
            P(None, ("tensor", "fsdp")),
            P("tensor", "fsdp"),
            P("fsdp"),
            P("fsdp", "tensor"),
            P(("tensor", "fsdp")),
            P("tensor", "fsdp"),
            P("fsdp"),
            P("fsdp"),
            P("fsdp"),
            P("fsdp"),
            P("fsdp"),
        ),
        out_specs=(
            P("fsdp", "context", None),
            P("fsdp", "context", None),
            P("fsdp", None, "tensor"),
            P(None, ("tensor", "fsdp")),
            P("tensor", "fsdp"),
            P("fsdp"),
            P("fsdp", "tensor"),
            P(("tensor", "fsdp")),
            P("tensor", "fsdp"),
            P("fsdp"),
            P("fsdp"),
            P("fsdp"),
            P("fsdp"),
            P("fsdp"),
        ),
        check_vma=False,
    )
```

```python
import functools

import jax
import jax.numpy as jnp
import numpy as np
from jax import lax
from jax.experimental import pallas as pl
from jax.experimental.pallas import tpu as pltpu
from jax.sharding import PartitionSpec as P

HEAD_DIM = 64
ROTARY = 16
TILE = 128
SEQS = 3


epsilon = 1e-05


def layout(lengths, index):
    padded = (lengths + TILE - 1) // TILE * TILE
    labels = jnp.arange(SEQS, dtype=jnp.int32)
    finish = jnp.sum(jnp.where(labels[:, None] <= labels[None, :], padded[:, None], 0), axis=0)
    before = (index[:, None] >= finish[None, :]).astype(jnp.int32)
    number = jnp.sum(before, axis=1)
    start = jnp.sum(before * padded[None, :], axis=1)
    position = index - start
    length = jnp.sum(jnp.where(number[:, None] == labels[None, :], lengths[None, :], 0), axis=1)
    return (number, position, position < length)


def turn_tables(position):
    frequency = 10000.0 ** (-jnp.arange(0, ROTARY, 2, dtype=jnp.float32) / ROTARY)
    angles = position.astype(jnp.float32)[:, None] * frequency[None, :]
    angles = jnp.concatenate([angles, angles], axis=1)
    return (jnp.cos(angles)[:, None, :], jnp.sin(angles)[:, None, :])


def rotate(field, cosine, sine):
    half = ROTARY // 2
    front = field[..., :ROTARY]
    turned = jnp.concatenate([-front[..., half:], front[..., :half]], axis=-1)
    return jnp.concatenate([front * cosine + turned * sine, field[..., ROTARY:]], axis=-1)


def rotate_back(slope, cosine, sine):
    half = ROTARY // 2
    front = slope[..., :ROTARY]
    scaled = front * sine
    turned = jnp.concatenate([scaled[..., half:], -scaled[..., :half]], axis=-1)
    return jnp.concatenate([front * cosine + turned, slope[..., ROTARY:]], axis=-1)


def normalize(values, gain, shift):
    average = jnp.mean(values, axis=-1, keepdims=True)
    centered = values - average
    spread = jnp.mean(centered * centered, axis=-1, keepdims=True)
    factor = lax.rsqrt(spread + epsilon)
    unit = centered * factor
    return (unit, factor, unit * gain + shift)


def normalize_back(slope, unit, factor, gain):
    scaled = slope * gain
    return factor * (
        scaled
        - jnp.mean(scaled, axis=-1, keepdims=True)
        - unit * jnp.mean(scaled * unit, axis=-1, keepdims=True)
    )


def gelu_slope(values):
    return (
        0.5 * (1.0 + lax.erf(values * 0.7071067811865476))
        + values * jnp.exp(-0.5 * values * values) * 0.3989422804014327
    )


def allowed_mask(
    query_number, query_position, query_index, key_number, key_position, key_valid, key_index
):
    same = (
        (query_number[:, None] == key_number[None, :])
        & (key_position[None, :] <= query_position[:, None])
        & key_valid[None, :]
    )
    return same | (query_index[:, None] == key_index[None, :])


def general_body(
    tokens,
    pack_lengths,
    cotangent,
    projection,
    projection_bias,
    outgoing,
    outgoing_bias,
    widening,
    widening_bias,
    narrowing,
    narrowing_bias,
    first_gain,
    first_shift,
    second_gain,
    second_shift,
):
    packs, local, width = tokens.shape
    group = local * lax.axis_size("context")
    rows = packs * local
    (
        projection,
        projection_bias,
        outgoing,
        outgoing_bias,
        widening,
        widening_bias,
        narrowing,
        narrowing_bias,
        first_gain,
        first_shift,
        second_gain,
        second_shift,
    ) = (
        lax.all_gather(projection, "fsdp", axis=0, tiled=True),
        lax.all_gather(projection_bias, "fsdp", axis=1, tiled=True),
        lax.all_gather(outgoing, "fsdp", axis=1, tiled=True),
        lax.all_gather(outgoing_bias, "fsdp", axis=0, tiled=True),
        lax.all_gather(widening, "fsdp", axis=0, tiled=True),
        lax.all_gather(widening_bias, "fsdp", axis=0, tiled=True),
        lax.all_gather(narrowing, "fsdp", axis=1, tiled=True),
        lax.all_gather(narrowing_bias, "fsdp", axis=0, tiled=True),
        lax.all_gather(first_gain, "fsdp", axis=0, tiled=True),
        lax.all_gather(first_shift, "fsdp", axis=0, tiled=True),
        lax.all_gather(second_gain, "fsdp", axis=0, tiled=True),
        lax.all_gather(second_shift, "fsdp", axis=0, tiled=True),
    )
    inner = projection.shape[2]
    heads_here = inner // HEAD_DIM
    score_scale = HEAD_DIM ** (-0.5)
    gain_one = first_gain.astype(jnp.float32)
    gain_two = second_gain.astype(jnp.float32)
    source = tokens.reshape(rows, width).astype(jnp.float32)
    unit_one, factor_one, normed_one = normalize(source, gain_one, first_shift.astype(jnp.float32))
    unit_two, factor_two, normed_two = normalize(source, gain_two, second_shift.astype(jnp.float32))
    normed_one = normed_one.astype(jnp.bfloat16)
    normed_two = normed_two.astype(jnp.bfloat16)
    projected = jnp.dot(
        normed_one, projection.reshape(width, 3 * inner), preferred_element_type=jnp.float32
    ).reshape(rows, 3, inner)
    projected = projected + projection_bias.astype(jnp.float32)[None]
    query_index = lax.axis_index("context") * local + jnp.arange(local, dtype=jnp.int32)
    key_index = jnp.arange(group, dtype=jnp.int32)
    query_number, query_position, query_valid = jax.vmap(layout, in_axes=(0, None))(
        pack_lengths, query_index
    )
    key_number, key_position, key_valid = jax.vmap(layout, in_axes=(0, None))(
        pack_lengths, key_index
    )
    cosine, sine = turn_tables(query_position.reshape(rows))
    shaped = projected.reshape(rows, 3, heads_here, HEAD_DIM)
    queries = rotate(shaped[:, 0], cosine, sine).astype(jnp.bfloat16)
    keys = rotate(shaped[:, 1], cosine, sine).astype(jnp.bfloat16)
    values = shaped[:, 2].astype(jnp.bfloat16)
    all_keys, all_values = (
        lax.all_gather(keys.reshape(packs, local, inner), "context", axis=1, tiled=True),
        lax.all_gather(values.reshape(packs, local, inner), "context", axis=1, tiled=True),
    )
    query_packs = queries.reshape(packs, local, heads_here, HEAD_DIM)

    def scores_for(pack):
        key_block = all_keys[pack].reshape(group, heads_here, HEAD_DIM)
        raw = (
            jnp.einsum(
                "qhd,khd->hqk", query_packs[pack], key_block, preferred_element_type=jnp.float32
            )
            * score_scale
        )
        allowed = allowed_mask(
            query_number[pack],
            query_position[pack],
            query_index,
            key_number[pack],
            key_position[pack],
            key_valid[pack],
            key_index,
        )
        return jnp.where(allowed[None], raw, -1e30)

    pack = 0
    scores = scores_for(pack)
    top = jnp.max(scores, axis=-1, keepdims=True)
    total = jnp.log(jnp.sum(jnp.exp(scores - top), axis=-1, keepdims=True)) + top
    weights = jnp.exp(scores - total).astype(jnp.bfloat16)
    value_block = all_values[pack].reshape(group, heads_here, HEAD_DIM)
    head_blocks = [
        jnp.einsum("hqk,khd->qhd", weights, value_block, preferred_element_type=jnp.float32)
    ]
    totals = [total]
    mixed_heads = jnp.stack(head_blocks).reshape(rows, inner).astype(jnp.bfloat16)
    hidden = jnp.dot(
        normed_two, widening, preferred_element_type=jnp.float32
    ) + widening_bias.astype(jnp.float32)
    active = jax.nn.gelu(hidden, approximate=False).astype(jnp.bfloat16)
    attention_part = jnp.dot(mixed_heads, outgoing, preferred_element_type=jnp.float32)
    feed_part = jnp.dot(active, narrowing, preferred_element_type=jnp.float32)
    biases = outgoing_bias.astype(jnp.float32) + narrowing_bias.astype(jnp.float32)
    attention_sum, feed_sum = (
        lax.psum(attention_part.astype(jnp.bfloat16), "tensor").astype(jnp.float32),
        lax.psum(feed_part.astype(jnp.bfloat16), "tensor").astype(jnp.float32),
    )
    result = source + attention_sum + feed_sum + biases
    mixed = result.astype(jnp.bfloat16).reshape(packs, local, width)
    slope_out = cotangent.reshape(rows, width)
    slope_float = slope_out.astype(jnp.float32)
    outgoing_bias_slope = jnp.sum(slope_float, axis=0)
    outgoing_slope = jnp.einsum(
        "rf,rd->fd", mixed_heads, slope_out, preferred_element_type=jnp.float32
    )
    narrowing_slope = jnp.einsum("rf,rd->fd", active, slope_out, preferred_element_type=jnp.float32)
    heads_slope = jnp.einsum(
        "rd,fd->rf", slope_out, outgoing, preferred_element_type=jnp.float32
    ).astype(jnp.bfloat16)
    hidden_slope = (
        jnp.einsum("rd,fd->rf", slope_out, narrowing, preferred_element_type=jnp.float32)
        * gelu_slope(hidden)
    ).astype(jnp.bfloat16)
    widening_slope = jnp.einsum(
        "rd,rf->df", normed_two, hidden_slope, preferred_element_type=jnp.float32
    )
    widening_bias_slope = jnp.sum(hidden_slope.astype(jnp.float32), axis=0)
    second_back = jnp.einsum(
        "rf,df->rd", hidden_slope, widening, preferred_element_type=jnp.float32
    )
    heads_slope_packs = heads_slope.reshape(packs, local, heads_here, HEAD_DIM)
    balances = []
    pack = 0
    scores = scores_for(pack)
    probs = jnp.exp(scores - totals[pack])
    key_block = all_keys[pack].reshape(group, heads_here, HEAD_DIM)
    value_block = all_values[pack].reshape(group, heads_here, HEAD_DIM)
    outer = heads_slope_packs[pack]
    probs_slope = jnp.einsum("qhd,khd->hqk", outer, value_block, preferred_element_type=jnp.float32)
    balance = jnp.sum(probs * probs_slope, axis=-1, keepdims=True)
    balances.append(balance)
    score_slope = (probs * (probs_slope - balance)).astype(jnp.bfloat16)
    query_slopes = [
        jnp.einsum("hqk,khd->qhd", score_slope, key_block, preferred_element_type=jnp.float32)
        * score_scale
    ]
    weights = probs.astype(jnp.bfloat16)
    key_slopes = [
        jnp.einsum(
            "hqk,qhd->khd", score_slope, query_packs[pack], preferred_element_type=jnp.float32
        )
        * score_scale
    ]
    value_slopes = [jnp.einsum("hqk,qhd->khd", weights, outer, preferred_element_type=jnp.float32)]
    key_total, value_total = (
        lax.psum_scatter(
            jnp.stack(key_slopes).reshape(packs, group, inner).astype(jnp.bfloat16),
            "context",
            scatter_dimension=1,
            tiled=True,
        ).astype(jnp.float32),
        lax.psum_scatter(
            jnp.stack(value_slopes).reshape(packs, group, inner).astype(jnp.bfloat16),
            "context",
            scatter_dimension=1,
            tiled=True,
        ).astype(jnp.float32),
    )
    query_back = rotate_back(
        jnp.stack(query_slopes).reshape(rows, heads_here, HEAD_DIM), cosine, sine
    )
    key_back = rotate_back(key_total.reshape(rows, heads_here, HEAD_DIM), cosine, sine)
    projected_slope = jnp.stack(
        [
            query_back.reshape(rows, inner),
            key_back.reshape(rows, inner),
            value_total.reshape(rows, inner),
        ],
        axis=1,
    ).astype(jnp.bfloat16)
    projection_slope = jnp.einsum(
        "rd,rcf->dcf", normed_one, projected_slope, preferred_element_type=jnp.float32
    )
    projection_bias_slope = jnp.sum(projected_slope.astype(jnp.float32), axis=0)
    first_back = jnp.einsum(
        "rcf,dcf->rd", projected_slope, projection, preferred_element_type=jnp.float32
    )
    first_total, second_total = (
        lax.psum(first_back.astype(jnp.bfloat16), "tensor").astype(jnp.float32),
        lax.psum(second_back.astype(jnp.bfloat16), "tensor").astype(jnp.float32),
    )
    first_gain_slope = jnp.sum(first_total * unit_one, axis=0)
    first_shift_slope = jnp.sum(first_total, axis=0)
    second_gain_slope = jnp.sum(second_total * unit_two, axis=0)
    second_shift_slope = jnp.sum(second_total, axis=0)
    tokens_gradient = (
        slope_float
        + normalize_back(first_total, unit_one, factor_one, gain_one)
        + normalize_back(second_total, unit_two, factor_two, gain_two)
    )
    tokens_gradient = tokens_gradient.reshape(packs, local, width)
    owned = (
        lax.psum_scatter(
            projection_slope.astype(jnp.bfloat16), "fsdp", scatter_dimension=0, tiled=True
        ).astype(jnp.float32),
        lax.psum_scatter(
            projection_bias_slope.astype(jnp.bfloat16), "fsdp", scatter_dimension=1, tiled=True
        ).astype(jnp.float32),
        lax.psum_scatter(
            outgoing_slope.astype(jnp.bfloat16), "fsdp", scatter_dimension=1, tiled=True
        ).astype(jnp.float32),
        lax.psum_scatter(
            outgoing_bias_slope.astype(jnp.bfloat16), "fsdp", scatter_dimension=0, tiled=True
        ).astype(jnp.float32),
        lax.psum_scatter(
            widening_slope.astype(jnp.bfloat16), "fsdp", scatter_dimension=0, tiled=True
        ).astype(jnp.float32),
        lax.psum_scatter(
            widening_bias_slope.astype(jnp.bfloat16), "fsdp", scatter_dimension=0, tiled=True
        ).astype(jnp.float32),
        lax.psum_scatter(
            narrowing_slope.astype(jnp.bfloat16), "fsdp", scatter_dimension=1, tiled=True
        ).astype(jnp.float32),
        lax.psum_scatter(
            outgoing_bias_slope.astype(jnp.bfloat16), "fsdp", scatter_dimension=0, tiled=True
        ).astype(jnp.float32),
        lax.psum_scatter(
            first_gain_slope.astype(jnp.bfloat16), "fsdp", scatter_dimension=0, tiled=True
        ).astype(jnp.float32),
        lax.psum_scatter(
            first_shift_slope.astype(jnp.bfloat16), "fsdp", scatter_dimension=0, tiled=True
        ).astype(jnp.float32),
        lax.psum_scatter(
            second_gain_slope.astype(jnp.bfloat16), "fsdp", scatter_dimension=0, tiled=True
        ).astype(jnp.float32),
        lax.psum_scatter(
            second_shift_slope.astype(jnp.bfloat16), "fsdp", scatter_dimension=0, tiled=True
        ).astype(jnp.float32),
    )
    final = (
        lax.psum(owned[0].astype(jnp.bfloat16), "context").astype(jnp.float32),
        lax.psum(owned[1].astype(jnp.bfloat16), "context").astype(jnp.float32),
        lax.psum(owned[2].astype(jnp.bfloat16), "context").astype(jnp.float32),
        lax.psum(owned[3].astype(jnp.bfloat16), "context").astype(jnp.float32),
        lax.psum(owned[4].astype(jnp.bfloat16), "context").astype(jnp.float32),
        lax.psum(owned[5].astype(jnp.bfloat16), "context").astype(jnp.float32),
        lax.psum(owned[6].astype(jnp.bfloat16), "context").astype(jnp.float32),
        lax.psum(owned[7].astype(jnp.bfloat16), "context").astype(jnp.float32),
        lax.psum(owned[8].astype(jnp.bfloat16), "context").astype(jnp.float32),
        lax.psum(owned[9].astype(jnp.bfloat16), "context").astype(jnp.float32),
        lax.psum(owned[10].astype(jnp.bfloat16), "context").astype(jnp.float32),
        lax.psum(owned[11].astype(jnp.bfloat16), "context").astype(jnp.float32),
    )
    return (mixed, tokens_gradient) + tuple(final)


BLOCK = 256
FLOAT = jnp.float32
LOW = jnp.bfloat16


def nn(left, right):
    return lax.dot_general(left, right, (((1,), (0,)), ((), ())), preferred_element_type=FLOAT)


def nt(left, right):
    return lax.dot_general(left, right, (((1,), (1,)), ((), ())), preferred_element_type=FLOAT)


def tn(left, right):
    return lax.dot_general(left, right, (((0,), (0,)), ((), ())), preferred_element_type=FLOAT)


def center(values):
    average = jnp.mean(values, axis=-1, keepdims=True)
    centered = values - average
    spread = jnp.mean(centered * centered, axis=-1, keepdims=True)
    factor = lax.rsqrt(spread + epsilon)
    return centered * factor, factor


def widen_lanes(table, times):
    return jnp.concatenate([table] * times, axis=1)


def call(kernel, name, place, steps, inputs, outputs, scratch=(), flops=0):
    def fixed(rank):
        return lambda s, place: (0,) * rank

    def spec(shape, block, index):
        return pl.BlockSpec(shape if block is None else block, fixed(len(shape)) if block is None else index)

    return pl.pallas_call(
        kernel,
        grid_spec=pltpu.PrefetchScalarGridSpec(
            num_scalar_prefetch=1,
            grid=(steps,),
            in_specs=[spec(array.shape, block, index) for array, block, index in inputs],
            out_specs=[spec(shape, block, index) for shape, _, block, index in outputs],
            scratch_shapes=list(scratch),
        ),
        out_shape=[jax.ShapeDtypeStruct(shape, kind) for shape, kind, _, _ in outputs],
        compiler_params=pltpu.CompilerParams(vmem_limit_bytes=48 << 20),
        cost_estimate=pl.CostEstimate(flops=1, bytes_accessed=1, transcendentals=0),
        name=name,
    )(place, *[array for array, _, _ in inputs])


ROWS = 512


def rank_two(value):
    return value.reshape(1, -1)


def pick(index, left, right):
    return jnp.where(index == 0, left, right)


def rolled(rows, shift, width):
    return pltpu.roll(
        jnp.concatenate([rows, jnp.zeros((rows.shape[0], width - rows.shape[1]), FLOAT)], axis=1), shift, 1
    )


def stacked(rows, width):
    rows = list(rows) + [jnp.zeros((16 - len(rows), width), FLOAT)]
    return jnp.concatenate(rows, axis=0).astype(LOW)


def pack_attend_kernel(place, project, out, gain, shift, first_bias, second_bias, third, piece):
    y, me = place[0], place[12]
    share = project.shape[1]
    inner = out.shape[1] // 2
    width = piece.shape[1]
    parts = []
    for c in range(3):
        block = project[c].astype(FLOAT)
        parts.append(pick(y, block[:, :inner], block[:, inner:]))
    parts.append(pick(y, out[:, :inner].astype(FLOAT), out[:, inner:].astype(FLOAT)))
    piece[:share, :] = jnp.concatenate(parts, axis=1).astype(LOW)
    rows = [rolled(ref[...].astype(FLOAT), me * share, width) for ref in (gain, shift, first_bias, second_bias)]
    bias = rolled(third[...].astype(FLOAT), me * third.shape[1], 2 * inner)
    bias = pick(y, bias[:, :inner], bias[:, inner:])
    bias = jnp.concatenate([bias[c : c + 1] for c in range(3)] + [jnp.zeros((1, width - 3 * inner), FLOAT)], axis=1)
    piece[share:, :] = stacked([rows[0], rows[1], bias, rows[2], rows[3]], width)


def pack_feed_kernel(place, wide, narrow, gain, shift, bias, piece):
    y, me = place[0], place[12]
    share = wide.shape[0]
    units = narrow.shape[1] // 2
    width = piece.shape[1]
    piece[:share, :] = pick(y, wide[:, :units].astype(FLOAT), wide[:, units:].astype(FLOAT)).astype(LOW)
    piece[share : 2 * share, :] = pick(
        y, narrow[:, :units].astype(FLOAT), narrow[:, units:].astype(FLOAT)
    ).astype(LOW)
    rows = [rolled(ref[...].astype(FLOAT), me * share, width) for ref in (gain, shift)]
    full = rolled(bias[...].astype(FLOAT), me * bias.shape[1], 2 * units)
    rows.append(pick(y, full[:, :units], full[:, units:]))
    piece[2 * share :, :] = stacked(rows, width)


def place_pieces(place, pieces, first, target, at, share):
    for spot, piece in enumerate(pieces):
        rows = pl.ds(pl.multiple_of(at + place[spot + 2] * share, 32), share)
        target[rows, :] = piece[first : first + share, :]


def sum_rows(pieces, first):
    total = pieces[0][first:, :].astype(FLOAT)
    for piece in pieces[1:]:
        total = total + piece[first:, :].astype(FLOAT)
    return total


def prepare_kernel(place, own_x, peer_x, coarse, fine, *refs):
    pieces, (q_out, k_out, v_out, weight, lines) = refs[:-5], refs[-5:]
    inner = q_out.shape[1]
    step = pl.program_id(0)
    half = pl.num_programs(0) // 2
    share = weight.shape[0] // 8

    @pl.when(step == 0)
    def _():
        place_pieces(place, pieces, 0, weight, 0, share)
        lines[...] = sum_rows(pieces, share)

    def work(x_ref):
        unit, _ = center(x_ref[...].astype(FLOAT))
        normed = (unit * lines[0:1, :] + lines[1:2, :]).astype(LOW)
        raw = nn(normed, weight[:, : 3 * inner + 64]) + lines[2:3, : 3 * inner + 64]
        both = raw[:, : 2 * inner]
        times = 2 * inner // 128
        tiles = ROWS // TILE
        block = jnp.where(step < half, place[0] * half + step, (1 - place[0]) * half + step - half)
        cosine, left, right = turns(place, 13 + block * tiles, tiles, coarse, fine)
        turned = (
            both * widen_lanes(cosine, times)
            + pltpu.roll(both, 2 * inner - ROTARY // 2, 1) * widen_lanes(left, times)
            + pltpu.roll(both, ROTARY // 2, 1) * widen_lanes(right, times)
        )
        q_out[...] = (turned[:, :inner] * HEAD_DIM ** (-0.5)).astype(LOW)
        k_out[...] = turned[:, inner:].astype(LOW)
        v_out[...] = raw[:, 2 * inner : 3 * inner].astype(LOW)

    @pl.when(step < half)
    def _():
        work(own_x)

    @pl.when(step >= half)
    def _():
        work(peer_x)


def turning():
    lane = np.arange(128)
    rate = 10000.0 ** (-2.0 * (lane % (ROTARY // 2)) / ROTARY) * (lane % HEAD_DIM < ROTARY)
    coarse = TILE * np.arange(16)[:, None] * rate[None, :]
    fine = np.arange(TILE)[:, None] * rate[None, :]
    tables = [np.concatenate([np.cos(t), np.sin(t)], axis=1) for t in (coarse, fine)]
    return [jnp.asarray(t.astype(np.float32)) for t in tables]


def turns(scalars, at, count, coarse, fine):
    lane = lax.broadcasted_iota(jnp.int32, (1, 128), 1) % HEAD_DIM
    cosines, sines = [], []
    for tile in range(count):
        row = coarse[pl.ds(scalars[at + tile], 1), :]
        cosines.append(row[:, :128] * fine[:, :128] - row[:, 128:] * fine[:, 128:])
        sines.append(row[:, 128:] * fine[:, :128] + row[:, :128] * fine[:, 128:])
    cosine = jnp.concatenate(cosines, axis=0)
    sine = jnp.concatenate(sines, axis=0)
    left = jnp.where(lane < ROTARY // 2, -sine, 0.0)
    right = jnp.where((lane >= ROTARY // 2) & (lane < ROTARY), sine, 0.0)
    return cosine, left, right


def halves(half):
    def own(s, place):
        return (jnp.minimum(s, half - 1), 0)

    def peer(s, place):
        return (jnp.maximum(s - half, 0), 0)

    def target(s, place):
        return (jnp.where(s < half, place[0] * half + s, (1 - place[0]) * half + s - half), 0)

    return own, peer, target


def prepare(place, own_x, peer_x, tables, pieces, inner):
    rows, width = own_x.shape
    half = rows // ROWS
    own, peer, target = halves(half)
    block = (ROWS, width)
    thin = ((2 * rows, inner), LOW, (ROWS, inner), target)
    return call(
        prepare_kernel,
        "prepare",
        place,
        2 * half,
        [(own_x, block, own), (peer_x, block, peer)]
        + [(table, None, None) for table in tables]
        + [(piece, None, None) for piece in pieces],
        [thin, thin, thin, ((width, 4 * inner), LOW, None, None), ((16, width), FLOAT, None, None)],
        flops=4 * rows * width * 3 * inner,
    )


def spread(source, target, head, heads):
    rows = source.shape[0]
    for h in range(heads):
        target[h * rows : (h + 1) * rows, :] = jnp.where(head == h, source, 0.0).astype(LOW)


def span(j, size=1):
    return pl.ds(pl.multiple_of(j * BLOCK, BLOCK), size * BLOCK)


def sweep(first, last, work, carry):
    pairs = (last - first) // 2
    carry = lax.fori_loop(0, pairs, lambda i, kept: work(2, first + 2 * i, kept), carry)
    return lax.fori_loop(first + 2 * pairs, last, lambda j, kept: work(1, j, kept), carry)


def diagonal(raw, block, start, stop, heads):
    key = lax.broadcasted_iota(jnp.int32, raw.shape, 0) + block * BLOCK
    itself = widen_lanes(lax.broadcasted_iota(jnp.int32, (1, BLOCK), 1) + block * BLOCK, heads)
    return jnp.where(((key >= start) & (key < stop)) | (key == itself), raw, -1e30)


def forward_kernel(
    first, q_ref, k_ref, v_ref, start_ref, stop_ref,
    heads_out, total_out, exact_out,
    vt, qm, scores, ot,
):
    inner = q_ref.shape[1]
    heads = inner // HEAD_DIM
    wide = heads * BLOCK
    step = pl.program_id(0)
    count = pl.num_programs(0)
    block = count - 1 - step

    @pl.when(step == 0)
    def _():
        ot[...] = jnp.zeros_like(ot)

        @pl.loop(0, count)
        def _(j):
            vt[:, span(j)] = jnp.transpose(v_ref[span(j), :].astype(FLOAT)).astype(LOW)

    head = lax.broadcasted_iota(jnp.int32, (BLOCK, inner), 1) // HEAD_DIM
    spread(q_ref[...].astype(FLOAT), qm, head, heads)
    start = widen_lanes(start_ref[...], heads)
    stop = widen_lanes(stop_ref[...], heads)
    low = first[block]
    row = lax.broadcasted_iota(jnp.int32, (BLOCK, wide), 0)

    def score(masked, size, j, top):
        raw = nt(k_ref[span(j, size), :], qm[...])
        if masked:
            raw = jnp.where(row >= start - j * BLOCK, raw, -1e30)
        scores[span(j, size), :] = raw
        return jnp.maximum(top, jnp.max(raw, axis=0, keepdims=True))

    raw = diagonal(nt(k_ref[span(block), :], qm[...]), block, start, stop, heads)
    scores[span(block), :] = raw
    clear = first[count + count * (BLOCK // TILE) + block]
    top = jnp.max(raw, axis=0, keepdims=True)
    top = lax.fori_loop(low, clear, functools.partial(score, True, 1), top)
    top = sweep(clear, block, functools.partial(score, False), top)
    ot[:inner, :] = jnp.zeros((inner, BLOCK), FLOAT)

    def weigh(size, j, total):
        weight = jnp.exp(scores[span(j, size), :] - top)
        rounded = weight.astype(LOW)
        for h in range(heads):
            lines = slice(h * HEAD_DIM, (h + 1) * HEAD_DIM)
            ot[lines, :] += nn(vt[lines, span(j, size)], rounded[:, h * BLOCK : (h + 1) * BLOCK])
        return total + jnp.sum(weight, axis=0, keepdims=True)

    total = sweep(low, block + 1, weigh, jnp.zeros((1, wide), FLOAT))
    total_out[...] = (jnp.log(total) + top).reshape(1, 1, wide)
    scale = 1.0 / total
    for h in range(heads):
        lines = slice(h * HEAD_DIM, (h + 1) * HEAD_DIM)
        ot[lines, :] = ot[lines, :] * scale[:, h * BLOCK : (h + 1) * BLOCK]
    exact_out[...] = ot[:inner, :]
    heads_out[...] = jnp.transpose(ot[...])[:, :inner].astype(LOW)


def forward(first, q, k, v, start, stop):
    group, inner = q.shape
    count = group // BLOCK
    wide = inner // HEAD_DIM * BLOCK

    def rows(s, first):
        return (count - 1 - s, 0)

    def lanes(s, first):
        return (0, count - 1 - s)

    def deep(s, first):
        return (count - 1 - s, 0, 0)

    thin = (BLOCK, inner)
    stat = ((count, 1, wide), FLOAT, (1, 1, wide), deep)
    return call(
        forward_kernel,
        "forward",
        first,
        count,
        [(q, thin, rows), (k, None, None), (v, None, None)]
        + [(start, (1, BLOCK), lanes), (stop, (1, BLOCK), lanes)],
        [((group, inner), LOW, thin, rows), stat, ((inner, group), FLOAT, (inner, BLOCK), lanes)],
        [
            pltpu.VMEM((inner, group), LOW),
            pltpu.VMEM((wide, inner), LOW),
            pltpu.VMEM((group, wide), FLOAT),
            pltpu.VMEM((BLOCK, BLOCK), FLOAT),
        ],
        flops=8 * group * group * inner,
    )


def backward_kernel(
    first, q_ref, k_ref, v_ref, o_ref, start_ref, stop_ref, total_ref, exact_ref, coarse, fine,
    slope_out,
    kt, qm, om, dk, dv, dqt,
):
    inner = q_ref.shape[1]
    heads = inner // HEAD_DIM
    wide = heads * BLOCK
    step = pl.program_id(0)
    count = pl.num_programs(0)
    block = count - 1 - step

    @pl.when(step == 0)
    def _():
        dk[...] = jnp.zeros_like(dk)
        dv[...] = jnp.zeros_like(dv)
        dqt[...] = jnp.zeros_like(dqt)

        @pl.loop(0, count)
        def _(j):
            kt[:, span(j)] = jnp.transpose(k_ref[span(j), :].astype(FLOAT)).astype(LOW)

    head = lax.broadcasted_iota(jnp.int32, (BLOCK, inner), 1) // HEAD_DIM
    spread(q_ref[...].astype(FLOAT), qm, head, heads)
    outer = o_ref[...].astype(FLOAT)
    spread(outer, om, head, heads)
    product = exact_ref[...] * jnp.transpose(outer)
    start = widen_lanes(start_ref[...], heads)
    stop = widen_lanes(stop_ref[...], heads)
    total = total_ref[0]
    balance = jnp.concatenate(
        [
            jnp.sum(product[h * HEAD_DIM : (h + 1) * HEAD_DIM, :], axis=0, keepdims=True)
            for h in range(heads)
        ],
        axis=1,
    )
    row = lax.broadcasted_iota(jnp.int32, (BLOCK, wide), 0)
    dqt[:inner, :] = jnp.zeros((inner, BLOCK), FLOAT)

    def spend(j, raw, size=1):
        normal = jnp.exp(raw - total)
        weight = normal.astype(LOW)
        change = (normal * (nt(v_ref[span(j, size), :], om[...]) - balance)).astype(LOW)
        dv[span(j, size), :] += nn(weight, om[...])
        dk[span(j, size), :] += nn(change, qm[...])
        for h in range(heads):
            lines = slice(h * HEAD_DIM, (h + 1) * HEAD_DIM)
            dqt[lines, :] += nn(kt[lines, span(j, size)], change[:, h * BLOCK : (h + 1) * BLOCK])

    clear = first[count + count * (BLOCK // TILE) + block]

    @pl.loop(first[block], clear)
    def _(j):
        raw = nt(k_ref[span(j), :], qm[...])
        spend(j, jnp.where(row >= start - j * BLOCK, raw, -1e30))

    def plain(size, j, carry):
        spend(j, nt(k_ref[span(j, size), :], qm[...]), size)
        return carry

    sweep(clear, block, plain, 0)

    spend(block, diagonal(nt(k_ref[span(block), :], qm[...]), block, start, stop, heads))
    dq = jnp.transpose(dqt[...])[:, :inner] * HEAD_DIM ** (-0.5)
    both = jnp.concatenate([dq, dk[span(block), :]], axis=1)
    times = 2 * inner // 128
    tiles = BLOCK // TILE
    cosine, left, right = turns(first, count + block * tiles, tiles, coarse, fine)
    turned = (
        both * widen_lanes(cosine, times)
        - pltpu.roll(both, 2 * inner - ROTARY // 2, 1) * widen_lanes(left, times)
        - pltpu.roll(both, ROTARY // 2, 1) * widen_lanes(right, times)
    )
    slope_out[...] = jnp.concatenate([turned, dv[span(block), :]], axis=1).astype(LOW)


def backward(first, q, k, v, o, start, stop, total, exact, tables):
    group, inner = q.shape
    count = group // BLOCK
    wide = inner // HEAD_DIM * BLOCK

    def rows(s, first):
        return (count - 1 - s, 0)

    def lanes(s, first):
        return (0, count - 1 - s)

    def deep(s, first):
        return (count - 1 - s, 0, 0)

    thin = (BLOCK, inner)
    return call(
        backward_kernel,
        "backward",
        first,
        count,
        [(q, thin, rows), (k, None, None), (v, None, None), (o, thin, rows)]
        + [(start, (1, BLOCK), lanes), (stop, (1, BLOCK), lanes)]
        + [(total, (1, 1, wide), deep), (exact, (inner, BLOCK), lanes)]
        + [(table, None, None) for table in tables],
        [((group, 3 * inner), LOW, (BLOCK, 3 * inner), rows)],
        [
            pltpu.VMEM((inner, group), LOW),
            pltpu.VMEM((wide, inner), LOW),
            pltpu.VMEM((wide, inner), LOW),
            pltpu.VMEM((group, inner), FLOAT),
            pltpu.VMEM((group, inner), FLOAT),
            pltpu.VMEM((BLOCK, BLOCK), FLOAT),
        ],
        flops=16 * group * group * inner,
    )[0]


def mix_kernel(place, own_g, peer_g, heads_ref, weight, o_out, own_out, peer_out, extra, outer):
    inner = heads_ref.shape[1]
    step = pl.program_id(0)
    half = pl.num_programs(0) // 2
    share = weight.shape[0] // 8

    @pl.when(step == 0)
    def _():
        outer[...] = jnp.zeros_like(outer)

    def work(g_ref, target):
        heads = heads_ref[...]
        slope = g_ref[...]
        lower = jnp.concatenate([jnp.zeros((heads.shape[0], 64), LOW), heads], axis=1)
        o_out[...] = nn(slope, weight[:, 3 * inner - 64 :])[:, 64:].astype(LOW)
        target[...] = nt(lower, weight[:, 3 * inner - 64 :]).astype(LOW)
        outer[...] += tn(slope, heads)

    @pl.when(step < half)
    def _():
        work(own_g, own_out)

    @pl.when(step >= half)
    def _():
        work(peer_g, peer_out)

    @pl.when(step == 2 * half - 1)
    def _():
        for f in range(8):
            parts = [outer[f * share + 32 * c : f * share + 32 * (c + 1), :] for c in range(3)]
            parts.append(jnp.zeros((32, extra.shape[2] - 3 * inner), FLOAT))
            extra[f] = jnp.concatenate(parts, axis=1).astype(LOW)


def mix(place, own_g, peer_g, heads, weight):
    rows, width = own_g.shape
    inner = heads.shape[1]
    half = rows // ROWS
    own, peer, target = halves(half)
    block = (ROWS, width)
    thin = (ROWS, inner)
    return call(
        mix_kernel,
        "mix",
        place,
        2 * half,
        [(own_g, block, own), (peer_g, block, peer), (heads, thin, target), (weight, None, None)],
        [
            ((2 * rows, inner), LOW, thin, target),
            ((rows, width), LOW, block, own),
            ((rows, width), LOW, block, peer),
            ((8, 32, width), LOW, None, None),
        ],
        [pltpu.VMEM((width, inner), FLOAT)],
        12 * rows * width * inner,
    )


def write_parts(x, parts, kept, sent):
    for own in range(2):

        @pl.when(x == own)
        def _(own=own):
            for f in range(8):
                target = kept if f % 2 == own else sent
                for first, value in parts(f):
                    target[f // 2, first : first + value.shape[0], : value.shape[1]] = value


def feed_kernel(place, own_x, peer_x, own_g, peer_g, own_m, peer_m, *refs):
    pieces, extra, refs = refs[:8], refs[8], refs[9:]
    own_far, own_near, peer_far, peer_near, own_e, peer_e, kept, sent, *later, weight, lines, total, sums_all = refs
    step = pl.program_id(0)
    half = pl.num_programs(0) // 2
    width = own_x.shape[1]
    share = width // 8

    @pl.when(step == 0)
    def _():
        place_pieces(place, pieces, 0, weight, 0, share)
        place_pieces(place, pieces, share, weight, width, share)
        lines[...] = sum_rows(pieces, 2 * share)
        total[...] = jnp.zeros_like(total)
        sums_all[...] = jnp.zeros_like(sums_all)

    def work(x_ref, g_ref, m_ref, e_out, targets, once):
        gain = lines[0:1, :]
        unit, _ = center(x_ref[...].astype(FLOAT))
        normed = (unit * gain + lines[1:2, :]).astype(LOW)
        slope = g_ref[...]
        hidden = nn(normed, weight[:width, :]) + lines[2:3, :]
        phi = 0.5 * (1.0 + lax.erf(hidden * 0.7071067811865476))
        active = (hidden * phi).astype(LOW)
        fed = (nt(active, weight[width:, :]) + m_ref[...].astype(FLOAT)).astype(LOW)
        inside = phi + hidden * jnp.exp(-0.5 * hidden * hidden) * 0.3989422804014327
        change = (nn(slope, weight[width:, :]) * inside).astype(LOW)
        back = nt(change, weight[:width, :])
        e_out[...] = (back * gain).astype(LOW)
        total[:width, :] += tn(normed, change)
        total[width:, :] += tn(slope, active)
        rows = [
            jnp.sum(back * unit, axis=0, keepdims=True),
            jnp.sum(back, axis=0, keepdims=True),
            jnp.sum(change.astype(FLOAT), axis=0, keepdims=True),
            jnp.sum(slope.astype(FLOAT), axis=0, keepdims=True) * once,
            jnp.zeros((12, width), FLOAT),
        ]
        sums_all[...] += jnp.concatenate(rows, axis=0)
        for spot, target in enumerate(targets):

            @pl.when(step % half == spot)
            def _(target=target):
                target[...] = fed

    @pl.when(step < half)
    def _():
        work(own_x, own_g, own_m, own_e, (own_far, own_near), jnp.where(place[1] == 0, 1.0, 0.0))

    @pl.when(step >= half)
    def _():
        work(peer_x, peer_g, peer_m, peer_e, (peer_far, peer_near), 0.0)

    @pl.when(step == 2 * half - 1)
    def _():
        vectors = sums_all[...].astype(LOW)

        def parts(f):
            later_rows = slice(width + f * share, width + (f + 1) * share)
            return [(0, total[later_rows, :].astype(LOW)), (share, extra[f])]

        write_parts(place[10], parts, kept, sent)
        for ahead, target in enumerate(later):
            depth = lax.rem(place[11] + ahead, 4)
            for side in range(2):
                f = 2 * depth + side
                target[side, :share, :] = total[pl.ds(pl.multiple_of(f * share, 32), share), :].astype(LOW)
                target[side, share:, :] = vectors


def crossed(first):
    def index(s, place):
        return (jnp.where(s <= first, 1 - place[1], place[1]), 0)

    return index


def feed(place, own_x, peer_x, own_g, peer_g, own_m, peer_m, pieces, extra):
    rows, width = own_x.shape
    block = (ROWS, width)
    own, peer = crossed(0), crossed(2)
    half = ((ROWS, width), LOW, None, None)
    return call(
        feed_kernel,
        "feed",
        place,
        4,
        [(own_x, block, own), (peer_x, block, peer), (own_g, block, own), (peer_g, block, peer)]
        + [(own_m, block, own), (peer_m, block, peer)]
        + [(array, None, None) for array in (*pieces, extra)],
        [half] * 4
        + [((rows, width), LOW, block, own), ((rows, width), LOW, block, peer)]
        + [((4, width // 8 + 32, width), LOW, None, None)] * 2
        + [((2, width // 8 + 16, width), LOW, None, None)] * 4,
        [
            pltpu.VMEM((2 * width, width), LOW),
            pltpu.VMEM((16, width), FLOAT),
            pltpu.VMEM((2 * width, width), FLOAT),
            pltpu.VMEM((16, width), FLOAT),
        ],
    )


def finish_kernel(
    place, own_x, peer_x, own_e, peer_e, slope_ref, lines, weight,
    peer_far, peer_near, own_far, own_near, kept, sent,
    total, sums_all,
):
    step = pl.program_id(0)
    half = pl.num_programs(0) // 2
    width, size = total.shape
    share = width // 8

    @pl.when(step == 0)
    def _():
        total[...] = jnp.zeros_like(total)
        sums_all[...] = jnp.zeros_like(sums_all)

    slope = jnp.concatenate([slope_ref[...], jnp.zeros((slope_ref.shape[0], 64), LOW)], axis=1)

    def work(x_ref, e_ref, targets):
        unit, _ = center(x_ref[...].astype(FLOAT))
        total[...] += tn(unit.astype(LOW), slope)
        sums_all[0:1, :] += jnp.sum(slope.astype(FLOAT), axis=0, keepdims=True)
        back = nt(slope, weight[:, :size])
        value = (back * lines[0:1, :] + e_ref[...].astype(FLOAT)).astype(LOW)
        for spot, target in enumerate(targets):

            @pl.when(step % half == spot)
            def _(target=target):
                target[...] = value

    @pl.when(step < half)
    def _():
        work(peer_x, peer_e, (peer_far, peer_near))

    @pl.when(step >= half)
    def _():
        work(own_x, own_e, (own_far, own_near))

    @pl.when(step == 2 * half - 1)
    def _():
        column = jnp.transpose(jnp.concatenate([lines[...], jnp.zeros((112, width), FLOAT)], axis=0))
        flat = sums_all[0:1, :]
        part = weight[:, :size].astype(FLOAT)
        lane = lax.broadcasted_iota(jnp.int32, (1, size), 1)
        part = jnp.where(lane < size - 64, part, 0.0)
        gain_part = jnp.sum(part * total[...], axis=1, keepdims=True)
        shift_part = jnp.sum(part * flat, axis=1, keepdims=True)
        both = jnp.concatenate([gain_part, shift_part, jnp.zeros((width, 126), FLOAT)], axis=1)
        both = jnp.transpose(both)
        middle = width // 2
        none = jnp.zeros((1, size - middle), FLOAT)
        vectors = [
            jnp.concatenate([both[line : line + 1, a : a + middle], none], axis=1)
            for line in range(2)
            for a in (0, middle)
        ]
        vectors = stacked(vectors + [flat], size)
        total[...] = total[...] * column[:, 0:1] + column[:, 1:2] * flat

        def parts(f):
            return [(0, total[f * share : (f + 1) * share, :].astype(LOW)), (share, vectors)]

        write_parts(place[10], parts, kept, sent)


def finish(place, own_x, peer_x, own_e, peer_e, slope, lines, weight):
    rows, width = own_x.shape
    size = slope.shape[1] + 64
    block = (ROWS, width)

    def peer(s, place):
        return (jnp.where(s == 0, 1 - place[1], place[1]), 0)

    def own(s, place):
        return (jnp.where(s < 3, 1 - place[1], place[1]), 0)

    def target(s, place):
        side = jnp.where(s < 2, 1 - place[0], place[0])
        return (2 * side + jnp.where(s % 2 == 0, 1 - place[1], place[1]), 0)

    return call(
        finish_kernel,
        "finish",
        place,
        4,
        [(own_x, block, own), (peer_x, block, peer), (own_e, block, own), (peer_e, block, peer)]
        + [(slope, (ROWS, slope.shape[1]), target), (lines, None, None), (weight, None, None)],
        [((ROWS, width), LOW, None, None)] * 4 + [((4, width // 8 + 16, size), LOW, None, None)] * 2,
        [pltpu.VMEM((width, size), FLOAT), pltpu.VMEM((8, size), FLOAT)],
    )


def cross_kernel(place, kept, got, own, *sent):
    for step, target in enumerate((own,) + sent):
        spot = lax.rem(place[11] + step, 4)
        target[...] = (kept[spot].astype(FLOAT) + got[spot].astype(FLOAT)).astype(LOW)


def cross(place, kept, got):
    return call(
        cross_kernel,
        "cross",
        place,
        1,
        [(kept, None, None), (got, None, None)],
        [(kept.shape[1:], LOW, None, None)] * 4,
    )


def cross_feed_kernel(place, kept, got, mine, *refs):
    later, (own, one, two, three, own_late, sent_late) = refs[:3], refs[3:]
    cross_kernel(place, kept, got, own, one, two, three)
    for target, side in ((own_late, place[10]), (sent_late, 1 - place[10])):
        total = mine[side].astype(FLOAT)
        for part in later:
            total = total + part[side].astype(FLOAT)
        target[...] = total.astype(LOW)


def cross_feed(place, kept, got, mine, later):
    return call(
        cross_feed_kernel,
        "cross_feed",
        place,
        1,
        [(array, None, None) for array in (kept, got, mine, *later)],
        [(kept.shape[1:], LOW, None, None)] * 4 + [(mine.shape[1:], LOW, None, None)] * 2,
    )


def join_kernel(place, own, one, two, three, own_late, got_late, out):
    first = own.shape[0]
    total = own[...].astype(FLOAT) + one[...].astype(FLOAT) + two[...].astype(FLOAT) + three[...].astype(FLOAT)
    out[:first, :] = total.astype(LOW)
    out[first:, :] = (own_late[...].astype(FLOAT) + got_late[...].astype(FLOAT)).astype(LOW)


def join(place, own, got, own_late, got_late):
    rows = own.shape[0] + own_late.shape[0]
    return call(
        join_kernel,
        "join",
        place,
        1,
        [(array, None, None) for array in (own, *got, own_late, got_late)],
        [((rows, own.shape[1]), LOW, None, None)],
    )[0]


def last_feed_kernel(place, own, far, wide, narrow, out, sums, units):
    y = place[0]
    width = own.shape[1]
    share = width // 8
    inner = out.shape[1] // 2

    def both(first, count):
        mine = own[first : first + count, :].astype(FLOAT)
        theirs = far[first : first + count, :].astype(FLOAT)
        return mine, theirs, pick(y, mine, theirs), pick(y, theirs, mine)

    _, _, low, high = both(share + 32, share)
    wide[...] = jnp.concatenate([low, high], axis=1)
    _, _, low, high = both(0, share)
    narrow[...] = jnp.concatenate([low, high], axis=1)
    mine, theirs, low, high = both(2 * share + 32, 16)
    sums[...] = mine + theirs
    units[...] = jnp.concatenate([low[2:3, :], high[2:3, :]], axis=1)
    _, _, low, high = both(share, 32)

    def column(value):
        return jnp.concatenate([value[:, c * inner : (c + 1) * inner] for c in range(3)], axis=0)

    out[...] = jnp.concatenate([column(low), column(high)], axis=1)


def last_feed(place, own, far, inner):
    width = own.shape[1]
    share = width // 8
    return call(
        last_feed_kernel,
        "last_feed",
        place,
        1,
        [(own, None, None), (far, None, None)],
        [
            ((share, 2 * width), FLOAT, None, None),
            ((share, 2 * width), FLOAT, None, None),
            ((share, 2 * inner), FLOAT, None, None),
            ((16, width), FLOAT, None, None),
            ((1, 2 * width), FLOAT, None, None),
        ],
    )


def last_attend_kernel(place, own, far, project, sums, bias):
    y = place[0]
    _, share, double = project.shape
    inner = double // 2
    mine = own[:share, :].astype(FLOAT)
    theirs = far[:share, :].astype(FLOAT)
    low, high = pick(y, mine, theirs), pick(y, theirs, mine)
    for c in range(3):
        lanes = slice(c * inner, (c + 1) * inner)
        project[c] = jnp.concatenate([low[:, lanes], high[:, lanes]], axis=1)
    mine = own[share:, :].astype(FLOAT)
    theirs = far[share:, :].astype(FLOAT)
    sums[...] = mine + theirs
    low, high = pick(y, mine, theirs), pick(y, theirs, mine)
    rows = []
    for c in range(3):
        lanes = slice(c * inner, (c + 1) * inner)
        rows.append(jnp.concatenate([low[4:5, lanes], high[4:5, lanes]], axis=1))
    bias[...] = jnp.concatenate(rows, axis=0)


def last_attend(place, own, far, inner):
    share = own.shape[0] - 16
    return call(
        last_attend_kernel,
        "last_attend",
        place,
        1,
        [(own, None, None), (far, None, None)],
        [
            ((3, share, 2 * inner), FLOAT, None, None),
            ((16, own.shape[1]), FLOAT, None, None),
            ((3, 2 * inner), FLOAT, None, None),
        ],
    )


def settle_kernel(slope, place, x_ref, other_ref, mine, theirs, out):
    step = pl.program_id(0)
    source = x_ref[...].astype(FLOAT)

    def work(total):
        if slope:
            unit, factor = center(source)
            change = (
                total
                - jnp.mean(total, axis=-1, keepdims=True)
                - unit * jnp.mean(total * unit, axis=-1, keepdims=True)
            )
            out[...] = other_ref[...].astype(FLOAT) + factor * change
        else:
            out[...] = (source + total + (other_ref[3:4, :] + other_ref[4:5, :])).astype(LOW)

    @pl.when(step == place[1])
    def _():
        work(mine[...].astype(FLOAT))

    @pl.when(step != place[1])
    def _():
        work(theirs[...].astype(FLOAT))


def settle(place, slope, x, other, mine, theirs):
    rows, width = x.shape
    block = (ROWS, width)

    def moving(s, place):
        return (s, 0)

    return call(
        functools.partial(settle_kernel, slope),
        "settle",
        place,
        2,
        [(x, block, moving), (other, block, moving) if slope else (other, None, None)]
        + [(mine, None, None), (theirs, None, None)],
        [((rows, width), FLOAT if slope else LOW, block, moving)],
    )[0]


PAIR = [(0, 1), (1, 0)]


def swap(value, axis):
    return lax.ppermute(value, axis, PAIR)


def ring_order():
    return list(range(0, 8, 2)) + list(range(7, 0, -2))


def ring_owners(me):
    spot = jnp.where(me % 2 == 0, me // 2, 7 - me // 2)
    offsets = [0, -1, 1, -2, 2, -3, 3, -4]
    positions = [(spot + offset + 8) % 8 for offset in offsets]
    return [jnp.where(p < 4, 2 * p, 15 - 2 * p) for p in positions]


class Ring:
    def __init__(self, piece):
        self.pieces = [piece]
        self.ends = [piece, piece]
        order = ring_order()
        forward = [(order[i], order[(i + 1) % 8]) for i in range(8)]
        self.ways = [forward, [(b, a) for a, b in forward]]

    def step(self):
        ways = self.ways[: 8 - len(self.pieces)]
        self.ends = [lax.ppermute(end, "fsdp", way) for end, way in zip(self.ends, ways)]
        self.pieces += self.ends

    def newest(self):
        return tuple(self.ends)


def send_along(pieces):
    got = []
    for step, piece in enumerate(pieces, 1):
        pairs = [(2 * a + b, 2 * ((a + step) % 4) + b) for a in range(4) for b in range(2)]
        got.append(lax.ppermute(piece, "fsdp", pairs))
    return got


def add_along(own, got):
    total = own.astype(FLOAT)
    for piece in got:
        total = total + piece.astype(FLOAT)
    return total.astype(LOW)


def swap_x(value):
    return lax.ppermute(value, "fsdp", [(i, i ^ 1) for i in range(8)])


def after(values, *earlier):
    return lax.optimization_barrier((values, earlier))[0]


def add(*values):
    total = values[0].astype(FLOAT)
    for value in values[1:]:
        total = total + value.astype(FLOAT)
    return total.astype(LOW)


def ordered(own, peer, index, axis=0):
    first = jnp.where(index == 0, own, peer)
    second = jnp.where(index == 0, peer, own)
    return jnp.concatenate([first, second], axis=axis)


def take_half(value, index, axis=0):
    size = value.shape[axis] // 2
    return lax.dynamic_slice_in_dim(value, index * size, size, axis)


def split_body(
    tokens,
    pack_lengths,
    cotangent,
    projection,
    projection_bias,
    outgoing,
    outgoing_bias,
    widening,
    widening_bias,
    narrowing,
    narrowing_bias,
    first_gain,
    first_shift,
    second_gain,
    second_shift,
):
    _, local, width = tokens.shape
    group = 2 * local
    share = width // 8
    y = lax.axis_index("context")
    core = lax.axis_index("tensor")
    me = lax.axis_index("fsdp")
    own_x = tokens.reshape(local, width)
    own_g = cotangent.reshape(local, width)
    inner = outgoing.shape[0] // 2
    third = projection_bias.shape[1]
    owners = ring_owners(me)
    place = jnp.stack([y, core] + owners + [me % 2, me // 2, me])
    other = jnp.stack([1 - y, core] + owners + [me % 2, me // 2, me])

    def whole(*arrays):
        return [(array if array.ndim > 1 else rank_two(array), None, None) for array in arrays]

    attend_piece = call(
        pack_attend_kernel,
        "pack_attend",
        place,
        1,
        whole(projection.transpose(1, 0, 2), outgoing.T, first_gain, first_shift, outgoing_bias, narrowing_bias)
        + whole(projection_bias),
        [((share + 16, width), LOW, None, None)],
    )[0]
    index = jnp.arange(group, dtype=jnp.int32)
    number, position, valid = layout(pack_lengths[0], index)
    begin = index - position
    labels = jnp.arange(SEQS, dtype=jnp.int32)
    length = jnp.sum(
        jnp.where(number[:, None] == labels[None, :], pack_lengths[0][None, :], 0), axis=1
    )
    stop = jnp.minimum(index + 1, begin + length).reshape(1, group)
    start = jnp.where(number == SEQS, index, begin)
    blocks = start.reshape(group // BLOCK, BLOCK)
    first = jnp.min(blocks, axis=1) // BLOCK
    clear = (jnp.max(blocks, axis=1) + BLOCK - 1) // BLOCK
    clear = jnp.minimum(jnp.maximum(clear, first), jnp.arange(group // BLOCK, dtype=jnp.int32))
    start = start.reshape(1, group)
    tiles = position.reshape(group // TILE, TILE)[:, 0] // TILE
    first = jnp.concatenate([first, tiles, clear])
    tables = turning()
    place = jnp.concatenate([place, tiles])

    far_x = swap(take_half(own_x, core), "context")
    attend_ring = Ring(attend_piece)
    attend_ring.step()
    attend_ring.step()
    feed_piece = call(
        pack_feed_kernel,
        "pack_feed",
        place,
        1,
        whole(widening, narrowing.T, second_gain, second_shift, widening_bias),
        [((2 * share + 16, width), LOW, None, None)],
    )[0]
    feed_ring = Ring(after(feed_piece, attend_ring.newest()))
    attend_ring.step()
    far_x = after(far_x, attend_ring.newest())
    far_g = swap(after(take_half(own_g, core), far_x), "context")
    peer_x = ordered(far_x, swap(far_x, "tensor"), core)
    feed_ring.step()
    attend_ring.step()
    peer_x, feed_ring.ends = after((peer_x, feed_ring.ends))
    feed_ring.step()
    q, k, v, attend_weight, attend_lines = prepare(place, own_x, peer_x, tables, attend_ring.pieces, inner)
    q, far_g = after((q, far_g), feed_ring.newest())
    feed_ring.step()
    near_g = swap(far_g, "tensor")
    heads, total, exact = forward(first, q, k, v, start, stop)
    heads, near_g, feed_ring.ends = after((heads, near_g, feed_ring.ends))
    feed_ring.step()
    peer_g = ordered(far_g, near_g, core)
    o, mixed_own, mixed_peer, extra = mix(place, own_g, peer_g, heads, attend_weight)

    own_far, own_near, peer_far, peer_near, e_own, e_peer, kept, sent, *late = feed(
        place, own_x, peer_x, own_g, peer_g, mixed_own, mixed_peer, feed_ring.pieces, extra
    )
    got = swap_x(sent)
    late_got = send_along(late[1:])
    gone = add(peer_near, swap(peer_far, "tensor"))
    mixed_far = swap(gone, "context")
    own_got = swap(own_far, "tensor")

    o = after(o, gone, own_got)
    slope = backward(first, q, k, v, o, start, stop, total, exact, tables)
    slope, got, late_got, mixed_far = after((slope, got, late_got, mixed_far))
    feed_cross = cross_feed(place, kept, got, late[0], late_got)
    slope = after(slope, feed_cross)
    feed_got = send_along(feed_cross[1:4])
    late_got = swap_x(feed_cross[5])
    peer_far, peer_near, far_own, near_own, kept, sent = finish(
        place, own_x, peer_x, own_e=e_own, peer_e=e_peer, slope=slope, lines=attend_lines, weight=attend_weight
    )
    sent, peer_far, far_own, feed_got, late_got = after((sent, peer_far, far_own, feed_got, late_got))
    attend_got = swap_x(sent)
    peer_got = swap(peer_far, "tensor")
    e_got_own = swap(far_own, "tensor")
    gone = add(peer_near, peer_got)
    e_far = swap(gone, "context")
    feed_got, own_near = after((feed_got, own_near), gone)
    feed_sum = join(place, feed_cross[0], feed_got, feed_cross[4], late_got)
    mine = add(own_near, own_got, mixed_far)
    theirs = swap(mine, "tensor")
    mixed = settle(place, False, own_x, attend_lines, mine, theirs)
    attend_got = after(attend_got, mixed)
    attend_cross = cross(place, kept, attend_got)
    attend_along = send_along(attend_cross[1:])
    e_far = after(e_far, attend_cross[0])
    mine = add(near_own, e_got_own, e_far)
    feed_far = swap(after(feed_sum, e_far), "context")
    theirs = swap(mine, "tensor")
    wide_slope, narrow_slope, outgoing_slope, feed_sums, unit_slope = last_feed(place, feed_sum, feed_far, inner)
    attend_along, theirs = after((attend_along, theirs), wide_slope)
    attend_sum = add_along(attend_cross[0], attend_along)
    attend_far = swap(attend_sum, "context")
    theirs = after(theirs, attend_sum)
    tokens_gradient = settle(place, True, own_x, own_g, mine, theirs)
    attend_far = after(attend_far, tokens_gradient)

    projection_slope, attend_sums, bias_slope = last_attend(place, attend_sum, attend_far, inner)

    def across(rows):
        part = lax.dynamic_slice_in_dim(rows.astype(LOW), me * share, share, 1)
        return part.astype(FLOAT) + swap(part, "tensor").astype(FLOAT)

    feed_lines = across(feed_sums[:8])
    attend_slopes = across(attend_sums[:4, : width // 2].reshape(2, width))
    unit_slope = lax.dynamic_slice_in_dim(unit_slope[0], me * (width // 4), width // 4)
    bias_slope = lax.dynamic_slice_in_dim(bias_slope, me * third, third, 1)
    return (
        mixed.reshape(tokens.shape),
        tokens_gradient.reshape(tokens.shape),
        projection_slope.transpose(1, 0, 2),
        bias_slope,
        outgoing_slope.T,
        feed_lines[3],
        wide_slope,
        unit_slope,
        narrow_slope.T,
        feed_lines[3],
        attend_slopes[0],
        attend_slopes[1],
        feed_lines[0],
        feed_lines[1],
    )


def body(*arrays):
    tokens, outgoing, narrowing = arrays[0], arrays[5], arrays[9]
    fits = (
        lax.axis_size("fsdp") == 8
        and lax.axis_size("context") == 2
        and lax.axis_size("tensor") == 2
        and tokens.shape[0] == 1
        and tokens.shape[1] == 2 * ROWS
        and outgoing.shape[0] == 6 * HEAD_DIM
        and tokens.shape[2] * 2 == narrowing.shape[0]
    )
    return split_body(*arrays) if fits else general_body(*arrays)


def solution(mesh):
    return jax.shard_map(
        body,
        mesh=mesh,
        in_specs=(
            P("fsdp", "context", None),
            P("fsdp", None),
            P("fsdp", "context", None),
            P("fsdp", None, "tensor"),
            P(None, ("tensor", "fsdp")),
            P("tensor", "fsdp"),
            P("fsdp"),
            P("fsdp", "tensor"),
            P(("tensor", "fsdp")),
            P("tensor", "fsdp"),
            P("fsdp"),
            P("fsdp"),
            P("fsdp"),
            P("fsdp"),
            P("fsdp"),
        ),
        out_specs=(
            P("fsdp", "context", None),
            P("fsdp", "context", None),
            P("fsdp", None, "tensor"),
            P(None, ("tensor", "fsdp")),
            P("tensor", "fsdp"),
            P("fsdp"),
            P("fsdp", "tensor"),
            P(("tensor", "fsdp")),
            P("tensor", "fsdp"),
            P("fsdp"),
            P("fsdp"),
            P("fsdp"),
            P("fsdp"),
            P("fsdp"),
        ),
        check_vma=False,
    )
```
